32 devices in a mesh: grid: 4 (over y, core), dom: 8 (over z, x).
Axes of the slice: x: 2, y: 2, z: 4, core: 2. Of those that a mesh axis runs over, the one named last changes fastest.
Arguments:
- state: float32 [5, 125, 4096], P(None, None, ('grid', 'dom')), as said below
- inv_size: float32 [3, 4096], P(None, ('grid', 'dom')), may hold values from 1 to 4
- plus_order: int32 [3, 4096], P(None, ('grid', 'dom')), may hold values from 0 to 127, as said below
- minus_order: int32 [3, 4096], P(None, ('grid', 'dom')), may hold values from 0 to 127, as said below
- donor_cell: int32 [32, 1184], P(('grid', 'dom')), may hold values from 0 to 127
- donor_weights: float32 [32, 3, 5, 1184], P(('grid', 'dom')), as said below
- recv_slot: int32 [32, 600], P(('grid', 'dom')), may hold values from 0 to 1183, as said below
Outputs:
- rhs: float32 [5, 125, 4096], P(None, None, ('grid', 'dom'))
The draws below stay inside these ranges and needn't reach their ends.
Inputs may be any that keep to these rules, and one draw needn't show every extreme that they name: `plus_order`: within each device's block of 128 columns, every row is a permutation of the local element numbers. `minus_order`: within each device's block of 128 columns, every row is a permutation of the local element numbers. `state`: density lies in [0.9, 1.1], each momentum in [-0.1, 0.1], energy in [2.4, 2.6]. `donor_weights`: for each donor device, direction and slot, the five weights are the Lagrange basis of the five Gauss-Legendre points evaluated at one coordinate in [-0.8, 0.8]. `recv_slot`: entries of one device's row are distinct, and each names a slot whose source device (the slot // 37) lies in another grid than the row's device.
All inputs are finite; a program needn't handle non-finite values.
Results may differ from the reference program's by a relative error of at most 0.0003.
Values sent between devices are 32-bit elements; how exact they have to be, the bound alone decides.
No kernel may reach another device: no remote copies, remote signals or barrier semaphores. Data moves between devices by JAX's collectives and lax.ppermute only.
A program may use at most 64 MiB of HBM per device.

```python
import math
import jax
import jax.numpy as jnp
from jax import lax

E_DEV = 128
FRP = 4
NGRIDS = 4
NPARTS = 8
DEVICE_TOTAL = 32
CAP = 5
REMOTE = 40
FRINGE_PTS = 600
SLOTS = 37
ELEMS = 4096


gauss_points = (-0.906179845938664, -0.5384693101056831, 0.0, 0.5384693101056831, 0.906179845938664)


def draw_state(key, part):
    uniform_part = jax.random.uniform(key, (5, 125, ELEMS), jnp.float32, -1.0, 1.0)
    centre = jnp.array([1.0, 0.0, 0.0, 0.0, 2.5], jnp.float32).reshape(5, 1, 1)
    return centre + 0.1 * uniform_part


def local_orders(key):
    key_list = jax.random.split(key, DEVICE_TOTAL * 3)
    orders = jax.vmap(lambda single: jax.random.permutation(single, E_DEV))(key_list)
    return jnp.transpose(orders.reshape(DEVICE_TOTAL, 3, E_DEV), (1, 0, 2)).reshape(3, DEVICE_TOTAL * E_DEV).astype(jnp.int32)


def draw_plus_order(key, part):
    return local_orders(jax.random.fold_in(key, 11))


def draw_minus_order(key, part):
    return local_orders(jax.random.fold_in(key, 23))


def draw_donor_weights(key, part):
    coordinate = jax.random.uniform(jax.random.fold_in(key, 31), (DEVICE_TOTAL, 3, 1, DEVICE_TOTAL * SLOTS), jnp.float32, -0.8, 0.8)
    basis = []
    for column in range(5):
        value = jnp.ones_like(coordinate)
        for other in range(5):
            if other != column:
                value = value * (coordinate - gauss_points[other]) / (gauss_points[column] - gauss_points[other])
        basis.append(value)
    return jnp.concatenate(basis, axis=2)


def draw_recv_slot(key, part):
    slot_total = DEVICE_TOTAL * SLOTS
    extra_score_key, ordering_key = jax.random.split(jax.random.fold_in(key, 37))
    extra_score = jax.random.randint(extra_score_key, (DEVICE_TOTAL,), 0, 4)
    extra_score = extra_score.at[0].set(5).at[DEVICE_TOTAL - 1].set(5)
    source_index = jnp.arange(slot_total, dtype=jnp.int32) // SLOTS
    order_keys = jax.random.split(ordering_key, DEVICE_TOTAL)
    rank_positions = jax.vmap(lambda single: jax.random.permutation(single, slot_total))(order_keys).astype(jnp.int32)
    receiver_grid = (jnp.arange(DEVICE_TOTAL, dtype=jnp.int32) // NPARTS)[:, None]
    permitted_mask = (source_index // NPARTS)[None, :] != receiver_grid
    score_values = jnp.where(permitted_mask, extra_score[source_index][None, :] * 1048576 + rank_positions, -1 - rank_positions)
    return jax.lax.top_k(score_values, FRINGE_PTS)[1].astype(jnp.int32)


def plant(values, rng, low, top_value):
    longest = values.shape.index(max(values.shape))
    spots = []
    for shift in (0, 1):
        where = [jax.random.randint(jax.random.fold_in(rng, axis), (), 0, length) for axis, length in enumerate(values.shape)]
        where[longest] = (where[longest] + shift) % values.shape[longest]
        spots.append(tuple(where))
    return values.at[spots[0]].set(low).at[spots[1]].set(top_value)


def shard_levels(key, extent, cuts, least, top_value):
    gain = 1.0
    for dim, shards_of in cuts:
        steps = jax.random.uniform(jax.random.fold_in(jax.random.fold_in(key, 6), dim), (shards_of,), jnp.float32, least / len(cuts), top_value / len(cuts))
        gain = gain * jnp.repeat(jnp.exp(steps), extent[dim] // shards_of).reshape((-1,) + (1,) * (len(extent) - 1 - dim))
    return gain


def setup_inputs(seed: int = 0) -> dict:
    streams_of = jax.random.split(jax.random.key(seed), 8)
    state = draw_state(jax.random.fold_in(streams_of[7], 71), 0)
    inv_size = jnp.clip(jnp.exp(math.log(4.0) - 1.3862944 * jax.random.uniform(streams_of[1], (3, ELEMS), jnp.float32) ** shard_levels(streams_of[1], (3, ELEMS), ((1, 32),), -0.2, 0.2)), 1.0, 4.0)
    plus_order = draw_plus_order(jax.random.fold_in(streams_of[7], 71), 0)
    minus_order = draw_minus_order(jax.random.fold_in(streams_of[7], 71), 0)
    donor_cell = plant(jax.random.randint(streams_of[4], (DEVICE_TOTAL, DEVICE_TOTAL * SLOTS), 0, E_DEV), jax.random.fold_in(streams_of[4], 1), 0, E_DEV - 1).astype(jnp.int32)
    donor_weights = draw_donor_weights(jax.random.fold_in(streams_of[7], 71), 0)
    recv_slot = draw_recv_slot(jax.random.fold_in(streams_of[7], 71), 0)
    return dict(state=state, inv_size=inv_size, plus_order=plus_order, minus_order=minus_order, donor_cell=donor_cell, donor_weights=donor_weights, recv_slot=recv_slot)


precise = lax.Precision.HIGHEST
volume_forms = ('ia,vabce->vibce', 'ib,vabce->vaice', 'ic,vabce->vabie')
face_forms = ('a,vabce->vbce', 'b,vabce->vace', 'c,vabce->vabe')
lift_forms = ('i,vbce->vibce', 'i,vace->vaice', 'i,vabe->vabie')

def gauss_nodes():
    outer = math.sqrt(5.0 + 2.0 * math.sqrt(10.0 / 7.0)) / 3.0
    inner = math.sqrt(5.0 - 2.0 * math.sqrt(10.0 / 7.0)) / 3.0
    return [-outer, -inner, 0.0, inner, outer]

def basis_value(nodes, column, target_positions):
    value = 1.0
    for other in range(5):
        if other != column:
            value = value * (target_positions - nodes[other]) / (nodes[column] - nodes[other])
    return value

def basis_slope(nodes, column, target_positions):
    total = 0.0
    for skipped in range(5):
        if skipped != column:
            value = 1.0 / (nodes[column] - nodes[skipped])
            for other in range(5):
                if other != column and other != skipped:
                    value = value * (target_positions - nodes[other]) / (nodes[column] - nodes[other])
            total = total + value
    return total

def legendre_slopes(target_positions):
    values = [1.0, target_positions]
    slopes = [0.0, 1.0]
    for order in range(1, 5):
        values.append(((2 * order + 1) * target_positions * values[order] - order * values[order - 1]) / (order + 1))
        slopes.append(slopes[order - 1] + (2 * order + 1) * values[order])
    return (slopes[4], slopes[5])

def tables():
    nodes = gauss_nodes()
    deriv = [[basis_slope(nodes, column, nodes[row]) for column in range(5)] for row in range(5)]
    lower = [basis_value(nodes, column, -1.0) for column in range(5)]
    upper = [basis_value(nodes, column, 1.0) for column in range(5)]
    lift_low = []
    lift_high = []
    for row in range(5):
        slope_four, slope_five = legendre_slopes(nodes[row])
        lift_low.append(-0.5 * (slope_five - slope_four))
        lift_high.append(0.5 * (slope_five + slope_four))
    return tuple((jnp.asarray(matrix, jnp.float32) for matrix in (deriv, lower, upper, lift_low, lift_high)))

def euler_flux(state, direction):
    density = state[0]
    momenta = state[1:4]
    energy = state[4]
    speed = momenta[direction] / density
    pressure = 0.4 * (energy - 0.5 * lax.optimization_barrier(jnp.sum(momenta * momenta, axis=0)) / density)
    pieces = [momenta[direction], momenta[0] * speed, momenta[1] * speed, momenta[2] * speed, (energy + pressure) * speed]
    pieces[1 + direction] = pieces[1 + direction] + pressure
    sound = jnp.sqrt(1.4 * pressure / density)
    return (jnp.stack(pieces), jnp.abs(speed) + sound)

def common_flux(left_state, right_state, direction):
    left_flux, left_wave = euler_flux(left_state, direction)
    right_flux, right_wave = euler_flux(right_state, direction)
    wave = jnp.maximum(left_wave, right_wave)
    return 0.5 * (left_flux + right_flux) - 0.5 * wave * (right_state - left_state)

def remote_fluxes(left_states, right_states):
    return jnp.stack([common_flux(left_states[direction], right_states[direction], direction) for direction in range(3)])

def slot_states(state, plus_rows, minus_rows):
    deriv, lower, upper, lift_low, lift_high = tables()
    columns = state.shape[-1]
    grid_form = state.reshape(5, 5, 5, 5, columns)
    high_slots = []
    low_slots = []
    for direction in range(3):
        high_face = jnp.einsum(face_forms[direction], upper, grid_form, precision=precise).reshape(5, 25, columns)
        low_face = jnp.einsum(face_forms[direction], lower, grid_form, precision=precise).reshape(5, 25, columns)
        high_slots.append(jnp.take(high_face, plus_rows[direction], axis=2))
        low_slots.append(jnp.take(low_face, minus_rows[direction], axis=2))
    return (jnp.stack(high_slots), jnp.stack(low_slots))

def interpolate(state, cells, weights, blocks):
    block_width = cells.shape[0] // blocks

    def one_block(index):
        block_cells = lax.dynamic_slice_in_dim(cells, index * block_width, block_width)
        block_weights = lax.dynamic_slice_in_dim(weights, index * block_width, block_width, axis=2)
        gathered = jnp.take(state, block_cells, axis=2).reshape(5, 5, 5, 5, block_width)
        reduced = jnp.einsum('as,vabcs->vbcs', block_weights[0], gathered, precision=precise)
        reduced = jnp.einsum('bs,vbcs->vcs', block_weights[1], reduced, precision=precise)
        return jnp.einsum('cs,vcs->vs', block_weights[2], reduced, precision=precise)
    values = lax.map(one_block, jnp.arange(blocks, dtype=jnp.int32))
    return jnp.transpose(values, (1, 0, 2)).reshape(5, blocks * block_width)

def assemble(high_slots, low_slots, remote_plus, remote_minus, fringe, plus_rows, minus_rows):
    remote = remote_plus.shape[-1]
    start = remote + fringe.shape[-1]
    plus_parts = []
    minus_parts = []
    for direction in range(3):
        local_flux = common_flux(high_slots[direction][:, :, start:], low_slots[direction][:, :, start:], direction)
        fringe_high = common_flux(high_slots[direction][:, :, remote:start], fringe[direction, 1], direction)
        fringe_low = common_flux(fringe[direction, 0], low_slots[direction][:, :, remote:start], direction)
        plus_slots = jnp.concatenate([remote_plus[direction], fringe_high, local_flux], axis=2)
        minus_slots = jnp.concatenate([remote_minus[direction], fringe_low, local_flux], axis=2)
        plus_parts.append(jnp.zeros_like(plus_slots).at[:, :, plus_rows[direction]].set(plus_slots))
        minus_parts.append(jnp.zeros_like(minus_slots).at[:, :, minus_rows[direction]].set(minus_slots))
    return (jnp.stack(plus_parts), jnp.stack(minus_parts))

def divergence(state, scales, plus_common, minus_common):
    deriv, lower, upper, lift_low, lift_high = tables()
    columns = state.shape[-1]
    grid_form = state.reshape(5, 5, 5, 5, columns)
    total = jnp.zeros_like(grid_form)
    for direction in range(3):
        flux = euler_flux(grid_form, direction)[0]
        inner = jnp.einsum(volume_forms[direction], deriv, flux, precision=precise)
        low_jump = minus_common[direction].reshape(5, 5, 5, columns) - jnp.einsum(face_forms[direction], lower, flux, precision=precise)
        high_jump = plus_common[direction].reshape(5, 5, 5, columns) - jnp.einsum(face_forms[direction], upper, flux, precision=precise)
        inner = inner + jnp.einsum(lift_forms[direction], lift_low, low_jump, precision=precise)
        inner = inner + jnp.einsum(lift_forms[direction], lift_high, high_jump, precision=precise)
        total = total + scales[direction] * inner
    return (-total).reshape(5, 125, columns)

def reference(state, inv_size, plus_order, minus_order, donor_cell, donor_weights, recv_slot):

    def gather_side(index):
        offset = index.astype(jnp.int32) * E_DEV
        block = lax.dynamic_slice_in_dim(state, offset, E_DEV, axis=2)
        plus_rows = lax.dynamic_slice_in_dim(plus_order, offset, E_DEV, axis=1)
        minus_rows = lax.dynamic_slice_in_dim(minus_order, offset, E_DEV, axis=1)
        high_slots, low_slots = slot_states(block, plus_rows, minus_rows)
        values = interpolate(block, donor_cell[index], donor_weights[index], NGRIDS)
        return (high_slots[..., :REMOTE], low_slots[..., :REMOTE], values)
    sent_high, sent_low, donor_values = lax.map(gather_side, jnp.arange(DEVICE_TOTAL, dtype=jnp.int32))

    def regroup(sent):
        shaped = sent.reshape(NGRIDS, NPARTS, 3, 5, 25, NPARTS, CAP)
        return jnp.transpose(shaped, (0, 5, 2, 3, 4, 1, 6)).reshape(DEVICE_TOTAL, 3, 5, 25, REMOTE)
    partner_high = regroup(sent_high)
    partner_low = regroup(sent_low)
    arrived = jnp.transpose(donor_values.reshape(DEVICE_TOTAL, 5, DEVICE_TOTAL, SLOTS), (2, 1, 0, 3)).reshape(DEVICE_TOTAL, 5, DEVICE_TOTAL * SLOTS)

    def finish(index, result):
        index = index.astype(jnp.int32)
        offset = index * E_DEV
        block = lax.dynamic_slice_in_dim(state, offset, E_DEV, axis=2)
        scales = lax.dynamic_slice_in_dim(inv_size, offset, E_DEV, axis=1)
        plus_rows = lax.dynamic_slice_in_dim(plus_order, offset, E_DEV, axis=1)
        minus_rows = lax.dynamic_slice_in_dim(minus_order, offset, E_DEV, axis=1)
        high_slots, low_slots = slot_states(block, plus_rows, minus_rows)
        fringe = jnp.take(arrived[index], recv_slot[index], axis=1)
        fringe = jnp.transpose(fringe.reshape(5, 3, 2, 25, FRP), (1, 2, 0, 3, 4))
        remote_plus = remote_fluxes(high_slots[..., :REMOTE], partner_low[index])
        remote_minus = remote_fluxes(partner_high[index], low_slots[..., :REMOTE])
        plus_common, minus_common = assemble(high_slots, low_slots, remote_plus, remote_minus, fringe, plus_rows, minus_rows)
        rhs_block = divergence(block, scales, plus_common, minus_common)
        return lax.dynamic_update_slice_in_dim(result, rhs_block, offset, axis=2)
    result = jnp.zeros((5, 125, DEVICE_TOTAL * E_DEV), jnp.float32)
    return lax.fori_loop(0, DEVICE_TOTAL, finish, result)
```

```python
import functools
import math

import jax
import jax.numpy as jnp
import numpy as np
from jax import lax
from jax.experimental import pallas as pl
from jax.experimental.pallas import tpu as pltpu
from jax.sharding import PartitionSpec as P

precise = lax.Precision.HIGHEST
LANES = 128
ROWS = 32
VMEM = 48 * 1024 * 1024


def gauss_nodes():
    outer = math.sqrt(5.0 + 2.0 * math.sqrt(10.0 / 7.0)) / 3.0
    inner = math.sqrt(5.0 - 2.0 * math.sqrt(10.0 / 7.0)) / 3.0
    return [-outer, -inner, 0.0, inner, outer]


def basis_value(nodes, column, target):
    value = 1.0
    for other in range(5):
        if other != column:
            value = value * (target - nodes[other]) / (nodes[column] - nodes[other])
    return value


def basis_slope(nodes, column, target):
    total = 0.0
    for skipped in range(5):
        if skipped != column:
            value = 1.0 / (nodes[column] - nodes[skipped])
            for other in range(5):
                if other != column and other != skipped:
                    value = value * (target - nodes[other]) / (nodes[column] - nodes[other])
            total = total + value
    return total


def legendre_slopes(target):
    values = [1.0, target]
    slopes = [0.0, 1.0]
    for order in range(1, 5):
        values.append(
            ((2 * order + 1) * target * values[order] - order * values[order - 1]) / (order + 1)
        )
        slopes.append(slopes[order - 1] + (2 * order + 1) * values[order])
    return (slopes[4], slopes[5])


def tables():
    nodes = gauss_nodes()
    deriv = [[basis_slope(nodes, column, nodes[row]) for column in range(5)] for row in range(5)]
    lower = [basis_value(nodes, column, -1.0) for column in range(5)]
    upper = [basis_value(nodes, column, 1.0) for column in range(5)]
    lift_low = []
    lift_high = []
    for row in range(5):
        slope_four, slope_five = legendre_slopes(nodes[row])
        lift_low.append(-0.5 * (slope_five - slope_four))
        lift_high.append(0.5 * (slope_five + slope_four))
    return tuple(np.asarray(m, np.float64) for m in (deriv, lower, upper, lift_low, lift_high))


def split_point(point, direction):
    index = [point // 25, point // 5 % 5, point % 5]
    along = index.pop(direction)
    return along, 5 * index[0] + index[1]


def matrices():
    deriv, lower, upper, lift_low, lift_high = tables()
    faces = np.zeros((6 * ROWS, 125))
    volume = np.zeros((125, 3 * LANES))
    lift = np.zeros((125, 6 * ROWS))
    own = deriv - np.outer(lift_low, lower) - np.outer(lift_high, upper)
    for d in range(3):
        for p in range(125):
            i, t = split_point(p, d)
            faces[(2 * d) * ROWS + t, p] = lower[i]
            faces[(2 * d + 1) * ROWS + t, p] = upper[i]
            lift[p, (2 * d) * ROWS + t] = -lift_low[i]
            lift[p, (2 * d + 1) * ROWS + t] = -lift_high[i]
            for other in range(125):
                m, line = split_point(other, d)
                if line == t:
                    volume[p, d * LANES + other] = -own[i, m]
    for k in range(6):
        faces[k * ROWS + 25 : (k + 1) * ROWS] = faces[k * ROWS + 24]
    expand = np.zeros((3 * LANES, 15))
    for p in range(125):
        for axis, index in enumerate((p // 25, p // 5 % 5, p % 5)):
            expand[axis * LANES + p, 5 * axis + index] = 1.0
    return tuple(m.astype(np.float32) for m in (faces, volume, lift, expand))


def partner(index, step, count):
    if count & (count - 1) == 0:
        return index ^ step
    return (index + step) % count


def lane_gather(values, index):
    return jnp.take_along_axis(values, index, axis=1, mode="promise_in_bounds")


def euler(state, direction):
    density, momenta, energy = state[0], state[1:4], state[4]
    inverse = 1.0 / density
    speed = momenta[direction] * inverse
    squares = momenta[0] * momenta[0] + momenta[1] * momenta[1] + momenta[2] * momenta[2]
    pressure = 0.4 * (energy - 0.5 * squares * inverse)
    flux = [
        momenta[direction],
        momenta[0] * speed,
        momenta[1] * speed,
        momenta[2] * speed,
        (energy + pressure) * speed,
    ]
    flux[1 + direction] = flux[1 + direction] + pressure
    return flux, speed, pressure, inverse


def euler_wave(state, direction):
    flux, speed, pressure, inverse = euler(state, direction)
    return flux, jnp.abs(speed) + jnp.sqrt(1.4 * pressure * inverse)


def mix(left, left_flux, left_wave, right, right_flux, right_wave):
    wave = 0.5 * jnp.maximum(left_wave, right_wave)
    return [
        0.5 * (left_flux[v] + right_flux[v]) - wave * (right[v] - left[v]) for v in range(5)
    ]


def donor_kernel(
    grids, parts, count, state_ref, cell_ref, weight_ref, expand_ref, *refs
):
    outs = refs[: grids - 1]
    cells, weights, values, windows = refs[grids - 1 :]
    total = grids * parts * count
    blocks = cells.shape[1] // LANES
    cells[...] = jnp.zeros_like(cells)
    weights[...] = jnp.zeros_like(weights)
    cells[0:1, :total] = cell_ref[...]
    for k in range(15):
        weights[k : k + 1, :total] = weight_ref[k]
    expand = expand_ref[...]
    for block in range(blocks):
        lanes = slice(block * LANES, (block + 1) * LANES)
        wide = jnp.dot(
            expand, weights[:15, lanes], precision=precise, preferred_element_type=jnp.float32
        )
        weight = (wide[:LANES] * wide[LANES : 2 * LANES] * wide[2 * LANES :])[:125]
        index = jnp.broadcast_to(cells[0:1, lanes], (125, LANES))
        for v in range(5):
            picked = lane_gather(state_ref[v], index)
            values[v : v + 1, lanes] = jnp.sum(picked * weight, axis=0, keepdims=True)
    lane = lax.broadcasted_iota(jnp.int32, (8, LANES), 1)
    me = lax.axis_index("grid")
    for step in range(1, grids):
        wanted = (lane >= (step - 1) * count) & (lane < step * count)
        for g in range(grids):

            @pl.when(partner(me, step, grids) == g)
            def _():
                for q in range(parts):
                    start = (g * parts + q) * count
                    block = start // LANES
                    width = 2 * LANES if block + 1 < blocks else LANES
                    pair = values[:, block * LANES : block * LANES + width]
                    shift = ((step - 1) * count - (start - block * LANES)) % width
                    moved = pltpu.roll(pair, shift, 1)[:, :LANES] if shift else pair[:, :LANES]
                    outs[step - 1][q] = jnp.where(wanted, moved, 0.0)


def face_kernel(
    parts, capacity, rows, state_ref, plus_ref, minus_ref, faces_ref, lanes_ref, slots_ref, pay_ref, turn
):
    wide = jnp.concatenate([state_ref[v] for v in range(5)], axis=1)
    face = jnp.dot(
        faces_ref[...], wide, precision=precise, preferred_element_type=jnp.float32
    )
    to_slot = lanes_ref[...]
    turn[120:128, :] = jnp.zeros((8, LANES), jnp.float32)
    for k in range(6):
        order = (minus_ref, plus_ref)[k % 2][k // 2 : k // 2 + 1, :]
        index = lane_gather(jnp.broadcast_to(order, (8, LANES)), to_slot)
        index = jnp.concatenate([index] * (ROWS // 8), axis=0)
        for v in range(5):
            block = face[k * ROWS : (k + 1) * ROWS, v * LANES : (v + 1) * LANES]
            picked = lane_gather(block, index)
            slots_ref[k, v] = picked
            turn[25 * v : 25 * v + 25, :] = picked[:25]
        turned = turn[...].T
        for s in range(capacity):
            pay_ref[pl.ds(k * capacity + s, parts, stride=rows), :] = turned[
                s * parts : (s + 1) * parts
            ]


def volume_kernel(
    grids,
    parts,
    count,
    state_ref,
    size_ref,
    plus_ref,
    minus_ref,
    recv_ref,
    slots_ref,
    volume_ref,
    lanes_ref,
    part_ref,
    flux_ref,
    local_ref,
    back_ref,
    where_ref,
    wide,
    index,
):
    state = [state_ref[v] for v in range(5)]
    for d in range(3):
        flux = euler(state, d)[0]
        scale = size_ref[d : d + 1, :]
        wide[d * LANES + 120 : (d + 1) * LANES, :] = jnp.zeros((8, 5 * LANES), jnp.float32)
        for v in range(5):
            wide[d * LANES : d * LANES + 125, v * LANES : (v + 1) * LANES] = flux[v] * scale
    part_ref[...] = jnp.dot(
        volume_ref[...], wide[...], precision=precise, preferred_element_type=jnp.float32
    )
    for d in range(3):
        low = [slots_ref[2 * d, v] for v in range(5)]
        high = [slots_ref[2 * d + 1, v] for v in range(5)]
        low_flux, low_wave = euler_wave(low, d)
        high_flux, high_wave = euler_wave(high, d)
        local = mix(high, high_flux, high_wave, low, low_flux, low_wave)
        for v in range(5):
            flux_ref[2 * d, v] = low_flux[v]
            flux_ref[2 * d + 1, v] = high_flux[v]
            local_ref[d, v] = local[v]
        flux_ref[2 * d, 5] = low_wave
        flux_ref[2 * d + 1, 5] = high_wave
    to_slot = lanes_ref[...]
    rank = lax.broadcasted_iota(jnp.int32, (LANES, LANES), 0)
    lane = lax.broadcasted_iota(jnp.int32, (LANES, LANES), 1)
    index[...] = jnp.zeros_like(index)
    for k in range(6):
        order = (minus_ref, plus_ref)[k % 2][k // 2 : k // 2 + 1, :]
        order = lane_gather(jnp.broadcast_to(order, (8, LANES)), to_slot)
        index[k : k + 1, :] = order[0:1].astype(jnp.float32)
    turned = index[...].T.astype(jnp.int32)
    back_ref[...] = jnp.zeros_like(back_ref)
    for k in range(6):
        found = jnp.where(turned[:, k : k + 1] == lane, rank, 0)
        back_ref[k : k + 1, :] = jnp.sum(found, axis=0, keepdims=True)
    me = lax.axis_index("grid")
    points = recv_ref.shape[1] // 6
    where_ref[...] = jnp.zeros_like(where_ref)
    for k in range(6):
        slot = recv_ref[:, k * points : (k + 1) * points]
        device = ((slot.astype(jnp.float32) + 0.5) * (1.0 / count)).astype(jnp.int32)
        rest = slot - device * count
        grid = ((device.astype(jnp.float32) + 0.5) * (1.0 / parts)).astype(jnp.int32)
        step = jnp.zeros_like(grid)
        for g in range(grids):
            if grids & (grids - 1) == 0:
                away = me ^ g
            else:
                away = lax.rem(me + grids - g, grids)
            step = jnp.where(grid == g, away, step)
        where_ref[0, k : k + 1, :points] = device - grid * parts
        where_ref[1, k : k + 1, :points] = jnp.maximum(step - 1, 0) * count + rest


def finish_kernel(
    parts,
    capacity,
    rows,
    first,
    fringes,
    come_ref,
    slots_ref,
    flux_ref,
    local_ref,
    back_ref,
    where_ref,
    part_ref,
    size_ref,
    lift_ref,
    out_ref,
    turn,
    turned,
    wide,
):
    remote = parts * capacity
    row = lax.broadcasted_iota(jnp.int32, (ROWS, LANES), 0)
    lane = lax.broadcasted_iota(jnp.int32, (ROWS, LANES), 1)
    is_remote = (lane < remote) & (row < 25)
    is_outer = lane < remote + fringes
    spread = jnp.clip(jnp.minimum(row, 24) * fringes + lane - remote, 0, LANES - 1)
    source = where_ref[0]
    place = where_ref[1]
    fringe = []
    for v in range(5):
        sent = come_ref[pl.ds(first + v, parts, stride=rows), :]
        total = jnp.zeros((8, LANES), jnp.float32)
        for q in range(parts):
            picked = lane_gather(jnp.broadcast_to(sent[q : q + 1], (8, LANES)), place)
            total = jnp.where(source == q, picked, total)
        fringe.append(total)
    turn[...] = jnp.zeros_like(turn)
    turned[LANES:, :] = jnp.zeros((8, LANES), jnp.float32)
    for k in range(6):
        d = k // 2
        other = k ^ 1
        for s in range(capacity):
            turn[s * parts : (s + 1) * parts, :] = come_ref[
                pl.ds(other * capacity + s, parts, stride=rows), :
            ]
        turned[:LANES, :] = turn[...].T
        own = [slots_ref[k, v] for v in range(5)]
        theirs = []
        for v in range(5):
            outer = lane_gather(jnp.broadcast_to(fringe[v][k : k + 1], (ROWS, LANES)), spread)
            outer = jnp.where(is_outer, outer, slots_ref[other, v])
            theirs.append(jnp.where(is_remote, turned[25 * v : 25 * v + ROWS, :], outer))
        their_flux, their_wave = euler_wave(theirs, d)
        own_flux = [flux_ref[k, v] for v in range(5)]
        own_wave = flux_ref[k, 5]
        if k % 2:
            common = mix(own, own_flux, own_wave, theirs, their_flux, their_wave)
        else:
            common = mix(theirs, their_flux, their_wave, own, own_flux, own_wave)
        index = jnp.broadcast_to(back_ref[k : k + 1, :], (ROWS, LANES))
        scale = size_ref[d : d + 1, :]
        for v in range(5):
            value = jnp.where(is_outer, common[v], local_ref[d, v])
            wide[k * ROWS : (k + 1) * ROWS, v * LANES : (v + 1) * LANES] = (
                lane_gather(value, index) * scale
            )
    total = part_ref[...] + jnp.dot(
        lift_ref[...], wide[...], precision=precise, preferred_element_type=jnp.float32
    )
    for v in range(5):
        out_ref[v] = total[:, v * LANES : (v + 1) * LANES]


def call(kernel, name, out_shape, scratch, flops, size, *operands):
    return pl.pallas_call(
        kernel,
        name=name,
        out_shape=out_shape,
        scratch_shapes=scratch,
        compiler_params=pltpu.CompilerParams(vmem_limit_bytes=VMEM),
        cost_estimate=pl.CostEstimate(flops=flops, bytes_accessed=size, transcendentals=0),
    )(*operands)


def body(state, inv_size, plus_order, minus_order, donor_cell, donor_weights, recv_slot):
    columns = state.shape[-1]
    parts = lax.axis_size("dom")
    grids = lax.axis_size("grid")
    capacity = max(1, columns // (3 * parts))
    remote = parts * capacity
    fringes = recv_slot.shape[-1] // 150
    total = donor_cell.shape[-1]
    count = total // (grids * parts)
    padded = -(-total // LANES) * LANES
    first = -(-6 * capacity // 8) * 8
    rows = first + 8
    faces, volume, lift, expand = matrices()
    lanes = np.arange(LANES)
    lanes[:remote] = (lanes[:remote] % parts) * capacity + lanes[:remote] // parts
    lanes = np.ascontiguousarray(np.broadcast_to(lanes.astype(np.int32), (8, LANES)))
    f32 = functools.partial(jax.ShapeDtypeStruct, dtype=jnp.float32)
    i32 = functools.partial(jax.ShapeDtypeStruct, dtype=jnp.int32)

    sent = call(
        functools.partial(donor_kernel, grids, parts, count),
        "donors",
        tuple(f32((parts, 8, LANES)) for _ in range(grids - 1)),
        [
            pltpu.VMEM((8, padded), jnp.int32),
            pltpu.VMEM((16, padded), jnp.float32),
            pltpu.VMEM((8, padded), jnp.float32),
            pltpu.VMEM((8, LANES), jnp.float32),
        ],
        5_000_000,
        500_000,
        state,
        donor_cell,
        donor_weights.reshape(15, 1, total),
        expand,
    )
    arrived = [
        lax.ppermute(sent[step - 1], "grid", [(g, partner(g, step, grids)) for g in range(grids)])
        for step in range(1, grids)
    ]
    slots, pay = call(
        functools.partial(face_kernel, parts, capacity, rows),
        "faces",
        (f32((6, 5, ROWS, LANES)), f32((parts * rows, LANES))),
        [pltpu.VMEM((LANES, LANES), jnp.float32)],
        200_000_000,
        1_500_000,
        state,
        plus_order,
        minus_order,
        faces,
        lanes,
    )
    merged = arrived[0]
    for extra in arrived[1:]:
        merged = merged + extra
    pay = lax.dynamic_update_slice(pay.reshape(parts, rows, LANES), merged, (0, first, 0))
    come = lax.all_to_all(pay, "dom", split_axis=0, concat_axis=0, tiled=True)
    part, flux, local, back, where = call(
        functools.partial(volume_kernel, grids, parts, count),
        "volume",
        (
            f32((125, 5 * LANES)),
            f32((6, 6, ROWS, LANES)),
            f32((3, 5, ROWS, LANES)),
            i32((8, LANES)),
            i32((2, 8, LANES)),
        ),
        [pltpu.VMEM((3 * LANES, 5 * LANES), jnp.float32), pltpu.VMEM((LANES, LANES), jnp.float32)],
        400_000_000,
        3_000_000,
        state,
        inv_size,
        plus_order,
        minus_order,
        recv_slot,
        slots,
        volume,
        lanes,
    )
    return call(
        functools.partial(finish_kernel, parts, capacity, rows, first, fringes),
        "finish",
        f32((5, 125, columns)),
        [
            pltpu.VMEM((LANES, LANES), jnp.float32),
            pltpu.VMEM((LANES + 8, LANES), jnp.float32),
            pltpu.VMEM((6 * ROWS, 5 * LANES), jnp.float32),
        ],
        200_000_000,
        3_000_000,
        come.reshape(parts * rows, LANES),
        slots,
        flux,
        local,
        back,
        where,
        part,
        inv_size,
        lift,
    )


def solution(mesh):
    return jax.shard_map(
        body,
        mesh=mesh,
        in_specs=(
            P(None, None, ("grid", "dom")),
            P(None, ("grid", "dom")),
            P(None, ("grid", "dom")),
            P(None, ("grid", "dom")),
            P(("grid", "dom"), None),
            P(("grid", "dom"), None, None, None),
            P(("grid", "dom"), None),
        ),
        out_specs=P(None, None, ("grid", "dom")),
        check_vma=False,
    )
```

```python
import functools
import math

import jax
import jax.numpy as jnp
import numpy as np
from jax import lax
from jax.experimental import pallas as pl
from jax.experimental.pallas import tpu as pltpu
from jax.sharding import PartitionSpec as P

precise = lax.Precision.HIGHEST
closer = lax.Precision.HIGH
LANES = 128
ROWS = 32
VMEM = 48 * 1024 * 1024


def gauss_nodes():
    outer = math.sqrt(5.0 + 2.0 * math.sqrt(10.0 / 7.0)) / 3.0
    inner = math.sqrt(5.0 - 2.0 * math.sqrt(10.0 / 7.0)) / 3.0
    return [-outer, -inner, 0.0, inner, outer]


def basis_value(nodes, column, target):
    value = 1.0
    for other in range(5):
        if other != column:
            value = value * (target - nodes[other]) / (nodes[column] - nodes[other])
    return value


def basis_slope(nodes, column, target):
    total = 0.0
    for skipped in range(5):
        if skipped != column:
            value = 1.0 / (nodes[column] - nodes[skipped])
            for other in range(5):
                if other != column and other != skipped:
                    value = value * (target - nodes[other]) / (nodes[column] - nodes[other])
            total = total + value
    return total


def legendre_slopes(target):
    values = [1.0, target]
    slopes = [0.0, 1.0]
    for order in range(1, 5):
        values.append(
            ((2 * order + 1) * target * values[order] - order * values[order - 1]) / (order + 1)
        )
        slopes.append(slopes[order - 1] + (2 * order + 1) * values[order])
    return (slopes[4], slopes[5])


def tables():
    nodes = gauss_nodes()
    deriv = [[basis_slope(nodes, column, nodes[row]) for column in range(5)] for row in range(5)]
    lower = [basis_value(nodes, column, -1.0) for column in range(5)]
    upper = [basis_value(nodes, column, 1.0) for column in range(5)]
    lift_low = []
    lift_high = []
    for row in range(5):
        slope_four, slope_five = legendre_slopes(nodes[row])
        lift_low.append(-0.5 * (slope_five - slope_four))
        lift_high.append(0.5 * (slope_five + slope_four))
    return tuple(np.asarray(m, np.float64) for m in (deriv, lower, upper, lift_low, lift_high))


def split_point(point, direction):
    index = [point // 25, point // 5 % 5, point % 5]
    along = index.pop(direction)
    return along, 5 * index[0] + index[1]


def matrices():
    deriv, lower, upper, lift_low, lift_high = tables()
    faces = np.zeros((6 * ROWS, 125))
    volume = np.zeros((125, 3 * LANES))
    lift = np.zeros((125, 6 * ROWS))
    own = deriv - np.outer(lift_low, lower) - np.outer(lift_high, upper)
    for d in range(3):
        for p in range(125):
            i, t = split_point(p, d)
            faces[(2 * d) * ROWS + t, p] = lower[i]
            faces[(2 * d + 1) * ROWS + t, p] = upper[i]
            lift[p, (2 * d) * ROWS + t] = -lift_low[i]
            lift[p, (2 * d + 1) * ROWS + t] = -lift_high[i]
            for other in range(125):
                m, line = split_point(other, d)
                if line == t:
                    volume[p, d * LANES + other] = -own[i, m]
    for k in range(6):
        faces[k * ROWS + 25 : (k + 1) * ROWS] = faces[k * ROWS + 24]
    expand = np.zeros((3 * LANES, 48))
    for p in range(125):
        for axis, index in enumerate((p // 25, p // 5 % 5, p % 5)):
            for part in range(3):
                expand[axis * LANES + p, 16 * part + 5 * axis + index] = 1.0
    return tuple(m.astype(np.float32) for m in (faces, volume, lift, expand))


def slot_lanes(parts, capacity, fringes):
    remote = parts * capacity
    lanes = np.zeros((8, LANES), np.int32)
    for d in range(3):
        held = {}
        for lane in range(remote):
            held[d * remote + lane] = lane % parts * capacity + lane // parts
        for i in range(fringes):
            held[(3 * remote + d * fringes + i) % LANES] = remote + i
        free = iter(range(remote + fringes, LANES))
        for lane in range(LANES):
            lanes[d, lane] = held[lane] if lane in held else next(free)
    return lanes


def fringe_lanes(fringes):
    found = np.zeros((8, LANES), np.int32)
    for side in range(2):
        for t in range(ROWS):
            for d in range(3):
                for i in range(fringes):
                    point = ((2 * d + side) * 25 + min(t, 24)) * fringes + i
                    found[side * 4 + t // 8, (t % 8 * 3 + d) * fringes + i] = point
    return found


def partner(index, step, count):
    if count & (count - 1) == 0:
        return index ^ step
    return (index + step) % count


def lane_gather(values, index):
    return jnp.take_along_axis(values, index, axis=1, mode="promise_in_bounds")


def in_lanes(lane, start, width):
    start = start % LANES
    if start + width <= LANES:
        return (lane >= start) & (lane < start + width)
    return (lane >= start) | (lane < start + width - LANES)


def euler(state, choose, along):
    density, momenta, energy = state[0], state[1:4], state[4]
    inverse = 1.0 / density
    normal = choose(momenta)
    speed = normal * inverse
    squares = momenta[0] * momenta[0] + momenta[1] * momenta[1] + momenta[2] * momenta[2]
    pressure = 0.4 * (energy - 0.5 * squares * inverse)
    flux = [normal] + [m * speed for m in momenta] + [(energy + pressure) * speed]
    for d in range(3):
        flux[1 + d] = along(d, flux[1 + d], pressure - 1.0)
    return flux, speed, pressure, inverse


def euler_wave(state, choose, along):
    flux, speed, pressure, inverse = euler(state, choose, along)
    return flux, jnp.abs(speed) + jnp.sqrt(1.4 * pressure * inverse)


def fixed(direction):
    def choose(parts):
        return parts[direction]

    def along(d, flux, pressure):
        return flux + pressure if d == direction else flux

    return choose, along


def by_lane(first, second):
    def choose(parts):
        return jnp.where(first, parts[0], jnp.where(second, parts[1], parts[2]))

    third = ~(first | second)

    def along(d, flux, pressure):
        return flux + jnp.where((first, second, third)[d], pressure, 0.0)

    return choose, along


def mix(left, left_flux, left_wave, right, right_flux, right_wave):
    wave = 0.5 * jnp.maximum(left_wave, right_wave)
    return [
        0.5 * (left_flux[v] + right_flux[v]) - wave * (right[v] - left[v]) for v in range(5)
    ]


def donor_kernel(grids, parts, count, *refs):
    inputs = refs[:4]
    outs = refs[4 : 3 + grids]
    copies = refs[3 + grids : 7 + grids]
    cells, weights, values, done = refs[7 + grids :]
    moves = [
        pltpu.make_async_copy(source, target, done.at[k])
        for k, (source, target) in enumerate(zip(inputs, copies))
    ]
    for move in moves:
        move.start()
    state, cell, weight, expand = copies
    total = grids * parts * count
    padded = cells.shape[1]
    cells[...] = jnp.zeros_like(cells)
    weights[...] = jnp.zeros_like(weights)
    moves[1].wait()
    cells[0:1, :total] = cell[...]
    moves[2].wait()
    for k in range(15):
        weights[k : k + 1, :total] = weight[k]
    high = weights[...].astype(jnp.bfloat16)
    rest = weights[...] - high.astype(jnp.float32)
    middle = rest.astype(jnp.bfloat16)
    low = (rest - middle.astype(jnp.float32)).astype(jnp.bfloat16)
    pieces = jnp.concatenate([high, middle, low], axis=0)
    moves[3].wait()
    wide = jnp.dot(expand[...], pieces, preferred_element_type=jnp.float32)
    weight = (wide[:LANES] * wide[LANES : 2 * LANES] * wide[2 * LANES :])[:125]
    element = lax.broadcasted_iota(jnp.int32, (LANES, padded), 0)
    chosen = jnp.where(element == cells[0:1, :], 1.0, 0.0).astype(jnp.bfloat16)
    chosen = jnp.concatenate([chosen, chosen], axis=0)
    moves[0].wait()
    for v in range(5):
        shift = (1.0, 0.0, 0.0, 0.0, 2.5)[v]
        shifted = state[v] - shift
        high = shifted.astype(jnp.bfloat16)
        low = (shifted - high.astype(jnp.float32)).astype(jnp.bfloat16)
        halves = jnp.concatenate([high, low], axis=1)
        picked = jnp.dot(halves, chosen, preferred_element_type=jnp.float32)
        values[v : v + 1, :] = jnp.sum(picked * weight, axis=0, keepdims=True) + shift
    lane = lax.broadcasted_iota(jnp.int32, (8, LANES), 1)
    me = lax.axis_index("grid")
    for step in range(1, grids):
        wanted = in_lanes(lane, (step - 1) * count, count)
        for g in range(grids):

            @pl.when(partner(me, step, grids) == g)
            def _():
                for q in range(parts):
                    start = (g * parts + q) * count
                    block = start // LANES * LANES
                    width = min(2 * LANES, padded - block)
                    pair = values[:, block : block + width]
                    shift = ((step - 1) * count - (start - block)) % width
                    moved = pltpu.roll(pair, shift, 1)[:, :LANES] if shift else pair[:, :LANES]
                    outs[step - 1][q] = jnp.where(wanted, moved, 0.0)


def face_kernel(
    parts,
    capacity,
    rows,
    state_ref,
    plus_ref,
    minus_ref,
    faces_ref,
    lanes_ref,
    slots_ref,
    both_ref,
    pay_ref,
    turn,
):
    remote = parts * capacity
    wide = jnp.concatenate([state_ref[v] for v in range(5)], axis=1)
    face = jnp.dot(
        faces_ref[...], wide, precision=precise, preferred_element_type=jnp.float32
    )
    for side in range(2):
        order = (minus_ref, plus_ref)[side]
        for d in range(3):
            k = 2 * d + side
            index = lane_gather(
                jnp.broadcast_to(order[d : d + 1, :], (ROWS, LANES)),
                jnp.broadcast_to(lanes_ref[d : d + 1, :], (ROWS, LANES)),
            )
            for v in range(5):
                block = face[k * ROWS : (k + 1) * ROWS, v * LANES : (v + 1) * LANES]
                slots_ref[k, v] = lane_gather(block, index)
    lane = lax.broadcasted_iota(jnp.int32, (ROWS, LANES), 1)
    turn[:, 120:128, :] = jnp.zeros((2, 8, LANES), jnp.float32)
    for side in range(2):
        for v in range(5):
            both = jnp.where(
                lane < remote,
                slots_ref[side, v],
                jnp.where(lane < 2 * remote, slots_ref[2 + side, v], slots_ref[4 + side, v]),
            )
            both_ref[side, v] = both
            turn[side, 25 * v : 25 * v + 25, :] = both[:25]
        turned = turn[side].T
        for d in range(3):
            for s in range(capacity):
                start = d * remote + s * parts
                pay_ref[pl.ds((2 * d + side) * capacity + s, parts, stride=rows), :] = turned[
                    start : start + parts
                ]


def merge_kernel(parts, rows, first, pay_ref, *refs):
    out_ref = refs[-1]
    for q in range(parts):
        total = refs[0][q]
        for extra in refs[1:-1]:
            total = total + extra[q]
        out_ref[q * rows : q * rows + first, :] = pay_ref[q * rows : q * rows + first, :]
        out_ref[q * rows + first : q * rows + first + 8, :] = total


def volume_kernel(
    grids,
    parts,
    count,
    remote,
    fringes,
    state_ref,
    size_ref,
    plus_ref,
    minus_ref,
    recv_ref,
    slots_ref,
    both_ref,
    volume_ref,
    lanes_ref,
    points_ref,
    part_ref,
    flux_ref,
    edge_ref,
    local_ref,
    back_ref,
    where_ref,
    wide,
    index,
    received,
):
    state = [state_ref[v] for v in range(5)]
    for d in range(3):
        flux = euler(state, *fixed(d))[0]
        scale = size_ref[d : d + 1, :]
        wide[d * LANES + 120 : (d + 1) * LANES, :] = jnp.zeros((8, 5 * LANES), jnp.float32)
        for v in range(5):
            wide[d * LANES : d * LANES + 125, v * LANES : (v + 1) * LANES] = flux[v] * scale
    part_ref[...] = jnp.dot(
        volume_ref[...], wide[...], precision=closer, preferred_element_type=jnp.float32
    )
    for d in range(3):
        low = [slots_ref[2 * d, v] for v in range(5)]
        high = [slots_ref[2 * d + 1, v] for v in range(5)]
        low_flux, low_wave = euler_wave(low, *fixed(d))
        high_flux, high_wave = euler_wave(high, *fixed(d))
        local = mix(high, high_flux, high_wave, low, low_flux, low_wave)
        for v in range(5):
            local_ref[d, v] = local[v]
    lane = lax.broadcasted_iota(jnp.int32, (ROWS, LANES), 1)
    for side in range(2):
        own = [both_ref[side, v] for v in range(5)]
        flux, wave = euler_wave(own, *by_lane(lane < remote, in_lanes(lane, remote, remote)))
        for v in range(5):
            flux_ref[side, v] = flux[v]
        flux_ref[side, 5] = wave
        second = in_lanes(lane, 3 * remote + fringes, fringes)
        third = in_lanes(lane, 3 * remote + 2 * fringes, fringes)
        edge = [
            jnp.where(
                second,
                slots_ref[2 + side, v],
                jnp.where(third, slots_ref[4 + side, v], slots_ref[side, v]),
            )
            for v in range(5)
        ]
        flux, wave = euler_wave(edge, *by_lane(~(second | third), second))
        for v in range(5):
            edge_ref[side, v] = edge[v]
            edge_ref[side, 5 + v] = flux[v]
        edge_ref[side, 10] = wave
    rank = lax.broadcasted_iota(jnp.int32, (LANES, LANES), 0)
    column = lax.broadcasted_iota(jnp.int32, (LANES, LANES), 1)
    index[...] = jnp.zeros_like(index)
    for k in range(6):
        d = k // 2
        order = lane_gather(
            jnp.broadcast_to((minus_ref, plus_ref)[k % 2][d : d + 1, :], (8, LANES)),
            jnp.broadcast_to(lanes_ref[d : d + 1, :], (8, LANES)),
        )
        index[k : k + 1, :] = order[0:1].astype(jnp.float32)
    turned = index[...].T.astype(jnp.int32)
    back_ref[...] = jnp.zeros_like(back_ref)
    for k in range(6):
        found = jnp.where(turned[:, k : k + 1] == column, rank, 0)
        back_ref[k : k + 1, :] = jnp.sum(found, axis=0, keepdims=True)
    me = lax.axis_index("grid")
    received[...] = jnp.zeros_like(received)
    received[0:1, : recv_ref.shape[1]] = recv_ref[...]
    points = points_ref[...]
    slot = jnp.zeros((8, LANES), jnp.int32)
    for block in range(received.shape[1] // LANES):
        held = jnp.broadcast_to(received[0:1, block * LANES : (block + 1) * LANES], (8, LANES))
        inside = (points >= block * LANES) & (points < (block + 1) * LANES)
        picked = lane_gather(held, jnp.where(inside, points - block * LANES, 0))
        slot = jnp.where(inside, picked, slot)
    device = ((slot.astype(jnp.float32) + 0.5) * (1.0 / count)).astype(jnp.int32)
    rest = slot - device * count
    grid = ((device.astype(jnp.float32) + 0.5) * (1.0 / parts)).astype(jnp.int32)
    step = jnp.zeros_like(grid)
    for g in range(grids):
        if grids & (grids - 1) == 0:
            away = me ^ g
        else:
            away = lax.rem(me + grids - g, grids)
        step = jnp.where(grid == g, away, step)
    where_ref[0] = device - grid * parts
    where_ref[1] = jnp.maximum(step - 1, 0) * count + rest


def finish_kernel(
    parts,
    capacity,
    rows,
    first,
    fringes,
    come_ref,
    both_ref,
    flux_ref,
    edge_ref,
    local_ref,
    back_ref,
    where_ref,
    part_ref,
    size_ref,
    lift_ref,
    out_ref,
    turn,
    turned,
    wide,
):
    remote = parts * capacity
    row = lax.broadcasted_iota(jnp.int32, (ROWS, LANES), 0)
    lane = lax.broadcasted_iota(jnp.int32, (ROWS, LANES), 1)
    is_remote = [in_lanes(lane, d * remote, remote) for d in range(3)]
    is_fringe = [in_lanes(lane, 3 * remote + d * fringes, fringes) for d in range(3)]
    any_remote = (lane < 3 * remote) & (row < 25)
    any_fringe = is_fringe[0] | is_fringe[1] | is_fringe[2]
    spread = row[:8] * (3 * fringes) + ((lane[:8] - 3 * remote) & (LANES - 1))
    spread = jnp.where(any_fringe[:8], spread, 0)
    for side in range(2):
        for d in range(3):
            for s in range(capacity):
                start = d * remote + s * parts
                turn[side, start : start + parts, :] = come_ref[
                    pl.ds((2 * d + 1 - side) * capacity + s, parts, stride=rows), :
                ]
        turned[side, :LANES, :] = turn[side].T
    fringe = []
    for v in range(5):
        sent = come_ref[pl.ds(first + v, parts, stride=rows), :]
        total = jnp.zeros((8, LANES), jnp.float32)
        for q in range(parts):
            picked = lane_gather(jnp.broadcast_to(sent[q : q + 1], (8, LANES)), where_ref[1])
            total = jnp.where(where_ref[0] == q, picked, total)
        fringe.append(total)
    for side in range(2):
        own = [both_ref[side, v] for v in range(5)]
        theirs = [
            jnp.where(any_remote, turned[side, 25 * v : 25 * v + ROWS, :], own[v])
            for v in range(5)
        ]
        their = (theirs, *euler_wave(theirs, *by_lane(is_remote[0], is_remote[1])))
        mine = (own, [flux_ref[side, v] for v in range(5)], flux_ref[side, 5])
        common = mix(*mine, *their) if side else mix(*their, *mine)
        own = [edge_ref[side, v] for v in range(5)]
        theirs = []
        for v in range(5):
            pieces = [
                lane_gather(
                    jnp.broadcast_to(fringe[v][side * 4 + r : side * 4 + r + 1], (8, LANES)), spread
                )
                for r in range(4)
            ]
            theirs.append(jnp.where(any_fringe, jnp.concatenate(pieces, axis=0), own[v]))
        their = (theirs, *euler_wave(theirs, *by_lane(~(is_fringe[1] | is_fringe[2]), is_fringe[1])))
        mine = (own, [edge_ref[side, 5 + v] for v in range(5)], edge_ref[side, 10])
        outer = mix(*mine, *their) if side else mix(*their, *mine)
        for d in range(3):
            k = 2 * d + side
            index = jnp.broadcast_to(back_ref[k : k + 1, :], (ROWS, LANES))
            scale = size_ref[d : d + 1, :]
            for v in range(5):
                value = jnp.where(is_fringe[d], outer[v], local_ref[d, v])
                value = jnp.where(is_remote[d], common[v], value)
                wide[k * ROWS : (k + 1) * ROWS, v * LANES : (v + 1) * LANES] = (
                    lane_gather(value, index) * scale
                )
    total = part_ref[...] + jnp.dot(
        lift_ref[...], wide[...], precision=closer, preferred_element_type=jnp.float32
    )
    for v in range(5):
        out_ref[v] = total[:, v * LANES : (v + 1) * LANES]


def call(kernel, name, out_shape, scratch, flops, size, *operands, limit=VMEM, **more):
    return pl.pallas_call(
        kernel,
        name=name,
        out_shape=out_shape,
        scratch_shapes=scratch,
        compiler_params=pltpu.CompilerParams(vmem_limit_bytes=limit),
        cost_estimate=pl.CostEstimate(flops=flops, bytes_accessed=size, transcendentals=0),
        **more,
    )(*operands)


def body(state, inv_size, plus_order, minus_order, donor_cell, donor_weights, recv_slot):
    columns = state.shape[-1]
    parts = lax.axis_size("dom")
    grids = lax.axis_size("grid")
    capacity = max(1, columns // (3 * parts))
    remote = parts * capacity
    fringes = recv_slot.shape[-1] // 150
    total = donor_cell.shape[-1]
    count = total // (grids * parts)
    padded = -(-total // LANES) * LANES
    held = -(-recv_slot.shape[-1] // LANES) * LANES
    first = -(-6 * capacity // 8) * 8
    rows = first + 8
    faces, volume, lift, expand = matrices()
    expand = jnp.asarray(expand, jnp.bfloat16)
    lanes = slot_lanes(parts, capacity, fringes)
    points = fringe_lanes(fringes)
    f32 = functools.partial(jax.ShapeDtypeStruct, dtype=jnp.float32)
    i32 = functools.partial(jax.ShapeDtypeStruct, dtype=jnp.int32)
    memory = functools.partial(pltpu.VMEM, dtype=jnp.float32)

    sent = call(
        functools.partial(donor_kernel, grids, parts, count),
        "donors",
        tuple(f32((parts, 8, LANES)) for _ in range(grids - 1)),
        [
            memory(state.shape),
            pltpu.VMEM(donor_cell.shape, jnp.int32),
            memory((15, 1, total)),
            pltpu.VMEM(expand.shape, jnp.bfloat16),
            pltpu.VMEM((8, padded), jnp.int32),
            memory((16, padded)),
            memory((8, padded)),
            pltpu.SemaphoreType.DMA((4,)),
        ],
        5_000_000,
        500_000,
        state,
        donor_cell,
        donor_weights.reshape(15, 1, total),
        expand,
        in_specs=[pl.BlockSpec(memory_space=pl.ANY)] * 4,
        limit=60 * 1024 * 1024,
    )
    arrived = [
        lax.ppermute(sent[step - 1], "grid", [(g, partner(g, step, grids)) for g in range(grids)])
        for step in (*range(2, grids), 1)
    ]
    slots, both, pay = call(
        functools.partial(face_kernel, parts, capacity, rows),
        "faces",
        (
            f32((6, 5, ROWS, LANES)),
            f32((2, 5, ROWS, LANES)),
            f32((parts * rows, LANES)),
        ),
        [memory((2, LANES, LANES))],
        200_000_000,
        1_500_000,
        state,
        plus_order,
        minus_order,
        faces,
        lanes,
    )
    pay = call(
        functools.partial(merge_kernel, parts, rows, first),
        "merge",
        f32((parts * rows, LANES)),
        [],
        50_000,
        200_000,
        pay,
        *arrived,
    )
    come = lax.all_to_all(
        pay.reshape(parts, rows, LANES), "dom", split_axis=0, concat_axis=0, tiled=True
    )
    part, flux, edge, local, back, where = call(
        functools.partial(volume_kernel, grids, parts, count, remote, fringes),
        "volume",
        (
            f32((125, 5 * LANES)),
            f32((2, 6, ROWS, LANES)),
            f32((2, 11, ROWS, LANES)),
            f32((3, 5, ROWS, LANES)),
            i32((8, LANES)),
            i32((2, 8, LANES)),
        ),
        [
            memory((3 * LANES, 5 * LANES)),
            memory((LANES, LANES)),
            pltpu.VMEM((8, held), jnp.int32),
        ],
        400_000_000,
        3_000_000,
        state,
        inv_size,
        plus_order,
        minus_order,
        recv_slot,
        slots,
        both,
        volume,
        lanes,
        points,
    )
    return call(
        functools.partial(finish_kernel, parts, capacity, rows, first, fringes),
        "finish",
        f32((5, 125, columns)),
        [
            memory((2, LANES, LANES)),
            memory((2, LANES + 8, LANES)),
            memory((6 * ROWS, 5 * LANES)),
        ],
        200_000_000,
        3_000_000,
        come.reshape(parts * rows, LANES),
        both,
        flux,
        edge,
        local,
        back,
        where,
        part,
        inv_size,
        lift,
    )


def solution(mesh):
    return jax.shard_map(
        body,
        mesh=mesh,
        in_specs=(
            P(None, None, ("grid", "dom")),
            P(None, ("grid", "dom")),
            P(None, ("grid", "dom")),
            P(None, ("grid", "dom")),
            P(("grid", "dom"), None),
            P(("grid", "dom"), None, None, None),
            P(("grid", "dom"), None),
        ),
        out_specs=P(None, None, ("grid", "dom")),
        check_vma=False,
    )
```

```python
import functools
import math

import jax
import jax.numpy as jnp
import numpy as np
from jax import lax
from jax.experimental import pallas as pl
from jax.experimental.pallas import tpu as pltpu
from jax.sharding import PartitionSpec as P

precise = lax.Precision.HIGHEST
closer = lax.Precision.HIGH
LANES = 128
ROWS = 32
VMEM = 48 * 1024 * 1024


def gauss_nodes():
    outer = math.sqrt(5.0 + 2.0 * math.sqrt(10.0 / 7.0)) / 3.0
    inner = math.sqrt(5.0 - 2.0 * math.sqrt(10.0 / 7.0)) / 3.0
    return [-outer, -inner, 0.0, inner, outer]


def basis_value(nodes, column, target):
    value = 1.0
    for other in range(5):
        if other != column:
            value = value * (target - nodes[other]) / (nodes[column] - nodes[other])
    return value


def basis_slope(nodes, column, target):
    total = 0.0
    for skipped in range(5):
        if skipped != column:
            value = 1.0 / (nodes[column] - nodes[skipped])
            for other in range(5):
                if other != column and other != skipped:
                    value = value * (target - nodes[other]) / (nodes[column] - nodes[other])
            total = total + value
    return total


def legendre_slopes(target):
    values = [1.0, target]
    slopes = [0.0, 1.0]
    for order in range(1, 5):
        values.append(
            ((2 * order + 1) * target * values[order] - order * values[order - 1]) / (order + 1)
        )
        slopes.append(slopes[order - 1] + (2 * order + 1) * values[order])
    return (slopes[4], slopes[5])


def tables():
    nodes = gauss_nodes()
    deriv = [[basis_slope(nodes, column, nodes[row]) for column in range(5)] for row in range(5)]
    lower = [basis_value(nodes, column, -1.0) for column in range(5)]
    upper = [basis_value(nodes, column, 1.0) for column in range(5)]
    lift_low = []
    lift_high = []
    for row in range(5):
        slope_four, slope_five = legendre_slopes(nodes[row])
        lift_low.append(-0.5 * (slope_five - slope_four))
        lift_high.append(0.5 * (slope_five + slope_four))
    return tuple(np.asarray(m, np.float64) for m in (deriv, lower, upper, lift_low, lift_high))


def split_point(point, direction):
    index = [point // 25, point // 5 % 5, point % 5]
    along = index.pop(direction)
    return along, 5 * index[0] + index[1]


def matrices():
    deriv, lower, upper, lift_low, lift_high = tables()
    faces = np.zeros((6 * ROWS, 125))
    volume = np.zeros((125, 3 * LANES))
    lift = np.zeros((125, 6 * ROWS))
    own = deriv - np.outer(lift_low, lower) - np.outer(lift_high, upper)
    for d in range(3):
        for p in range(125):
            i, t = split_point(p, d)
            faces[(2 * d) * ROWS + t, p] = lower[i]
            faces[(2 * d + 1) * ROWS + t, p] = upper[i]
            lift[p, (2 * d) * ROWS + t] = -lift_low[i]
            lift[p, (2 * d + 1) * ROWS + t] = -lift_high[i]
            for other in range(125):
                m, line = split_point(other, d)
                if line == t:
                    volume[p, d * LANES + other] = -own[i, m]
    for k in range(6):
        faces[k * ROWS + 25 : (k + 1) * ROWS] = faces[k * ROWS + 24]
    expand = np.zeros((2 * ROWS, 48))
    for r in range(ROWS):
        for part in range(3):
            expand[r, 16 * part + 5 + r % 25 // 5] = 1.0
            expand[ROWS + r, 16 * part + 10 + r % 5] = 1.0
    return tuple(m.astype(np.float32) for m in (faces, volume, lift, expand))


def slot_lanes(parts, capacity, fringes):
    remote = parts * capacity
    lanes = np.zeros((8, LANES), np.int32)
    for d in range(3):
        held = {}
        for lane in range(remote):
            held[d * remote + lane] = lane % parts * capacity + lane // parts
        for i in range(fringes):
            held[(3 * remote + d * fringes + i) % LANES] = remote + i
        free = iter(range(remote + fringes, LANES))
        for lane in range(LANES):
            lanes[d, lane] = held[lane] if lane in held else next(free)
    return lanes


def fringe_lanes(fringes):
    found = np.zeros((8, LANES), np.int32)
    for side in range(2):
        for t in range(ROWS):
            for d in range(3):
                for i in range(fringes):
                    point = ((2 * d + side) * 25 + min(t, 24)) * fringes + i
                    found[side * 4 + t // 8, (t % 8 * 3 + d) * fringes + i] = point
    return found


def partner(index, step, count):
    if count & (count - 1) == 0:
        return index ^ step
    return (index + step) % count


def lane_gather(values, index):
    return jnp.take_along_axis(values, index, axis=1, mode="promise_in_bounds")


def in_lanes(lane, start, width):
    start = start % LANES
    if start + width <= LANES:
        return (lane >= start) & (lane < start + width)
    return (lane >= start) | (lane < start + width - LANES)


def euler(state, choose, along):
    density, momenta, energy = state[0], state[1:4], state[4]
    inverse = 1.0 / density
    normal = choose(momenta)
    speed = normal * inverse
    squares = momenta[0] * momenta[0] + momenta[1] * momenta[1] + momenta[2] * momenta[2]
    pressure = 0.4 * (energy - 0.5 * squares * inverse)
    flux = [normal] + [m * speed for m in momenta] + [(energy + pressure) * speed]
    for d in range(3):
        flux[1 + d] = along(d, flux[1 + d], pressure - 1.0)
    return flux, speed, pressure, inverse


def euler_wave(state, choose, along):
    flux, speed, pressure, inverse = euler(state, choose, along)
    return flux, jnp.abs(speed) + jnp.sqrt(1.4 * pressure * inverse)


def fixed(direction):
    def choose(parts):
        return parts[direction]

    def along(d, flux, pressure):
        return flux + pressure if d == direction else flux

    return choose, along


def by_lane(first, second):
    def choose(parts):
        return jnp.where(first, parts[0], jnp.where(second, parts[1], parts[2]))

    third = ~(first | second)

    def along(d, flux, pressure):
        return flux + jnp.where((first, second, third)[d], pressure, 0.0)

    return choose, along


def mix(left, left_flux, left_wave, right, right_flux, right_wave):
    wave = 0.5 * jnp.maximum(left_wave, right_wave)
    return [
        0.5 * (left_flux[v] + right_flux[v]) - wave * (right[v] - left[v]) for v in range(5)
    ]


def donor_kernel(grids, parts, count, *refs):
    inputs = refs[:4]
    outs = refs[4 : 3 + grids]
    copies = refs[3 + grids : 7 + grids]
    cells, weights, planes, values, done = refs[7 + grids :]
    moves = [
        pltpu.make_async_copy(source, target, done.at[k])
        for k, (source, target) in enumerate(zip(inputs, copies))
    ]
    for move in moves:
        move.start()
    state, cell, weight, expand = copies
    total = grids * parts * count
    padded = cells.shape[1]
    cells[...] = jnp.zeros_like(cells)
    weights[...] = jnp.zeros_like(weights)
    moves[1].wait()
    cells[0:1, :total] = cell[...]
    element = lax.broadcasted_iota(jnp.int32, (LANES, padded), 0)
    chosen = jnp.where(element == cells[0:1, :], 1.0, 0.0).astype(jnp.bfloat16)
    chosen = jnp.concatenate([chosen, chosen], axis=0)
    moves[2].wait()
    for k in range(15):
        weights[k : k + 1, :total] = weight[k]
    high = weights[...].astype(jnp.bfloat16)
    rest = weights[...] - high.astype(jnp.float32)
    middle = rest.astype(jnp.bfloat16)
    low = (rest - middle.astype(jnp.float32)).astype(jnp.bfloat16)
    pieces = jnp.concatenate([high, middle, low], axis=0)
    moves[3].wait()
    plane = jnp.dot(expand[...], pieces, preferred_element_type=jnp.float32)
    planes[...] = plane[:ROWS] * plane[ROWS:]
    row = lax.broadcasted_iota(jnp.int32, (8, padded), 0)
    tiles = []
    for start in range(0, LANES, 8):
        a = start // 25
        outer = jnp.broadcast_to(weights[a : a + 1, :], (8, padded))
        if start < 25 * (a + 1) < start + 8 and a < 4:
            later = jnp.broadcast_to(weights[a + 1 : a + 2, :], (8, padded))
            outer = jnp.where(row < 25 * (a + 1) - start, outer, later)
        tiles.append(outer * planes[start % 25 : start % 25 + 8, :])
    weight = jnp.concatenate(tiles, axis=0)[:125]
    moves[0].wait()
    for v in range(5):
        shift = (1.0, 0.0, 0.0, 0.0, 2.5)[v]
        shifted = state[v] - shift
        high = shifted.astype(jnp.bfloat16)
        low = (shifted - high.astype(jnp.float32)).astype(jnp.bfloat16)
        halves = jnp.concatenate([high, low], axis=1)
        picked = jnp.dot(halves, chosen, preferred_element_type=jnp.float32)
        total = jnp.sum(picked * weight, axis=0, keepdims=True) + shift
        for block in range(padded // LANES):
            values[block, v : v + 1, :] = total[:, block * LANES : (block + 1) * LANES]
    lane = lax.broadcasted_iota(jnp.int32, (8, LANES), 1)
    me = lax.axis_index("grid")
    for step in range(1, grids):
        wanted = in_lanes(lane, (step - 1) * count, count)
        for q in range(parts):
            start = (partner(me, step, grids) * parts + q) * count
            block = start // LANES
            index = lane + (start - block * LANES - (step - 1) * count)
            inside = index & (LANES - 1)
            near = lane_gather(values[block], inside)
            far = lane_gather(values[block + 1], inside)
            outs[step - 1][q] = jnp.where(wanted, jnp.where(index < LANES, near, far), 0.0)


def face_kernel(
    parts,
    capacity,
    rows,
    state_ref,
    plus_ref,
    minus_ref,
    faces_ref,
    lanes_ref,
    slots_ref,
    both_ref,
    pay_ref,
    turn,
):
    remote = parts * capacity
    wide = jnp.concatenate([state_ref[v] for v in range(5)], axis=1)
    face = jnp.dot(
        faces_ref[...], wide, precision=precise, preferred_element_type=jnp.float32
    )
    for side in range(2):
        order = (minus_ref, plus_ref)[side]
        for d in range(3):
            k = 2 * d + side
            index = lane_gather(
                jnp.broadcast_to(order[d : d + 1, :], (ROWS, LANES)),
                jnp.broadcast_to(lanes_ref[d : d + 1, :], (ROWS, LANES)),
            )
            for v in range(5):
                block = face[k * ROWS : (k + 1) * ROWS, v * LANES : (v + 1) * LANES]
                slots_ref[k, v] = lane_gather(block, index)
    lane = lax.broadcasted_iota(jnp.int32, (ROWS, LANES), 1)
    turn[:, 120:128, :] = jnp.zeros((2, 8, LANES), jnp.float32)
    for side in range(2):
        for v in range(5):
            both = jnp.where(
                lane < remote,
                slots_ref[side, v],
                jnp.where(lane < 2 * remote, slots_ref[2 + side, v], slots_ref[4 + side, v]),
            )
            both_ref[side, v] = both
            turn[side, 25 * v : 25 * v + 25, :] = both[:25]
        turned = turn[side].T
        for d in range(3):
            for s in range(capacity):
                start = d * remote + s * parts
                pay_ref[pl.ds((2 * d + side) * capacity + s, parts, stride=rows), :] = turned[
                    start : start + parts
                ]


def merge_kernel(parts, rows, first, pay_ref, *refs):
    out_ref = refs[-1]
    for q in range(parts):
        total = refs[0][q]
        for extra in refs[1:-1]:
            total = total + extra[q]
        out_ref[q * rows : q * rows + first, :] = pay_ref[q * rows : q * rows + first, :]
        out_ref[q * rows + first : q * rows + first + 8, :] = total


def volume_kernel(
    grids,
    parts,
    count,
    remote,
    fringes,
    state_ref,
    size_ref,
    plus_ref,
    minus_ref,
    recv_ref,
    slots_ref,
    both_ref,
    volume_ref,
    lanes_ref,
    points_ref,
    part_ref,
    flux_ref,
    edge_ref,
    local_ref,
    back_ref,
    where_ref,
    wide,
    index,
    received,
):
    state = [state_ref[v] for v in range(5)]
    for d in range(3):
        flux = euler(state, *fixed(d))[0]
        scale = size_ref[d : d + 1, :]
        wide[d * LANES + 120 : (d + 1) * LANES, :] = jnp.zeros((8, 5 * LANES), jnp.float32)
        for v in range(5):
            wide[d * LANES : d * LANES + 125, v * LANES : (v + 1) * LANES] = flux[v] * scale
    part_ref[...] = jnp.dot(
        volume_ref[...], wide[...], precision=closer, preferred_element_type=jnp.float32
    )
    for d in range(3):
        low = [slots_ref[2 * d, v] for v in range(5)]
        high = [slots_ref[2 * d + 1, v] for v in range(5)]
        low_flux, low_wave = euler_wave(low, *fixed(d))
        high_flux, high_wave = euler_wave(high, *fixed(d))
        local = mix(high, high_flux, high_wave, low, low_flux, low_wave)
        for v in range(5):
            local_ref[d, v] = local[v]
    lane = lax.broadcasted_iota(jnp.int32, (ROWS, LANES), 1)
    for side in range(2):
        own = [both_ref[side, v] for v in range(5)]
        flux, wave = euler_wave(own, *by_lane(lane < remote, in_lanes(lane, remote, remote)))
        for v in range(5):
            flux_ref[side, v] = flux[v]
        flux_ref[side, 5] = wave
        second = in_lanes(lane, 3 * remote + fringes, fringes)
        third = in_lanes(lane, 3 * remote + 2 * fringes, fringes)
        edge = [
            jnp.where(
                second,
                slots_ref[2 + side, v],
                jnp.where(third, slots_ref[4 + side, v], slots_ref[side, v]),
            )
            for v in range(5)
        ]
        flux, wave = euler_wave(edge, *by_lane(~(second | third), second))
        for v in range(5):
            edge_ref[side, v] = edge[v]
            edge_ref[side, 5 + v] = flux[v]
        edge_ref[side, 10] = wave
    rank = lax.broadcasted_iota(jnp.int32, (LANES, LANES), 0)
    column = lax.broadcasted_iota(jnp.int32, (LANES, LANES), 1)
    index[...] = jnp.zeros_like(index)
    for k in range(6):
        d = k // 2
        order = lane_gather(
            jnp.broadcast_to((minus_ref, plus_ref)[k % 2][d : d + 1, :], (8, LANES)),
            jnp.broadcast_to(lanes_ref[d : d + 1, :], (8, LANES)),
        )
        index[k : k + 1, :] = order[0:1].astype(jnp.float32)
    turned = index[...].T.astype(jnp.int32)
    back_ref[...] = jnp.zeros_like(back_ref)
    for k in range(6):
        found = jnp.where(turned[:, k : k + 1] == column, rank, 0)
        back_ref[k : k + 1, :] = jnp.sum(found, axis=0, keepdims=True)
    me = lax.axis_index("grid")
    received[...] = jnp.zeros_like(received)
    received[0:1, : recv_ref.shape[1]] = recv_ref[...]
    points = points_ref[...]
    slot = jnp.zeros((8, LANES), jnp.int32)
    for block in range(received.shape[1] // LANES):
        held = jnp.broadcast_to(received[0:1, block * LANES : (block + 1) * LANES], (8, LANES))
        inside = (points >= block * LANES) & (points < (block + 1) * LANES)
        picked = lane_gather(held, jnp.where(inside, points - block * LANES, 0))
        slot = jnp.where(inside, picked, slot)
    device = ((slot.astype(jnp.float32) + 0.5) * (1.0 / count)).astype(jnp.int32)
    rest = slot - device * count
    grid = ((device.astype(jnp.float32) + 0.5) * (1.0 / parts)).astype(jnp.int32)
    step = jnp.zeros_like(grid)
    for g in range(grids):
        if grids & (grids - 1) == 0:
            away = me ^ g
        else:
            away = lax.rem(me + grids - g, grids)
        step = jnp.where(grid == g, away, step)
    where_ref[0] = device - grid * parts
    where_ref[1] = jnp.maximum(step - 1, 0) * count + rest


def finish_kernel(
    parts,
    capacity,
    rows,
    first,
    fringes,
    come_ref,
    both_ref,
    flux_ref,
    edge_ref,
    local_ref,
    back_ref,
    where_ref,
    part_ref,
    size_ref,
    lift_ref,
    out_ref,
    turn,
    turned,
    wide,
):
    remote = parts * capacity
    row = lax.broadcasted_iota(jnp.int32, (ROWS, LANES), 0)
    lane = lax.broadcasted_iota(jnp.int32, (ROWS, LANES), 1)
    is_remote = [in_lanes(lane, d * remote, remote) for d in range(3)]
    is_fringe = [in_lanes(lane, 3 * remote + d * fringes, fringes) for d in range(3)]
    any_remote = (lane < 3 * remote) & (row < 25)
    any_fringe = is_fringe[0] | is_fringe[1] | is_fringe[2]
    spread = row[:8] * (3 * fringes) + ((lane[:8] - 3 * remote) & (LANES - 1))
    spread = jnp.where(any_fringe[:8], spread, 0)
    for side in range(2):
        for d in range(3):
            for s in range(capacity):
                start = d * remote + s * parts
                turn[side, start : start + parts, :] = come_ref[
                    pl.ds((2 * d + 1 - side) * capacity + s, parts, stride=rows), :
                ]
        turned[side, :LANES, :] = turn[side].T
    fringe = []
    for v in range(5):
        sent = come_ref[pl.ds(first + v, parts, stride=rows), :]
        total = jnp.zeros((8, LANES), jnp.float32)
        for q in range(parts):
            picked = lane_gather(jnp.broadcast_to(sent[q : q + 1], (8, LANES)), where_ref[1])
            total = jnp.where(where_ref[0] == q, picked, total)
        fringe.append(total)
    for side in range(2):
        own = [both_ref[side, v] for v in range(5)]
        theirs = [
            jnp.where(any_remote, turned[side, 25 * v : 25 * v + ROWS, :], own[v])
            for v in range(5)
        ]
        their = (theirs, *euler_wave(theirs, *by_lane(is_remote[0], is_remote[1])))
        mine = (own, [flux_ref[side, v] for v in range(5)], flux_ref[side, 5])
        common = mix(*mine, *their) if side else mix(*their, *mine)
        own = [edge_ref[side, v] for v in range(5)]
        theirs = []
        for v in range(5):
            pieces = [
                lane_gather(
                    jnp.broadcast_to(fringe[v][side * 4 + r : side * 4 + r + 1], (8, LANES)), spread
                )
                for r in range(4)
            ]
            theirs.append(jnp.where(any_fringe, jnp.concatenate(pieces, axis=0), own[v]))
        their = (theirs, *euler_wave(theirs, *by_lane(~(is_fringe[1] | is_fringe[2]), is_fringe[1])))
        mine = (own, [edge_ref[side, 5 + v] for v in range(5)], edge_ref[side, 10])
        outer = mix(*mine, *their) if side else mix(*their, *mine)
        for d in range(3):
            k = 2 * d + side
            index = jnp.broadcast_to(back_ref[k : k + 1, :], (ROWS, LANES))
            scale = size_ref[d : d + 1, :]
            for v in range(5):
                value = jnp.where(is_fringe[d], outer[v], local_ref[d, v])
                value = jnp.where(is_remote[d], common[v], value)
                wide[k * ROWS : (k + 1) * ROWS, v * LANES : (v + 1) * LANES] = (
                    lane_gather(value, index) * scale
                )
    total = part_ref[...] + jnp.dot(
        lift_ref[...], wide[...], precision=closer, preferred_element_type=jnp.float32
    )
    for v in range(5):
        out_ref[v] = total[:, v * LANES : (v + 1) * LANES]


def call(kernel, name, out_shape, scratch, flops, size, *operands, limit=VMEM, **more):
    return pl.pallas_call(
        kernel,
        name=name,
        out_shape=out_shape,
        scratch_shapes=scratch,
        compiler_params=pltpu.CompilerParams(vmem_limit_bytes=limit),
        cost_estimate=pl.CostEstimate(flops=flops, bytes_accessed=size, transcendentals=0),
        **more,
    )(*operands)


def body(state, inv_size, plus_order, minus_order, donor_cell, donor_weights, recv_slot):
    columns = state.shape[-1]
    parts = lax.axis_size("dom")
    grids = lax.axis_size("grid")
    capacity = max(1, columns // (3 * parts))
    remote = parts * capacity
    fringes = recv_slot.shape[-1] // 150
    total = donor_cell.shape[-1]
    count = total // (grids * parts)
    padded = -(-total // LANES) * LANES
    held = -(-recv_slot.shape[-1] // LANES) * LANES
    first = -(-6 * capacity // 8) * 8
    rows = first + 8
    faces, volume, lift, expand = matrices()
    expand = jnp.asarray(expand, jnp.bfloat16)
    lanes = slot_lanes(parts, capacity, fringes)
    points = fringe_lanes(fringes)
    f32 = functools.partial(jax.ShapeDtypeStruct, dtype=jnp.float32)
    i32 = functools.partial(jax.ShapeDtypeStruct, dtype=jnp.int32)
    memory = functools.partial(pltpu.VMEM, dtype=jnp.float32)

    sent = call(
        functools.partial(donor_kernel, grids, parts, count),
        "donors",
        tuple(f32((parts, 8, LANES)) for _ in range(grids - 1)),
        [
            memory(state.shape),
            pltpu.VMEM(donor_cell.shape, jnp.int32),
            memory((15, 1, total)),
            pltpu.VMEM(expand.shape, jnp.bfloat16),
            pltpu.VMEM((8, padded), jnp.int32),
            memory((16, padded)),
            memory((ROWS, padded)),
            memory((padded // LANES + 1, 8, LANES)),
            pltpu.SemaphoreType.DMA((4,)),
        ],
        5_000_000,
        500_000,
        state,
        donor_cell,
        donor_weights.reshape(15, 1, total),
        expand,
        in_specs=[pl.BlockSpec(memory_space=pl.ANY)] * 4,
        limit=60 * 1024 * 1024,
    )
    arrived = [
        lax.ppermute(sent[step - 1], "grid", [(g, partner(g, step, grids)) for g in range(grids)])
        for step in (*range(2, grids), 1)
    ]
    slots, both, pay = call(
        functools.partial(face_kernel, parts, capacity, rows),
        "faces",
        (
            f32((6, 5, ROWS, LANES)),
            f32((2, 5, ROWS, LANES)),
            f32((parts * rows, LANES)),
        ),
        [memory((2, LANES, LANES))],
        200_000_000,
        1_500_000,
        state,
        plus_order,
        minus_order,
        faces,
        lanes,
    )
    pay = call(
        functools.partial(merge_kernel, parts, rows, first),
        "merge",
        f32((parts * rows, LANES)),
        [],
        50_000,
        200_000,
        pay,
        *arrived,
    )
    come = lax.all_to_all(
        pay.reshape(parts, rows, LANES), "dom", split_axis=0, concat_axis=0, tiled=True
    )
    part, flux, edge, local, back, where = call(
        functools.partial(volume_kernel, grids, parts, count, remote, fringes),
        "volume",
        (
            f32((125, 5 * LANES)),
            f32((2, 6, ROWS, LANES)),
            f32((2, 11, ROWS, LANES)),
            f32((3, 5, ROWS, LANES)),
            i32((8, LANES)),
            i32((2, 8, LANES)),
        ),
        [
            memory((3 * LANES, 5 * LANES)),
            memory((LANES, LANES)),
            pltpu.VMEM((8, held), jnp.int32),
        ],
        400_000_000,
        3_000_000,
        state,
        inv_size,
        plus_order,
        minus_order,
        recv_slot,
        slots,
        both,
        volume,
        lanes,
        points,
    )
    return call(
        functools.partial(finish_kernel, parts, capacity, rows, first, fringes),
        "finish",
        f32((5, 125, columns)),
        [
            memory((2, LANES, LANES)),
            memory((2, LANES + 8, LANES)),
            memory((6 * ROWS, 5 * LANES)),
        ],
        200_000_000,
        3_000_000,
        come.reshape(parts * rows, LANES),
        both,
        flux,
        edge,
        local,
        back,
        where,
        part,
        inv_size,
        lift,
    )


def solution(mesh):
    return jax.shard_map(
        body,
        mesh=mesh,
        in_specs=(
            P(None, None, ("grid", "dom")),
            P(None, ("grid", "dom")),
            P(None, ("grid", "dom")),
            P(None, ("grid", "dom")),
            P(("grid", "dom"), None),
            P(("grid", "dom"), None, None, None),
            P(("grid", "dom"), None),
        ),
        out_specs=P(None, None, ("grid", "dom")),
        check_vma=False,
    )
```

```python
import functools
import math

import jax
import jax.numpy as jnp
import numpy as np
from jax import lax
from jax.experimental import pallas as pl
from jax.experimental.pallas import tpu as pltpu
from jax.sharding import PartitionSpec as P

precise = lax.Precision.HIGHEST
closer = lax.Precision.HIGH
LANES = 128
SHIFT = (1.0, 0.0, 0.0, 0.0, 2.5)
ROWS = 32
VMEM = 48 * 1024 * 1024


def gauss_nodes():
    outer = math.sqrt(5.0 + 2.0 * math.sqrt(10.0 / 7.0)) / 3.0
    inner = math.sqrt(5.0 - 2.0 * math.sqrt(10.0 / 7.0)) / 3.0
    return [-outer, -inner, 0.0, inner, outer]


def basis_value(nodes, column, target):
    value = 1.0
    for other in range(5):
        if other != column:
            value = value * (target - nodes[other]) / (nodes[column] - nodes[other])
    return value


def basis_slope(nodes, column, target):
    total = 0.0
    for skipped in range(5):
        if skipped != column:
            value = 1.0 / (nodes[column] - nodes[skipped])
            for other in range(5):
                if other != column and other != skipped:
                    value = value * (target - nodes[other]) / (nodes[column] - nodes[other])
            total = total + value
    return total


def legendre_slopes(target):
    values = [1.0, target]
    slopes = [0.0, 1.0]
    for order in range(1, 5):
        values.append(
            ((2 * order + 1) * target * values[order] - order * values[order - 1]) / (order + 1)
        )
        slopes.append(slopes[order - 1] + (2 * order + 1) * values[order])
    return (slopes[4], slopes[5])


def tables():
    nodes = gauss_nodes()
    deriv = [[basis_slope(nodes, column, nodes[row]) for column in range(5)] for row in range(5)]
    lower = [basis_value(nodes, column, -1.0) for column in range(5)]
    upper = [basis_value(nodes, column, 1.0) for column in range(5)]
    lift_low = []
    lift_high = []
    for row in range(5):
        slope_four, slope_five = legendre_slopes(nodes[row])
        lift_low.append(-0.5 * (slope_five - slope_four))
        lift_high.append(0.5 * (slope_five + slope_four))
    return tuple(np.asarray(m, np.float64) for m in (deriv, lower, upper, lift_low, lift_high))


def split_point(point, direction):
    index = [point // 25, point // 5 % 5, point % 5]
    along = index.pop(direction)
    return along, 5 * index[0] + index[1]


def matrices():
    deriv, lower, upper, lift_low, lift_high = tables()
    faces = np.zeros((6 * ROWS, 125))
    volume = np.zeros((125, 3 * LANES))
    lift = np.zeros((125, 6 * ROWS))
    own = deriv - np.outer(lift_low, lower) - np.outer(lift_high, upper)
    for d in range(3):
        for p in range(125):
            i, t = split_point(p, d)
            faces[(2 * d) * ROWS + t, p] = lower[i]
            faces[(2 * d + 1) * ROWS + t, p] = upper[i]
            lift[p, (2 * d) * ROWS + t] = -lift_low[i]
            lift[p, (2 * d + 1) * ROWS + t] = -lift_high[i]
            for other in range(125):
                m, line = split_point(other, d)
                if line == t:
                    volume[p, d * LANES + other] = -own[i, m]
    for k in range(6):
        faces[k * ROWS + 25 : (k + 1) * ROWS] = faces[k * ROWS + 24]
    return tuple(m.astype(np.float32) for m in (faces, volume, lift))


def slot_lanes(parts, capacity, fringes):
    remote = parts * capacity
    lanes = np.zeros((8, LANES), np.int32)
    for d in range(3):
        held = {}
        for lane in range(remote):
            held[d * remote + lane] = lane % parts * capacity + lane // parts
        for i in range(fringes):
            held[(3 * remote + d * fringes + i) % LANES] = remote + i
        free = iter(range(remote + fringes, LANES))
        for lane in range(LANES):
            lanes[d, lane] = held[lane] if lane in held else next(free)
    return lanes


def fringe_lanes(fringes):
    found = np.zeros((8, LANES), np.int32)
    for side in range(2):
        for t in range(ROWS):
            for d in range(3):
                for i in range(fringes):
                    point = ((2 * d + side) * 25 + min(t, 24)) * fringes + i
                    found[side * 4 + t // 8, (t % 8 * 3 + d) * fringes + i] = point
    return found


def partner(index, step):
    return index ^ step


def lane_gather(values, index):
    return jnp.take_along_axis(values, index, axis=1, mode="promise_in_bounds")


def in_lanes(lane, start, width):
    start = start % LANES
    if start + width <= LANES:
        return (lane >= start) & (lane < start + width)
    return (lane >= start) | (lane < start + width - LANES)


def euler(state, choose, along):
    density, momenta, energy = state[0], state[1:4], state[4]
    inverse = 1.0 / density
    normal = choose(momenta)
    speed = normal * inverse
    squares = momenta[0] * momenta[0] + momenta[1] * momenta[1] + momenta[2] * momenta[2]
    pressure = 0.4 * (energy - 0.5 * squares * inverse)
    flux = [normal] + [m * speed for m in momenta] + [(energy + pressure) * speed]
    for d in range(3):
        flux[1 + d] = along(d, flux[1 + d], pressure - 1.0)
    return flux, speed, pressure, inverse


def euler_wave(state, choose, along):
    flux, speed, pressure, inverse = euler(state, choose, along)
    return flux, jnp.abs(speed) + jnp.sqrt(1.4 * pressure * inverse)


def fixed(direction):
    def choose(parts):
        return parts[direction]

    def along(d, flux, pressure):
        return flux + pressure if d == direction else flux

    return choose, along


def by_lane(first, second):
    def choose(parts):
        return jnp.where(first, parts[0], jnp.where(second, parts[1], parts[2]))

    third = ~(first | second)

    def along(d, flux, pressure):
        return flux + jnp.where((first, second, third)[d], pressure, 0.0)

    return choose, along


def mix(left, left_flux, left_wave, right, right_flux, right_wave):
    wave = 0.5 * jnp.maximum(left_wave, right_wave)
    return [
        0.5 * (left_flux[v] + right_flux[v]) - wave * (right[v] - left[v]) for v in range(5)
    ]


def table_kernel(out_ref):
    row = lax.broadcasted_iota(jnp.int32, out_ref.shape, 0)
    column = lax.broadcasted_iota(jnp.int32, out_ref.shape, 1) & 15
    point = row & (ROWS - 1)
    point = jnp.where(point >= 25, point - 25, point)
    tens = ((point.astype(jnp.float32) + 0.5) * 0.2).astype(jnp.int32)
    wanted = jnp.where(row < ROWS, 5 + tens, 10 + point - 5 * tens)
    out_ref[...] = jnp.where(column == wanted, 1.0, 0.0).astype(jnp.bfloat16)


def donor_kernel(grids, parts, count, *refs):
    states, cell_refs, weight_refs, expand_ref = refs[0:2], refs[2:4], refs[4:6], refs[6]
    outs = refs[7 : 7 + grids // 2]
    cells, weights, planes, values = refs[7 + grids // 2 :]
    span = parts * count
    total = grids * span
    blocks = values.shape[1] - 1
    width = blocks * LANES
    cells[...] = jnp.zeros_like(cells)
    weights[...] = jnp.zeros_like(weights)
    halves = []
    for source in range(2):
        for block in range(-(-total // LANES)):
            lanes = slice(block * LANES, min((block + 1) * LANES, total))
            held = lanes.stop - lanes.start
            cells[source, block, 0:1, :held] = cell_refs[source][:, lanes]
            for k in range(15):
                weights[source, block, k : k + 1, :held] = weight_refs[source][k, :, lanes]
        for v in range(5):
            shifted = states[source][v] - SHIFT[v]
            high = shifted.astype(jnp.bfloat16)
            low = (shifted - high.astype(jnp.float32)).astype(jnp.bfloat16)
            halves.append(jnp.concatenate([high, low], axis=1))
    element = lax.broadcasted_iota(jnp.int32, (LANES, width), 0)
    row = lax.broadcasted_iota(jnp.int32, (8, width), 0)
    lane = lax.broadcasted_iota(jnp.int32, (8, LANES), 1)
    me = lax.axis_index("grid")
    number = 0
    for step in range(0, grids, 2):
        start = partner(me, step) * span
        first = start // LANES
        found = [jnp.zeros((8, LANES), jnp.float32)] * parts
        for source in range(0 if step else 1, 2):
            held = jnp.concatenate([cells[source, first + i] for i in range(blocks)], axis=1)
            chosen = jnp.where(element == held[0:1], 1.0, 0.0).astype(jnp.bfloat16)
            chosen = jnp.concatenate([chosen, chosen], axis=0)
            held = jnp.concatenate([weights[source, first + i] for i in range(blocks)], axis=1)
            high = held.astype(jnp.bfloat16)
            rest = held - high.astype(jnp.float32)
            middle = rest.astype(jnp.bfloat16)
            low = (rest - middle.astype(jnp.float32)).astype(jnp.bfloat16)
            pieces = jnp.concatenate([high, middle, low], axis=0)
            plane = jnp.dot(expand_ref[...], pieces, preferred_element_type=jnp.float32)
            planes[number] = plane[:ROWS] * plane[ROWS:]
            tiles = []
            for top in range(0, LANES, 8):
                a = top // 25
                outer = jnp.broadcast_to(held[a : a + 1], (8, width))
                if top < 25 * (a + 1) < top + 8 and a < 4:
                    later = jnp.broadcast_to(held[a + 1 : a + 2], (8, width))
                    outer = jnp.where(row < 25 * (a + 1) - top, outer, later)
                tiles.append(outer * planes[number, top % 25 : top % 25 + 8, :])
            weight = jnp.concatenate(tiles, axis=0)[:125]
            for v in range(5):
                picked = jnp.dot(
                    halves[5 * source + v], chosen, preferred_element_type=jnp.float32
                )
                value = jnp.sum(picked * weight, axis=0, keepdims=True) + SHIFT[v]
                for block in range(blocks):
                    values[number, block, v : v + 1, :] = value[
                        :, block * LANES : (block + 1) * LANES
                    ]
            place = (step + source - 1) * count
            wanted = in_lanes(lane, place, count)
            for q in range(parts):
                offset = start - first * LANES + q * count
                block = offset // LANES
                index = lane + (offset - block * LANES - place)
                inside = index & (LANES - 1)
                near = lane_gather(values[number, block], inside)
                far = lane_gather(values[number, block + 1], inside)
                found[q] = jnp.where(wanted, jnp.where(index < LANES, near, far), found[q])
            number += 1
        for q in range(parts):
            outs[step // 2][q] = found[q]


def face_kernel(
    parts,
    capacity,
    rows,
    state_ref,
    plus_ref,
    minus_ref,
    faces_ref,
    lanes_ref,
    slots_ref,
    both_ref,
    pay_ref,
    turn,
):
    remote = parts * capacity
    wide = jnp.concatenate([state_ref[v] for v in range(5)], axis=1)
    face = jnp.dot(
        faces_ref[...], wide, precision=precise, preferred_element_type=jnp.float32
    )
    for side in range(2):
        order = (minus_ref, plus_ref)[side]
        for d in range(3):
            k = 2 * d + side
            index = lane_gather(
                jnp.broadcast_to(order[d : d + 1, :], (ROWS, LANES)),
                jnp.broadcast_to(lanes_ref[d : d + 1, :], (ROWS, LANES)),
            )
            for v in range(5):
                block = face[k * ROWS : (k + 1) * ROWS, v * LANES : (v + 1) * LANES]
                slots_ref[k, v] = lane_gather(block, index)
    lane = lax.broadcasted_iota(jnp.int32, (ROWS, LANES), 1)
    turn[:, 120:128, :] = jnp.zeros((2, 8, LANES), jnp.float32)
    for side in range(2):
        for v in range(5):
            both = jnp.where(
                lane < remote,
                slots_ref[side, v],
                jnp.where(lane < 2 * remote, slots_ref[2 + side, v], slots_ref[4 + side, v]),
            )
            both_ref[side, v] = both
            turn[side, 25 * v : 25 * v + 25, :] = both[:25]
        turned = turn[side].T
        for d in range(3):
            for s in range(capacity):
                start = d * remote + s * parts
                pay_ref[pl.ds((2 * d + side) * capacity + s, parts, stride=rows), :] = turned[
                    start : start + parts
                ]


def merge_kernel(parts, rows, first, pay_ref, *refs):
    out_ref = refs[-1]
    for q in range(parts):
        total = refs[0][q]
        for extra in refs[1:-1]:
            total = total + extra[q]
        out_ref[q * rows : q * rows + first, :] = pay_ref[q * rows : q * rows + first, :]
        out_ref[q * rows + first : q * rows + first + 8, :] = total


def volume_kernel(
    grids,
    parts,
    count,
    remote,
    fringes,
    state_ref,
    size_ref,
    plus_ref,
    minus_ref,
    recv_ref,
    slots_ref,
    both_ref,
    volume_ref,
    lanes_ref,
    points_ref,
    part_ref,
    flux_ref,
    edge_ref,
    local_ref,
    back_ref,
    where_ref,
    wide,
    index,
    received,
):
    state = [state_ref[v] for v in range(5)]
    for d in range(3):
        flux = euler(state, *fixed(d))[0]
        scale = size_ref[d : d + 1, :]
        wide[d * LANES + 120 : (d + 1) * LANES, :] = jnp.zeros((8, 5 * LANES), jnp.float32)
        for v in range(5):
            wide[d * LANES : d * LANES + 125, v * LANES : (v + 1) * LANES] = flux[v] * scale
    part_ref[...] = jnp.dot(
        volume_ref[...], wide[...], precision=closer, preferred_element_type=jnp.float32
    )
    for d in range(3):
        low = [slots_ref[2 * d, v] for v in range(5)]
        high = [slots_ref[2 * d + 1, v] for v in range(5)]
        low_flux, low_wave = euler_wave(low, *fixed(d))
        high_flux, high_wave = euler_wave(high, *fixed(d))
        local = mix(high, high_flux, high_wave, low, low_flux, low_wave)
        for v in range(5):
            local_ref[d, v] = local[v]
    lane = lax.broadcasted_iota(jnp.int32, (ROWS, LANES), 1)
    for side in range(2):
        own = [both_ref[side, v] for v in range(5)]
        flux, wave = euler_wave(own, *by_lane(lane < remote, in_lanes(lane, remote, remote)))
        for v in range(5):
            flux_ref[side, v] = flux[v]
        flux_ref[side, 5] = wave
        second = in_lanes(lane, 3 * remote + fringes, fringes)
        third = in_lanes(lane, 3 * remote + 2 * fringes, fringes)
        edge = [
            jnp.where(
                second,
                slots_ref[2 + side, v],
                jnp.where(third, slots_ref[4 + side, v], slots_ref[side, v]),
            )
            for v in range(5)
        ]
        flux, wave = euler_wave(edge, *by_lane(~(second | third), second))
        for v in range(5):
            edge_ref[side, v] = edge[v]
            edge_ref[side, 5 + v] = flux[v]
        edge_ref[side, 10] = wave
    rank = lax.broadcasted_iota(jnp.int32, (LANES, LANES), 0)
    column = lax.broadcasted_iota(jnp.int32, (LANES, LANES), 1)
    index[...] = jnp.zeros_like(index)
    for k in range(6):
        d = k // 2
        order = lane_gather(
            jnp.broadcast_to((minus_ref, plus_ref)[k % 2][d : d + 1, :], (8, LANES)),
            jnp.broadcast_to(lanes_ref[d : d + 1, :], (8, LANES)),
        )
        index[k : k + 1, :] = order[0:1].astype(jnp.float32)
    turned = index[...].T.astype(jnp.int32)
    back_ref[...] = jnp.zeros_like(back_ref)
    for k in range(6):
        found = jnp.where(turned[:, k : k + 1] == column, rank, 0)
        back_ref[k : k + 1, :] = jnp.sum(found, axis=0, keepdims=True)
    me = lax.axis_index("grid")
    received[...] = jnp.zeros_like(received)
    received[0:1, : recv_ref.shape[1]] = recv_ref[...]
    points = points_ref[...]
    slot = jnp.zeros((8, LANES), jnp.int32)
    for block in range(received.shape[1] // LANES):
        held = jnp.broadcast_to(received[0:1, block * LANES : (block + 1) * LANES], (8, LANES))
        inside = (points >= block * LANES) & (points < (block + 1) * LANES)
        picked = lane_gather(held, jnp.where(inside, points - block * LANES, 0))
        slot = jnp.where(inside, picked, slot)
    device = ((slot.astype(jnp.float32) + 0.5) * (1.0 / count)).astype(jnp.int32)
    rest = slot - device * count
    grid = ((device.astype(jnp.float32) + 0.5) * (1.0 / parts)).astype(jnp.int32)
    step = jnp.zeros_like(grid)
    for g in range(grids):
        away = partner(me, g)
        step = jnp.where(grid == g, away, step)
    where_ref[0] = device - grid * parts
    where_ref[1] = jnp.maximum(step - 1, 0) * count + rest


def finish_kernel(
    parts,
    capacity,
    rows,
    first,
    fringes,
    come_ref,
    both_ref,
    flux_ref,
    edge_ref,
    local_ref,
    back_ref,
    where_ref,
    part_ref,
    size_ref,
    lift_ref,
    out_ref,
    turn,
    turned,
    wide,
):
    remote = parts * capacity
    row = lax.broadcasted_iota(jnp.int32, (ROWS, LANES), 0)
    lane = lax.broadcasted_iota(jnp.int32, (ROWS, LANES), 1)
    is_remote = [in_lanes(lane, d * remote, remote) for d in range(3)]
    is_fringe = [in_lanes(lane, 3 * remote + d * fringes, fringes) for d in range(3)]
    any_remote = (lane < 3 * remote) & (row < 25)
    any_fringe = is_fringe[0] | is_fringe[1] | is_fringe[2]
    spread = row[:8] * (3 * fringes) + ((lane[:8] - 3 * remote) & (LANES - 1))
    spread = jnp.where(any_fringe[:8], spread, 0)
    for side in range(2):
        for d in range(3):
            for s in range(capacity):
                start = d * remote + s * parts
                turn[side, start : start + parts, :] = come_ref[
                    pl.ds((2 * d + 1 - side) * capacity + s, parts, stride=rows), :
                ]
        turned[side, :LANES, :] = turn[side].T
    fringe = []
    for v in range(5):
        sent = come_ref[pl.ds(first + v, parts, stride=rows), :]
        total = jnp.zeros((8, LANES), jnp.float32)
        for q in range(parts):
            picked = lane_gather(jnp.broadcast_to(sent[q : q + 1], (8, LANES)), where_ref[1])
            total = jnp.where(where_ref[0] == q, picked, total)
        fringe.append(total)
    for side in range(2):
        own = [both_ref[side, v] for v in range(5)]
        theirs = [
            jnp.where(any_remote, turned[side, 25 * v : 25 * v + ROWS, :], own[v])
            for v in range(5)
        ]
        their = (theirs, *euler_wave(theirs, *by_lane(is_remote[0], is_remote[1])))
        mine = (own, [flux_ref[side, v] for v in range(5)], flux_ref[side, 5])
        common = mix(*mine, *their) if side else mix(*their, *mine)
        own = [edge_ref[side, v] for v in range(5)]
        theirs = []
        for v in range(5):
            pieces = [
                lane_gather(
                    jnp.broadcast_to(fringe[v][side * 4 + r : side * 4 + r + 1], (8, LANES)), spread
                )
                for r in range(4)
            ]
            theirs.append(jnp.where(any_fringe, jnp.concatenate(pieces, axis=0), own[v]))
        their = (theirs, *euler_wave(theirs, *by_lane(~(is_fringe[1] | is_fringe[2]), is_fringe[1])))
        mine = (own, [edge_ref[side, 5 + v] for v in range(5)], edge_ref[side, 10])
        outer = mix(*mine, *their) if side else mix(*their, *mine)
        for d in range(3):
            k = 2 * d + side
            index = jnp.broadcast_to(back_ref[k : k + 1, :], (ROWS, LANES))
            scale = size_ref[d : d + 1, :]
            for v in range(5):
                value = jnp.where(is_fringe[d], outer[v], local_ref[d, v])
                value = jnp.where(is_remote[d], common[v], value)
                wide[k * ROWS : (k + 1) * ROWS, v * LANES : (v + 1) * LANES] = (
                    lane_gather(value, index) * scale
                )
    total = part_ref[...] + jnp.dot(
        lift_ref[...], wide[...], precision=closer, preferred_element_type=jnp.float32
    )
    for v in range(5):
        out_ref[v] = total[:, v * LANES : (v + 1) * LANES]


def call(kernel, name, out_shape, scratch, flops, size, *operands, limit=VMEM, **more):
    return pl.pallas_call(
        kernel,
        name=name,
        out_shape=out_shape,
        scratch_shapes=scratch,
        compiler_params=pltpu.CompilerParams(vmem_limit_bytes=limit),
        cost_estimate=pl.CostEstimate(flops=flops, bytes_accessed=size, transcendentals=0),
        **more,
    )(*operands)


def body(state, inv_size, plus_order, minus_order, donor_cell, donor_weights, recv_slot):
    columns = state.shape[-1]
    parts = lax.axis_size("dom")
    grids = lax.axis_size("grid")
    capacity = max(1, columns // (3 * parts))
    remote = parts * capacity
    fringes = recv_slot.shape[-1] // 150
    total = donor_cell.shape[-1]
    count = total // (grids * parts)
    held = -(-recv_slot.shape[-1] // LANES) * LANES
    first = -(-6 * capacity // 8) * 8
    rows = first + 8
    faces, volume, lift = matrices()
    lanes = slot_lanes(parts, capacity, fringes)
    points = fringe_lanes(fringes)
    f32 = functools.partial(jax.ShapeDtypeStruct, dtype=jnp.float32)
    i32 = functools.partial(jax.ShapeDtypeStruct, dtype=jnp.int32)
    memory = functools.partial(pltpu.VMEM, dtype=jnp.float32)

    span = parts * count
    blocks = (2 * (LANES - 1) + span) // LANES
    sets = grids - 1
    held_blocks = -(-total // LANES) + blocks

    def exchange(values, step):
        return lax.ppermute(values, "grid", [(g, partner(g, step)) for g in range(grids)])

    expand = call(
        table_kernel,
        "tables",
        jax.ShapeDtypeStruct((2 * ROWS, 48), jnp.bfloat16),
        [],
        400_000_000,
        3_000_000,
    )
    weights = donor_weights.reshape(15, 1, total)
    sent = call(
        functools.partial(donor_kernel, grids, parts, count),
        "donors",
        tuple(f32((parts, 8, LANES)) for _ in range(grids // 2)),
        [
            pltpu.VMEM((2, held_blocks, 8, LANES), jnp.int32),
            memory((2, held_blocks, 16, LANES)),
            memory((sets, ROWS, blocks * LANES)),
            memory((sets, blocks + 1, 8, LANES)),
        ],
        5_000_000,
        500_000,
        state,
        exchange(state, 1),
        donor_cell,
        exchange(donor_cell, 1),
        weights,
        exchange(weights, 1),
        expand,
    )
    arrived = [sent[0]] + [exchange(sent[k], 2 * k) for k in range(1, grids // 2)]
    slots, both, pay = call(
        functools.partial(face_kernel, parts, capacity, rows),
        "faces",
        (
            f32((6, 5, ROWS, LANES)),
            f32((2, 5, ROWS, LANES)),
            f32((parts * rows, LANES)),
        ),
        [memory((2, LANES, LANES))],
        200_000_000,
        1_500_000,
        state,
        plus_order,
        minus_order,
        faces,
        lanes,
    )
    pay = call(
        functools.partial(merge_kernel, parts, rows, first),
        "merge",
        f32((parts * rows, LANES)),
        [],
        50_000,
        200_000,
        pay,
        *arrived,
    )
    come = lax.all_to_all(
        pay.reshape(parts, rows, LANES), "dom", split_axis=0, concat_axis=0, tiled=True
    )
    part, flux, edge, local, back, where = call(
        functools.partial(volume_kernel, grids, parts, count, remote, fringes),
        "volume",
        (
            f32((125, 5 * LANES)),
            f32((2, 6, ROWS, LANES)),
            f32((2, 11, ROWS, LANES)),
            f32((3, 5, ROWS, LANES)),
            i32((8, LANES)),
            i32((2, 8, LANES)),
        ),
        [
            memory((3 * LANES, 5 * LANES)),
            memory((LANES, LANES)),
            pltpu.VMEM((8, held), jnp.int32),
        ],
        400_000_000,
        3_000_000,
        state,
        inv_size,
        plus_order,
        minus_order,
        recv_slot,
        slots,
        both,
        volume,
        lanes,
        points,
    )
    return call(
        functools.partial(finish_kernel, parts, capacity, rows, first, fringes),
        "finish",
        f32((5, 125, columns)),
        [
            memory((2, LANES, LANES)),
            memory((2, LANES + 8, LANES)),
            memory((6 * ROWS, 5 * LANES)),
        ],
        200_000_000,
        3_000_000,
        come.reshape(parts * rows, LANES),
        both,
        flux,
        edge,
        local,
        back,
        where,
        part,
        inv_size,
        lift,
    )


def solution(mesh):
    return jax.shard_map(
        body,
        mesh=mesh,
        in_specs=(
            P(None, None, ("grid", "dom")),
            P(None, ("grid", "dom")),
            P(None, ("grid", "dom")),
            P(None, ("grid", "dom")),
            P(("grid", "dom"), None),
            P(("grid", "dom"), None, None, None),
            P(("grid", "dom"), None),
        ),
        out_specs=P(None, None, ("grid", "dom")),
        check_vma=False,
    )
```

```python
import functools
import math

import jax
import jax.numpy as jnp
import numpy as np
from jax import lax
from jax.experimental import pallas as pl
from jax.experimental.pallas import tpu as pltpu
from jax.sharding import PartitionSpec as P

precise = lax.Precision.HIGHEST
closer = lax.Precision.HIGH
LANES = 128
SHIFT = (1.0, 0.0, 0.0, 0.0, 2.5)
ROWS = 32
VMEM = 48 * 1024 * 1024


def gauss_nodes():
    outer = math.sqrt(5.0 + 2.0 * math.sqrt(10.0 / 7.0)) / 3.0
    inner = math.sqrt(5.0 - 2.0 * math.sqrt(10.0 / 7.0)) / 3.0
    return [-outer, -inner, 0.0, inner, outer]


def basis_value(nodes, column, target):
    value = 1.0
    for other in range(5):
        if other != column:
            value = value * (target - nodes[other]) / (nodes[column] - nodes[other])
    return value


def basis_slope(nodes, column, target):
    total = 0.0
    for skipped in range(5):
        if skipped != column:
            value = 1.0 / (nodes[column] - nodes[skipped])
            for other in range(5):
                if other != column and other != skipped:
                    value = value * (target - nodes[other]) / (nodes[column] - nodes[other])
            total = total + value
    return total


def legendre_slopes(target):
    values = [1.0, target]
    slopes = [0.0, 1.0]
    for order in range(1, 5):
        values.append(
            ((2 * order + 1) * target * values[order] - order * values[order - 1]) / (order + 1)
        )
        slopes.append(slopes[order - 1] + (2 * order + 1) * values[order])
    return (slopes[4], slopes[5])


def tables():
    nodes = gauss_nodes()
    deriv = [[basis_slope(nodes, column, nodes[row]) for column in range(5)] for row in range(5)]
    lower = [basis_value(nodes, column, -1.0) for column in range(5)]
    upper = [basis_value(nodes, column, 1.0) for column in range(5)]
    lift_low = []
    lift_high = []
    for row in range(5):
        slope_four, slope_five = legendre_slopes(nodes[row])
        lift_low.append(-0.5 * (slope_five - slope_four))
        lift_high.append(0.5 * (slope_five + slope_four))
    return tuple(np.asarray(m, np.float64) for m in (deriv, lower, upper, lift_low, lift_high))


def split_point(point, direction):
    index = [point // 25, point // 5 % 5, point % 5]
    along = index.pop(direction)
    return along, 5 * index[0] + index[1]


def matrices():
    deriv, lower, upper, lift_low, lift_high = tables()
    faces = np.zeros((6 * ROWS, 125))
    volume = np.zeros((125, 3 * LANES))
    lift = np.zeros((125, 6 * ROWS))
    own = deriv - np.outer(lift_low, lower) - np.outer(lift_high, upper)
    for d in range(3):
        for p in range(125):
            i, t = split_point(p, d)
            faces[(2 * d) * ROWS + t, p] = lower[i]
            faces[(2 * d + 1) * ROWS + t, p] = upper[i]
            lift[p, (2 * d) * ROWS + t] = -lift_low[i]
            lift[p, (2 * d + 1) * ROWS + t] = -lift_high[i]
            for other in range(125):
                m, line = split_point(other, d)
                if line == t:
                    volume[p, d * LANES + other] = -own[i, m]
    for k in range(6):
        faces[k * ROWS + 25 : (k + 1) * ROWS] = faces[k * ROWS + 24]
    return tuple(m.astype(np.float32) for m in (faces, volume, lift))


def fringe_lanes(fringes):
    found = np.zeros((8, LANES), np.int32)
    for side in range(2):
        for t in range(ROWS):
            for d in range(3):
                for i in range(fringes):
                    point = ((2 * d + side) * 25 + min(t, 24)) * fringes + i
                    found[side * 4 + t // 8, (t % 8 * 3 + d) * fringes + i] = point
    return found


def partner(index, step):
    return index ^ step


def lane_gather(values, index):
    return jnp.take_along_axis(values, index, axis=1, mode="promise_in_bounds")


def in_lanes(lane, start, width):
    start = start % LANES
    if start + width <= LANES:
        return (lane >= start) & (lane < start + width)
    return (lane >= start) | (lane < start + width - LANES)


def euler(state, choose, along):
    density, momenta, energy = state[0], state[1:4], state[4]
    inverse = 1.0 / density
    normal = choose(momenta)
    speed = normal * inverse
    squares = momenta[0] * momenta[0] + momenta[1] * momenta[1] + momenta[2] * momenta[2]
    pressure = 0.4 * (energy - 0.5 * squares * inverse)
    flux = [normal] + [m * speed for m in momenta] + [(energy + pressure) * speed]
    for d in range(3):
        flux[1 + d] = along(d, flux[1 + d], pressure - 1.0)
    return flux, speed, pressure, inverse


def euler_wave(state, choose, along):
    flux, speed, pressure, inverse = euler(state, choose, along)
    return flux, jnp.abs(speed) + jnp.sqrt(1.4 * pressure * inverse)


def fixed(direction):
    def choose(parts):
        return parts[direction]

    def along(d, flux, pressure):
        return flux + pressure if d == direction else flux

    return choose, along


def by_lane(first, second):
    def choose(parts):
        return jnp.where(first, parts[0], jnp.where(second, parts[1], parts[2]))

    third = ~(first | second)

    def along(d, flux, pressure):
        return flux + jnp.where((first, second, third)[d], pressure, 0.0)

    return choose, along


def mix(left, left_flux, left_wave, right, right_flux, right_wave):
    wave = 0.5 * jnp.maximum(left_wave, right_wave)
    return [
        0.5 * (left_flux[v] + right_flux[v]) - wave * (right[v] - left[v]) for v in range(5)
    ]


def floor_divide(values, divisor):
    return ((values.astype(jnp.float32) + 0.5) * (1.0 / divisor)).astype(jnp.int32)


def table_kernel(parts, capacity, fringes, expand_ref, lanes_ref):
    row = lax.broadcasted_iota(jnp.int32, expand_ref.shape, 0)
    column = lax.broadcasted_iota(jnp.int32, expand_ref.shape, 1) & 15
    point = row & (ROWS - 1)
    point = jnp.where(point >= 25, point - 25, point)
    tens = floor_divide(point, 5)
    wanted = jnp.where(row < ROWS, 5 + tens, 10 + point - 5 * tens)
    expand_ref[...] = jnp.where(column == wanted, 1.0, 0.0).astype(jnp.bfloat16)
    me = lax.axis_index("dom")
    remote = parts * capacity
    row = lax.broadcasted_iota(jnp.int32, (8, LANES), 0)
    lane = lax.broadcasted_iota(jnp.int32, (8, LANES), 1)
    total = jnp.zeros((8, LANES), jnp.int32)
    for d in range(3):
        near = jnp.clip(lane - d * remote, 0, remote - 1)
        away = floor_divide(near, capacity)
        slot = (away ^ me) * capacity + near - away * capacity
        edge = (lane - 3 * remote - d * fringes) & (LANES - 1)
        start = (3 * remote + d * fringes) % LANES
        taken = jnp.clip(lane - d * remote, 0, remote) + jnp.clip(
            lane - start, 0, min(fringes, LANES - start)
        )
        if start + fringes > LANES:
            taken = taken + jnp.clip(lane, 0, start + fringes - LANES)
        other = remote + fringes + lane - taken
        slot = jnp.where(
            in_lanes(lane, d * remote, remote),
            slot,
            jnp.where(edge < fringes, remote + edge, other),
        )
        total = jnp.where(row == d, slot, total)
    lanes_ref[...] = total


def donor_kernel(grids, parts, count, height, *refs):
    states, cell_refs, weight_refs, expand_ref, pay_ref = *(refs[k : k + 2] for k in (0, 2, 4)), *refs[6:8]
    keep_ref, side_ref = refs[8:10]
    outs = refs[10 : 8 + grids]
    cells, weights, planes, values = refs[8 + grids :]
    outer = parts // 2
    side_ref[: outer * height, :] = pay_ref[outer * height :, :]
    span = parts * count
    total = grids * span
    blocks = values.shape[1] - 1
    width = blocks * LANES
    cells[...] = jnp.zeros_like(cells)
    weights[...] = jnp.zeros_like(weights)
    halves = []
    for source in range(2):
        for block in range(-(-total // LANES)):
            lanes = slice(block * LANES, min((block + 1) * LANES, total))
            held = lanes.stop - lanes.start
            cells[source, block, 0:1, :held] = cell_refs[source][:, lanes]
            for k in range(15):
                weights[source, block, k : k + 1, :held] = weight_refs[source][k, :, lanes]
        for v in range(5):
            shifted = states[source][v] - SHIFT[v]
            high = shifted.astype(jnp.bfloat16)
            low = (shifted - high.astype(jnp.float32)).astype(jnp.bfloat16)
            halves.append(jnp.concatenate([high, low], axis=1))
    element = lax.broadcasted_iota(jnp.int32, (LANES, width), 0)
    row = lax.broadcasted_iota(jnp.int32, (8, width), 0)
    lane = lax.broadcasted_iota(jnp.int32, (8, LANES), 1)
    me = lax.axis_index("grid")
    here = lax.axis_index("dom")
    number = 0
    for step in range(0, grids, 2):
        start = partner(me, step) * span
        first = start // LANES
        found = [jnp.zeros((8, LANES), jnp.float32)] * parts
        for source in range(0 if step else 1, 2):
            held = jnp.concatenate([cells[source, first + i] for i in range(blocks)], axis=1)
            chosen = jnp.where(element == held[0:1], 1.0, 0.0).astype(jnp.bfloat16)
            chosen = jnp.concatenate([chosen, chosen], axis=0)
            held = jnp.concatenate([weights[source, first + i] for i in range(blocks)], axis=1)
            high = held.astype(jnp.bfloat16)
            rest = held - high.astype(jnp.float32)
            middle = rest.astype(jnp.bfloat16)
            low = (rest - middle.astype(jnp.float32)).astype(jnp.bfloat16)
            pieces = jnp.concatenate([high, middle, low], axis=0)
            plane = jnp.dot(expand_ref[...], pieces, preferred_element_type=jnp.float32)
            planes[number] = plane[:ROWS] * plane[ROWS:]
            tiles = []
            for top in range(0, LANES, 8):
                a = top // 25
                factor = jnp.broadcast_to(held[a : a + 1], (8, width))
                if top < 25 * (a + 1) < top + 8 and a < 4:
                    later = jnp.broadcast_to(held[a + 1 : a + 2], (8, width))
                    factor = jnp.where(row < 25 * (a + 1) - top, factor, later)
                tiles.append(factor * planes[number, top % 25 : top % 25 + 8, :])
            weight = jnp.concatenate(tiles, axis=0)[:125]
            for v in range(5):
                picked = jnp.dot(
                    halves[5 * source + v], chosen, preferred_element_type=jnp.float32
                )
                value = jnp.sum(picked * weight, axis=0, keepdims=True) + SHIFT[v]
                for block in range(blocks):
                    values[number, block, v : v + 1, :] = value[
                        :, block * LANES : (block + 1) * LANES
                    ]
            place = (step + source - 1) * count
            wanted = in_lanes(lane, place, count)
            for q in range(parts):
                offset = start - first * LANES + partner(here, q) * count
                block = offset // LANES
                index = lane + (offset - block * LANES - place)
                inside = index & (LANES - 1)
                near = lane_gather(values[number, block], inside)
                far = lane_gather(values[number, block + 1], inside)
                found[q] = jnp.where(wanted, jnp.where(index < LANES, near, far), found[q])
            number += 1
        for z in range(outer):
            if step:
                outs[step - 2][z] = found[2 * z]
                outs[step - 1][z] = found[2 * z + 1]
            else:
                keep_ref[z] = found[2 * z]
                side_ref[outer * height + 8 * z : outer * height + 8 * z + 8, :] = found[2 * z + 1]


def face_kernel(
    parts,
    capacity,
    height,
    state_ref,
    plus_ref,
    minus_ref,
    faces_ref,
    lanes_ref,
    slots_ref,
    both_ref,
    pay_ref,
    turn,
):
    remote = parts * capacity
    wide = jnp.concatenate([state_ref[v] for v in range(5)], axis=1)
    face = jnp.dot(
        faces_ref[...], wide, precision=precise, preferred_element_type=jnp.float32
    )
    for side in range(2):
        order = (minus_ref, plus_ref)[side]
        for d in range(3):
            k = 2 * d + side
            index = lane_gather(
                jnp.broadcast_to(order[d : d + 1, :], (ROWS, LANES)),
                jnp.broadcast_to(lanes_ref[d : d + 1, :], (ROWS, LANES)),
            )
            for v in range(5):
                block = face[k * ROWS : (k + 1) * ROWS, v * LANES : (v + 1) * LANES]
                slots_ref[k, v] = lane_gather(block, index)
    lane = lax.broadcasted_iota(jnp.int32, (ROWS, LANES), 1)
    turn[:, 120:128, :] = jnp.zeros((2, 8, LANES), jnp.float32)
    for side in range(2):
        for v in range(5):
            both = jnp.where(
                lane < remote,
                slots_ref[side, v],
                jnp.where(lane < 2 * remote, slots_ref[2 + side, v], slots_ref[4 + side, v]),
            )
            both_ref[side, v] = both
            turn[side, 25 * v : 25 * v + 25, :] = both[:25]
        turned = turn[side].T
        for d in range(3):
            for q in range(parts):
                start = d * remote + q * capacity
                place = (q % 2 * (parts // 2) + q // 2) * height + (2 * d + side) * capacity
                pay_ref[place : place + capacity, :] = turned[start : start + capacity]


def repack_kernel(outer, height, pay_ref, keep_ref, side_ref, *refs):
    pairs = (len(refs) - outer) // 2
    across, straight, outs = refs[:pairs], refs[pairs : 2 * pairs], refs[2 * pairs :]
    for z in range(outer):
        outs[z][:height, :] = pay_ref[z * height : (z + 1) * height, :]
        outs[z][height : 2 * height, :] = side_ref[z * height : (z + 1) * height, :]
        total = keep_ref[z]
        for extra in straight:
            total = total + extra[z]
        outs[z][2 * height : 2 * height + 8, :] = total
        total = side_ref[outer * height + 8 * z : outer * height + 8 * z + 8, :]
        for extra in across:
            total = total + extra[z]
        outs[z][2 * height + 8 : 2 * height + 16, :] = total


def volume_kernel(
    grids,
    parts,
    count,
    remote,
    fringes,
    state_ref,
    size_ref,
    plus_ref,
    minus_ref,
    recv_ref,
    slots_ref,
    both_ref,
    volume_ref,
    lanes_ref,
    points_ref,
    part_ref,
    flux_ref,
    edge_ref,
    local_ref,
    back_ref,
    where_ref,
    wide,
    index,
    received,
):
    state = [state_ref[v] for v in range(5)]
    for d in range(3):
        flux = euler(state, *fixed(d))[0]
        scale = size_ref[d : d + 1, :]
        wide[d * LANES + 120 : (d + 1) * LANES, :] = jnp.zeros((8, 5 * LANES), jnp.float32)
        for v in range(5):
            wide[d * LANES : d * LANES + 125, v * LANES : (v + 1) * LANES] = flux[v] * scale
    part_ref[...] = jnp.dot(
        volume_ref[...], wide[...], precision=closer, preferred_element_type=jnp.float32
    )
    for d in range(3):
        low = [slots_ref[2 * d, v] for v in range(5)]
        high = [slots_ref[2 * d + 1, v] for v in range(5)]
        low_flux, low_wave = euler_wave(low, *fixed(d))
        high_flux, high_wave = euler_wave(high, *fixed(d))
        local = mix(high, high_flux, high_wave, low, low_flux, low_wave)
        for v in range(5):
            local_ref[d, v] = local[v]
    lane = lax.broadcasted_iota(jnp.int32, (ROWS, LANES), 1)
    for side in range(2):
        own = [both_ref[side, v] for v in range(5)]
        flux, wave = euler_wave(own, *by_lane(lane < remote, in_lanes(lane, remote, remote)))
        for v in range(5):
            flux_ref[side, v] = flux[v]
        flux_ref[side, 5] = wave
        second = in_lanes(lane, 3 * remote + fringes, fringes)
        third = in_lanes(lane, 3 * remote + 2 * fringes, fringes)
        edge = [
            jnp.where(
                second,
                slots_ref[2 + side, v],
                jnp.where(third, slots_ref[4 + side, v], slots_ref[side, v]),
            )
            for v in range(5)
        ]
        flux, wave = euler_wave(edge, *by_lane(~(second | third), second))
        for v in range(5):
            edge_ref[side, v] = edge[v]
            edge_ref[side, 5 + v] = flux[v]
        edge_ref[side, 10] = wave
    rank = lax.broadcasted_iota(jnp.int32, (LANES, LANES), 0)
    column = lax.broadcasted_iota(jnp.int32, (LANES, LANES), 1)
    index[...] = jnp.zeros_like(index)
    for k in range(6):
        d = k // 2
        order = lane_gather(
            jnp.broadcast_to((minus_ref, plus_ref)[k % 2][d : d + 1, :], (8, LANES)),
            jnp.broadcast_to(lanes_ref[d : d + 1, :], (8, LANES)),
        )
        index[k : k + 1, :] = order[0:1].astype(jnp.float32)
    turned = index[...].T.astype(jnp.int32)
    back_ref[...] = jnp.zeros_like(back_ref)
    for k in range(6):
        found = jnp.where(turned[:, k : k + 1] == column, rank, 0)
        back_ref[k : k + 1, :] = jnp.sum(found, axis=0, keepdims=True)
    me = lax.axis_index("grid")
    received[...] = jnp.zeros_like(received)
    received[0:1, : recv_ref.shape[1]] = recv_ref[...]
    points = points_ref[...]
    slot = jnp.zeros((8, LANES), jnp.int32)
    for block in range(received.shape[1] // LANES):
        held = jnp.broadcast_to(received[0:1, block * LANES : (block + 1) * LANES], (8, LANES))
        inside = (points >= block * LANES) & (points < (block + 1) * LANES)
        picked = lane_gather(held, jnp.where(inside, points - block * LANES, 0))
        slot = jnp.where(inside, picked, slot)
    device = floor_divide(slot, count)
    rest = slot - device * count
    grid = floor_divide(device, parts)
    step = jnp.zeros_like(grid)
    for g in range(grids):
        away = partner(me, g)
        step = jnp.where(grid == g, away, step)
    where_ref[0] = (device - grid * parts) ^ lax.axis_index("dom")
    where_ref[1] = jnp.maximum(step - 1, 0) * count + rest


def distances(outer):
    return [0, outer - 1, *range(1, outer - 1)]


def finish_kernel(parts, capacity, height, fringes, *refs):
    come = dict(zip(distances(parts // 2), refs[: parts // 2]))
    both_ref, flux_ref, edge_ref, local_ref, back_ref, where_ref, part_ref, size_ref, lift_ref = refs[
        parts // 2 : parts // 2 + 9
    ]
    out_ref, turn, turned, wide = refs[parts // 2 + 9 :]
    remote = parts * capacity
    row = lax.broadcasted_iota(jnp.int32, (ROWS, LANES), 0)
    lane = lax.broadcasted_iota(jnp.int32, (ROWS, LANES), 1)
    is_remote = [in_lanes(lane, d * remote, remote) for d in range(3)]
    is_fringe = [in_lanes(lane, 3 * remote + d * fringes, fringes) for d in range(3)]
    any_remote = (lane < 3 * remote) & (row < 25)
    any_fringe = is_fringe[0] | is_fringe[1] | is_fringe[2]
    spread = row[:8] * (3 * fringes) + ((lane[:8] - 3 * remote) & (LANES - 1))
    spread = jnp.where(any_fringe[:8], spread, 0)
    for side in range(2):
        for d in range(3):
            for q in range(parts):
                start = d * remote + q * capacity
                place = q % 2 * height + (2 * d + 1 - side) * capacity
                turn[side, start : start + capacity, :] = come[q // 2][place : place + capacity, :]
        turned[side, :LANES, :] = turn[side].T
    fringe = []
    for v in range(5):
        total = jnp.zeros((8, LANES), jnp.float32)
        for q in range(parts):
            place = 2 * height + q % 2 * 8 + v
            sent = come[q // 2][place : place + 1, :]
            picked = lane_gather(jnp.broadcast_to(sent, (8, LANES)), where_ref[1])
            total = jnp.where(where_ref[0] == q, picked, total)
        fringe.append(total)
    for side in range(2):
        own = [both_ref[side, v] for v in range(5)]
        theirs = [
            jnp.where(any_remote, turned[side, 25 * v : 25 * v + ROWS, :], own[v])
            for v in range(5)
        ]
        their = (theirs, *euler_wave(theirs, *by_lane(is_remote[0], is_remote[1])))
        mine = (own, [flux_ref[side, v] for v in range(5)], flux_ref[side, 5])
        common = mix(*mine, *their) if side else mix(*their, *mine)
        own = [edge_ref[side, v] for v in range(5)]
        theirs = []
        for v in range(5):
            pieces = [
                lane_gather(
                    jnp.broadcast_to(fringe[v][side * 4 + r : side * 4 + r + 1], (8, LANES)), spread
                )
                for r in range(4)
            ]
            theirs.append(jnp.where(any_fringe, jnp.concatenate(pieces, axis=0), own[v]))
        their = (theirs, *euler_wave(theirs, *by_lane(~(is_fringe[1] | is_fringe[2]), is_fringe[1])))
        mine = (own, [edge_ref[side, 5 + v] for v in range(5)], edge_ref[side, 10])
        outer = mix(*mine, *their) if side else mix(*their, *mine)
        for d in range(3):
            k = 2 * d + side
            index = jnp.broadcast_to(back_ref[k : k + 1, :], (ROWS, LANES))
            scale = size_ref[d : d + 1, :]
            for v in range(5):
                value = jnp.where(is_fringe[d], outer[v], local_ref[d, v])
                value = jnp.where(is_remote[d], common[v], value)
                wide[k * ROWS : (k + 1) * ROWS, v * LANES : (v + 1) * LANES] = (
                    lane_gather(value, index) * scale
                )
    total = part_ref[...] + jnp.dot(
        lift_ref[...], wide[...], precision=closer, preferred_element_type=jnp.float32
    )
    for v in range(5):
        out_ref[v] = total[:, v * LANES : (v + 1) * LANES]


def call(kernel, name, out_shape, scratch, flops, size, *operands, limit=VMEM, **more):
    return pl.pallas_call(
        kernel,
        name=name,
        out_shape=out_shape,
        scratch_shapes=scratch,
        compiler_params=pltpu.CompilerParams(vmem_limit_bytes=limit),
        cost_estimate=pl.CostEstimate(flops=flops, bytes_accessed=size, transcendentals=0),
        **more,
    )(*operands)


def body(state, inv_size, plus_order, minus_order, donor_cell, donor_weights, recv_slot):
    columns = state.shape[-1]
    parts = lax.axis_size("dom")
    grids = lax.axis_size("grid")
    capacity = max(1, columns // (3 * parts))
    remote = parts * capacity
    fringes = recv_slot.shape[-1] // 150
    total = donor_cell.shape[-1]
    count = total // (grids * parts)
    held = -(-recv_slot.shape[-1] // LANES) * LANES
    outer = parts // 2
    height = -(-6 * capacity // 8) * 8
    span = parts * count
    blocks = (2 * (LANES - 1) + span) // LANES
    sets = grids - 1
    held_blocks = -(-total // LANES) + blocks
    faces, volume, lift = matrices()
    points = fringe_lanes(fringes)
    f32 = functools.partial(jax.ShapeDtypeStruct, dtype=jnp.float32)
    i32 = functools.partial(jax.ShapeDtypeStruct, dtype=jnp.int32)
    memory = functools.partial(pltpu.VMEM, dtype=jnp.float32)

    def exchange(values, step, move):
        pairs = [
            (g * parts + q, partner(g, step) * parts + partner(q, move))
            for g in range(grids)
            for q in range(parts)
        ]
        return lax.ppermute(values, ("grid", "dom"), pairs)

    weights = donor_weights.reshape(15, 1, total)
    mates = [exchange(values, 1, 0) for values in (state, donor_cell, weights)]
    expand, lanes = call(
        functools.partial(table_kernel, parts, capacity, fringes),
        "tables",
        (jax.ShapeDtypeStruct((2 * ROWS, 48), jnp.bfloat16), i32((8, LANES))),
        [],
        400_000_000,
        3_000_000,
    )
    slots, both, pay = call(
        functools.partial(face_kernel, parts, capacity, height),
        "faces",
        (
            f32((6, 5, ROWS, LANES)),
            f32((2, 5, ROWS, LANES)),
            f32((parts * height, LANES)),
        ),
        [memory((2, LANES, LANES))],
        200_000_000,
        1_500_000,
        state,
        plus_order,
        minus_order,
        faces,
        lanes,
    )
    keep, side, *sent = call(
        functools.partial(donor_kernel, grids, parts, count, height),
        "donors",
        (
            f32((outer, 8, LANES)),
            f32((outer * (height + 8), LANES)),
            *(f32((outer, 8, LANES)) for _ in range(grids - 2)),
        ),
        [
            pltpu.VMEM((2, held_blocks, 8, LANES), jnp.int32),
            memory((2, held_blocks, 16, LANES)),
            memory((sets, ROWS, blocks * LANES)),
            memory((sets, blocks + 1, 8, LANES)),
        ],
        5_000_000,
        500_000,
        state,
        mates[0],
        donor_cell,
        mates[1],
        weights,
        mates[2],
        expand,
        pay,
    )
    side = exchange(side, 0, 1)
    across = [exchange(sent[k + 1], k + 2, 1) for k in range(0, grids - 2, 2)]
    straight = [exchange(sent[k], k + 2, 0) for k in range(0, grids - 2, 2)]
    packed = call(
        functools.partial(repack_kernel, outer, height),
        "repack",
        tuple(f32((2 * height + 16, LANES)) for _ in range(outer)),
        [],
        50_000,
        200_000,
        pay,
        keep,
        side,
        *across,
        *straight,
    )
    come = [exchange(packed[z], 0, 2 * z) if z else packed[z] for z in distances(outer)]
    part, flux, edge, local, back, where = call(
        functools.partial(volume_kernel, grids, parts, count, remote, fringes),
        "volume",
        (
            f32((125, 5 * LANES)),
            f32((2, 6, ROWS, LANES)),
            f32((2, 11, ROWS, LANES)),
            f32((3, 5, ROWS, LANES)),
            i32((8, LANES)),
            i32((2, 8, LANES)),
        ),
        [
            memory((3 * LANES, 5 * LANES)),
            memory((LANES, LANES)),
            pltpu.VMEM((8, held), jnp.int32),
        ],
        400_000_000,
        3_000_000,
        state,
        inv_size,
        plus_order,
        minus_order,
        recv_slot,
        slots,
        both,
        volume,
        lanes,
        points,
    )
    return call(
        functools.partial(finish_kernel, parts, capacity, height, fringes),
        "finish",
        f32((5, 125, columns)),
        [
            memory((2, LANES, LANES)),
            memory((2, LANES + 8, LANES)),
            memory((6 * ROWS, 5 * LANES)),
        ],
        200_000_000,
        3_000_000,
        *come,
        both,
        flux,
        edge,
        local,
        back,
        where,
        part,
        inv_size,
        lift,
    )


def solution(mesh):
    return jax.shard_map(
        body,
        mesh=mesh,
        in_specs=(
            P(None, None, ("grid", "dom")),
            P(None, ("grid", "dom")),
            P(None, ("grid", "dom")),
            P(None, ("grid", "dom")),
            P(("grid", "dom"), None),
            P(("grid", "dom"), None, None, None),
            P(("grid", "dom"), None),
        ),
        out_specs=P(None, None, ("grid", "dom")),
        check_vma=False,
    )
```

```python
import functools
import math

import jax
import jax.numpy as jnp
import ml_dtypes
import numpy as np
from jax import lax
from jax.experimental import pallas as pl
from jax.experimental.pallas import tpu as pltpu
from jax.sharding import PartitionSpec as P

closer = lax.Precision.HIGH
LANES = 128
SHIFT = (1.0, 0.0, 0.0, 0.0, 2.5)
ROWS = 32
VMEM = 48 * 1024 * 1024


def gauss_nodes():
    outer = math.sqrt(5.0 + 2.0 * math.sqrt(10.0 / 7.0)) / 3.0
    inner = math.sqrt(5.0 - 2.0 * math.sqrt(10.0 / 7.0)) / 3.0
    return [-outer, -inner, 0.0, inner, outer]


def basis_value(nodes, column, target):
    value = 1.0
    for other in range(5):
        if other != column:
            value = value * (target - nodes[other]) / (nodes[column] - nodes[other])
    return value


def basis_slope(nodes, column, target):
    total = 0.0
    for skipped in range(5):
        if skipped != column:
            value = 1.0 / (nodes[column] - nodes[skipped])
            for other in range(5):
                if other != column and other != skipped:
                    value = value * (target - nodes[other]) / (nodes[column] - nodes[other])
            total = total + value
    return total


def legendre_slopes(target):
    values = [1.0, target]
    slopes = [0.0, 1.0]
    for order in range(1, 5):
        values.append(
            ((2 * order + 1) * target * values[order] - order * values[order - 1]) / (order + 1)
        )
        slopes.append(slopes[order - 1] + (2 * order + 1) * values[order])
    return (slopes[4], slopes[5])


def tables():
    nodes = gauss_nodes()
    deriv = [[basis_slope(nodes, column, nodes[row]) for column in range(5)] for row in range(5)]
    lower = [basis_value(nodes, column, -1.0) for column in range(5)]
    upper = [basis_value(nodes, column, 1.0) for column in range(5)]
    lift_low = []
    lift_high = []
    for row in range(5):
        slope_four, slope_five = legendre_slopes(nodes[row])
        lift_low.append(-0.5 * (slope_five - slope_four))
        lift_high.append(0.5 * (slope_five + slope_four))
    return tuple(np.asarray(m, np.float64) for m in (deriv, lower, upper, lift_low, lift_high))


def split_point(point, direction):
    index = [point // 25, point // 5 % 5, point % 5]
    along = index.pop(direction)
    return along, 5 * index[0] + index[1]


def matrices():
    deriv, lower, upper, lift_low, lift_high = tables()
    faces = np.zeros((6 * ROWS, 125))
    volume = np.zeros((125, 3 * LANES))
    lift = np.zeros((125, 6 * ROWS))
    own = deriv - np.outer(lift_low, lower) - np.outer(lift_high, upper)
    for d in range(3):
        for p in range(125):
            i, t = split_point(p, d)
            faces[(2 * d) * ROWS + t, p] = lower[i]
            faces[(2 * d + 1) * ROWS + t, p] = upper[i]
            lift[p, (2 * d) * ROWS + t] = -lift_low[i]
            lift[p, (2 * d + 1) * ROWS + t] = -lift_high[i]
            for other in range(125):
                m, line = split_point(other, d)
                if line == t:
                    volume[p, d * LANES + other] = -own[i, m]
    for k in range(6):
        faces[k * ROWS + 25 : (k + 1) * ROWS] = faces[k * ROWS + 24]
    return tuple(m.astype(np.float32) for m in (faces, volume, lift))


def fringe_lanes(fringes):
    found = np.zeros((8, LANES), np.int32)
    for side in range(2):
        for t in range(ROWS):
            for d in range(3):
                for i in range(fringes):
                    point = ((2 * d + side) * 25 + min(t, 24)) * fringes + i
                    found[side * 4 + t // 8, (t % 8 * 3 + d) * fringes + i] = point
    return found


def partner(index, step):
    return index ^ step


def lane_gather(values, index):
    return jnp.take_along_axis(values, index, axis=1, mode="promise_in_bounds")


def in_lanes(lane, start, width):
    start = start % LANES
    if start + width <= LANES:
        return (lane >= start) & (lane < start + width)
    return (lane >= start) | (lane < start + width - LANES)


def euler(state, choose, along):
    density, momenta, energy = state[0], state[1:4], state[4]
    inverse = 1.0 / density
    normal = choose(momenta)
    speed = normal * inverse
    squares = momenta[0] * momenta[0] + momenta[1] * momenta[1] + momenta[2] * momenta[2]
    pressure = 0.4 * (energy - 0.5 * squares * inverse)
    flux = [normal] + [m * speed for m in momenta] + [(energy + pressure) * speed]
    for d in range(3):
        flux[1 + d] = along(d, flux[1 + d], pressure - 1.0)
    return flux, speed, pressure, inverse


def euler_wave(state, choose, along):
    flux, speed, pressure, inverse = euler(state, choose, along)
    return flux, jnp.abs(speed) + jnp.sqrt(1.4 * pressure * inverse)


def fixed(direction):
    def choose(parts):
        return parts[direction]

    def along(d, flux, pressure):
        return flux + pressure if d == direction else flux

    return choose, along


def by_lane(first, second):
    def choose(parts):
        return jnp.where(first, parts[0], jnp.where(second, parts[1], parts[2]))

    third = ~(first | second)

    def along(d, flux, pressure):
        return flux + jnp.where((first, second, third)[d], pressure, 0.0)

    return choose, along


def mix(left, left_flux, left_wave, right, right_flux, right_wave):
    wave = 0.5 * jnp.maximum(left_wave, right_wave)
    return [
        0.5 * (left_flux[v] + right_flux[v]) - wave * (right[v] - left[v]) for v in range(5)
    ]


def floor_divide(values, divisor):
    return ((values.astype(jnp.float32) + 0.5) * (1.0 / divisor)).astype(jnp.int32)


def table_kernel(parts, capacity, fringes, expand_ref, lanes_ref):
    row = lax.broadcasted_iota(jnp.int32, expand_ref.shape, 0)
    column = lax.broadcasted_iota(jnp.int32, expand_ref.shape, 1) & 15
    point = row & (ROWS - 1)
    point = jnp.where(point >= 25, point - 25, point)
    tens = floor_divide(point, 5)
    wanted = jnp.where(row < ROWS, 5 + tens, 10 + point - 5 * tens)
    expand_ref[...] = jnp.where(column == wanted, 1.0, 0.0).astype(jnp.bfloat16)
    me = lax.axis_index("dom")
    remote = parts * capacity
    row = lax.broadcasted_iota(jnp.int32, (8, LANES), 0)
    lane = lax.broadcasted_iota(jnp.int32, (8, LANES), 1)
    total = jnp.zeros((8, LANES), jnp.int32)
    for d in range(3):
        near = jnp.clip(lane - d * remote, 0, remote - 1)
        away = floor_divide(near, capacity)
        slot = (away ^ me) * capacity + near - away * capacity
        edge = (lane - 3 * remote - d * fringes) & (LANES - 1)
        start = (3 * remote + d * fringes) % LANES
        taken = jnp.clip(lane - d * remote, 0, remote) + jnp.clip(
            lane - start, 0, min(fringes, LANES - start)
        )
        if start + fringes > LANES:
            taken = taken + jnp.clip(lane, 0, start + fringes - LANES)
        other = remote + fringes + lane - taken
        slot = jnp.where(
            in_lanes(lane, d * remote, remote),
            slot,
            jnp.where(edge < fringes, remote + edge, other),
        )
        total = jnp.where(row == d, slot, total)
    lanes_ref[...] = total


def donor_kernel(grids, parts, count, height, *refs):
    states, cell_refs, weight_refs, expand_ref, pay_ref = *(refs[k : k + 2] for k in (0, 2, 4)), *refs[6:8]
    keep_ref, side_ref = refs[8:10]
    outs = refs[10 : 8 + grids]
    cells, weights, planes, values = refs[8 + grids :]
    outer = parts // 2
    side_ref[: outer * height, :] = pay_ref[outer * height :, :]
    span = parts * count
    total = grids * span
    blocks = values.shape[1] - 1
    width = blocks * LANES
    cells[...] = jnp.zeros_like(cells)
    weights[...] = jnp.zeros_like(weights)
    halves = []
    for source in range(2):
        for block in range(-(-total // LANES)):
            lanes = slice(block * LANES, min((block + 1) * LANES, total))
            held = lanes.stop - lanes.start
            cells[source, block, 0:1, :held] = cell_refs[source][:, lanes]
            for k in range(15):
                weights[source, block, k : k + 1, :held] = weight_refs[source][k, :, lanes]
        for v in range(5):
            shifted = states[source][v] - SHIFT[v]
            high = shifted.astype(jnp.bfloat16)
            low = (shifted - high.astype(jnp.float32)).astype(jnp.bfloat16)
            halves.append(jnp.concatenate([high, low], axis=1))
    element = lax.broadcasted_iota(jnp.int32, (LANES, width), 0)
    row = lax.broadcasted_iota(jnp.int32, (8, width), 0)
    lane = lax.broadcasted_iota(jnp.int32, (8, LANES), 1)
    me = lax.axis_index("grid")
    here = lax.axis_index("dom")
    number = 0
    for step in range(0, grids, 2):
        start = partner(me, step) * span
        first = start // LANES
        found = [jnp.zeros((8, LANES), jnp.float32)] * parts
        for source in range(0 if step else 1, 2):
            held = jnp.concatenate([cells[source, first + i] for i in range(blocks)], axis=1)
            chosen = jnp.where(element == held[0:1], 1.0, 0.0).astype(jnp.bfloat16)
            chosen = jnp.concatenate([chosen, chosen], axis=0)
            held = jnp.concatenate([weights[source, first + i] for i in range(blocks)], axis=1)
            high = held.astype(jnp.bfloat16)
            rest = held - high.astype(jnp.float32)
            middle = rest.astype(jnp.bfloat16)
            low = (rest - middle.astype(jnp.float32)).astype(jnp.bfloat16)
            pieces = jnp.concatenate([high, middle, low], axis=0)
            plane = jnp.dot(expand_ref[...], pieces, preferred_element_type=jnp.float32)
            planes[number] = plane[:ROWS] * plane[ROWS:]
            tiles = []
            for top in range(0, LANES, 8):
                a = top // 25
                factor = jnp.broadcast_to(held[a : a + 1], (8, width))
                if top < 25 * (a + 1) < top + 8 and a < 4:
                    later = jnp.broadcast_to(held[a + 1 : a + 2], (8, width))
                    factor = jnp.where(row < 25 * (a + 1) - top, factor, later)
                tiles.append(factor * planes[number, top % 25 : top % 25 + 8, :])
            weight = jnp.concatenate(tiles, axis=0)[:125]
            for v in range(5):
                picked = jnp.dot(
                    halves[5 * source + v], chosen, preferred_element_type=jnp.float32
                )
                value = jnp.sum(picked * weight, axis=0, keepdims=True) + SHIFT[v]
                for block in range(blocks):
                    values[number, block, v : v + 1, :] = value[
                        :, block * LANES : (block + 1) * LANES
                    ]
            place = (step + source - 1) * count
            wanted = in_lanes(lane, place, count)
            for q in range(parts):
                offset = start - first * LANES + partner(here, q) * count
                block = offset // LANES
                index = lane + (offset - block * LANES - place)
                inside = index & (LANES - 1)
                near = lane_gather(values[number, block], inside)
                far = lane_gather(values[number, block + 1], inside)
                found[q] = jnp.where(wanted, jnp.where(index < LANES, near, far), found[q])
            number += 1
        for z in range(outer):
            if step:
                outs[step - 2][z] = found[2 * z]
                outs[step - 1][z] = found[2 * z + 1]
            else:
                keep_ref[z] = found[2 * z]
                side_ref[outer * height + 8 * z : outer * height + 8 * z + 8, :] = found[2 * z + 1]


def face_kernel(
    parts,
    capacity,
    height,
    state_ref,
    plus_ref,
    minus_ref,
    faces_ref,
    lanes_ref,
    slots_ref,
    both_ref,
    pay_ref,
    turn,
):
    remote = parts * capacity
    wide = jnp.concatenate([state_ref[v] - SHIFT[v] for v in range(5)], axis=1)
    face = jnp.dot(
        faces_ref[...], wide, precision=closer, preferred_element_type=jnp.float32
    )
    for side in range(2):
        order = (minus_ref, plus_ref)[side]
        for d in range(3):
            k = 2 * d + side
            index = lane_gather(
                jnp.broadcast_to(order[d : d + 1, :], (ROWS, LANES)),
                jnp.broadcast_to(lanes_ref[d : d + 1, :], (ROWS, LANES)),
            )
            for v in range(5):
                block = face[k * ROWS : (k + 1) * ROWS, v * LANES : (v + 1) * LANES]
                slots_ref[k, v] = lane_gather(block, index) + SHIFT[v]
    lane = lax.broadcasted_iota(jnp.int32, (ROWS, LANES), 1)
    turn[:, 120:128, :] = jnp.zeros((2, 8, LANES), jnp.float32)
    for side in range(2):
        for v in range(5):
            both = jnp.where(
                lane < remote,
                slots_ref[side, v],
                jnp.where(lane < 2 * remote, slots_ref[2 + side, v], slots_ref[4 + side, v]),
            )
            both_ref[side, v] = both
            turn[side, 25 * v : 25 * v + 25, :] = both[:25]
        turned = turn[side].T
        for d in range(3):
            for q in range(parts):
                start = d * remote + q * capacity
                place = (q % 2 * (parts // 2) + q // 2) * height + (2 * d + side) * capacity
                pay_ref[place : place + capacity, :] = turned[start : start + capacity]


def repack_kernel(outer, height, pay_ref, keep_ref, side_ref, *refs):
    pairs = (len(refs) - outer) // 2
    across, straight, outs = refs[:pairs], refs[pairs : 2 * pairs], refs[2 * pairs :]
    for z in range(outer):
        outs[z][:height, :] = pay_ref[z * height : (z + 1) * height, :]
        outs[z][height : 2 * height, :] = side_ref[z * height : (z + 1) * height, :]
        total = keep_ref[z]
        for extra in straight:
            total = total + extra[z]
        outs[z][2 * height : 2 * height + 8, :] = total
        total = side_ref[outer * height + 8 * z : outer * height + 8 * z + 8, :]
        for extra in across:
            total = total + extra[z]
        outs[z][2 * height + 8 : 2 * height + 16, :] = total


def volume_kernel(
    grids,
    parts,
    count,
    remote,
    fringes,
    state_ref,
    size_ref,
    plus_ref,
    minus_ref,
    recv_ref,
    slots_ref,
    both_ref,
    volume_ref,
    lanes_ref,
    points_ref,
    part_ref,
    flux_ref,
    edge_ref,
    local_ref,
    back_ref,
    where_ref,
    wide,
    index,
    received,
):
    state = [state_ref[v] for v in range(5)]
    for d in range(3):
        flux = euler(state, *fixed(d))[0]
        scale = size_ref[d : d + 1, :]
        wide[d * LANES + 120 : (d + 1) * LANES, :] = jnp.zeros((8, 5 * LANES), jnp.float32)
        for v in range(5):
            wide[d * LANES : d * LANES + 125, v * LANES : (v + 1) * LANES] = flux[v] * scale
    part_ref[...] = jnp.dot(
        volume_ref[...], wide[...], precision=closer, preferred_element_type=jnp.float32
    )
    for d in range(3):
        low = [slots_ref[2 * d, v] for v in range(5)]
        high = [slots_ref[2 * d + 1, v] for v in range(5)]
        low_flux, low_wave = euler_wave(low, *fixed(d))
        high_flux, high_wave = euler_wave(high, *fixed(d))
        local = mix(high, high_flux, high_wave, low, low_flux, low_wave)
        for v in range(5):
            local_ref[d, v] = local[v]
    lane = lax.broadcasted_iota(jnp.int32, (ROWS, LANES), 1)
    for side in range(2):
        own = [both_ref[side, v] for v in range(5)]
        flux, wave = euler_wave(own, *by_lane(lane < remote, in_lanes(lane, remote, remote)))
        for v in range(5):
            flux_ref[side, v] = flux[v]
        flux_ref[side, 5] = wave
        second = in_lanes(lane, 3 * remote + fringes, fringes)
        third = in_lanes(lane, 3 * remote + 2 * fringes, fringes)
        edge = [
            jnp.where(
                second,
                slots_ref[2 + side, v],
                jnp.where(third, slots_ref[4 + side, v], slots_ref[side, v]),
            )
            for v in range(5)
        ]
        flux, wave = euler_wave(edge, *by_lane(~(second | third), second))
        for v in range(5):
            edge_ref[side, v] = edge[v]
            edge_ref[side, 5 + v] = flux[v]
        edge_ref[side, 10] = wave
    rank = lax.broadcasted_iota(jnp.int32, (LANES, LANES), 0)
    column = lax.broadcasted_iota(jnp.int32, (LANES, LANES), 1)
    index[...] = jnp.zeros_like(index)
    for k in range(6):
        d = k // 2
        order = lane_gather(
            jnp.broadcast_to((minus_ref, plus_ref)[k % 2][d : d + 1, :], (8, LANES)),
            jnp.broadcast_to(lanes_ref[d : d + 1, :], (8, LANES)),
        )
        index[k : k + 1, :] = order[0:1].astype(jnp.float32)
    turned = index[...].T.astype(jnp.int32)
    back_ref[...] = jnp.zeros_like(back_ref)
    for k in range(6):
        found = jnp.where(turned[:, k : k + 1] == column, rank, 0)
        back_ref[k : k + 1, :] = jnp.sum(found, axis=0, keepdims=True)
    me = lax.axis_index("grid")
    received[...] = jnp.zeros_like(received)
    received[0:1, : recv_ref.shape[1]] = recv_ref[...]
    points = points_ref[...]
    slot = jnp.zeros((8, LANES), jnp.int32)
    for block in range(received.shape[1] // LANES):
        held = jnp.broadcast_to(received[0:1, block * LANES : (block + 1) * LANES], (8, LANES))
        inside = (points >= block * LANES) & (points < (block + 1) * LANES)
        picked = lane_gather(held, jnp.where(inside, points - block * LANES, 0))
        slot = jnp.where(inside, picked, slot)
    device = floor_divide(slot, count)
    rest = slot - device * count
    grid = floor_divide(device, parts)
    step = jnp.zeros_like(grid)
    for g in range(grids):
        away = partner(me, g)
        step = jnp.where(grid == g, away, step)
    where_ref[0] = (device - grid * parts) ^ lax.axis_index("dom")
    where_ref[1] = jnp.maximum(step - 1, 0) * count + rest


def distances(outer):
    return [0, outer - 1, *range(1, outer - 1)]


def finish_kernel(parts, capacity, height, fringes, *refs):
    come = dict(zip(distances(parts // 2), refs[: parts // 2]))
    both_ref, flux_ref, edge_ref, local_ref, back_ref, where_ref, part_ref, size_ref, lift_ref = refs[
        parts // 2 : parts // 2 + 9
    ]
    out_ref, turn, turned, wide = refs[parts // 2 + 9 :]
    remote = parts * capacity
    row = lax.broadcasted_iota(jnp.int32, (ROWS, LANES), 0)
    lane = lax.broadcasted_iota(jnp.int32, (ROWS, LANES), 1)
    is_remote = [in_lanes(lane, d * remote, remote) for d in range(3)]
    is_fringe = [in_lanes(lane, 3 * remote + d * fringes, fringes) for d in range(3)]
    any_remote = (lane < 3 * remote) & (row < 25)
    any_fringe = is_fringe[0] | is_fringe[1] | is_fringe[2]
    spread = row[:8] * (3 * fringes) + ((lane[:8] - 3 * remote) & (LANES - 1))
    spread = jnp.where(any_fringe[:8], spread, 0)
    for side in range(2):
        for d in range(3):
            for q in range(parts):
                start = d * remote + q * capacity
                place = q % 2 * height + (2 * d + 1 - side) * capacity
                turn[side, start : start + capacity, :] = come[q // 2][place : place + capacity, :]
        turned[side, :LANES, :] = turn[side].T
    fringe = []
    for v in range(5):
        total = jnp.zeros((8, LANES), jnp.float32)
        for q in range(parts):
            place = 2 * height + q % 2 * 8 + v
            sent = come[q // 2][place : place + 1, :]
            picked = lane_gather(jnp.broadcast_to(sent, (8, LANES)), where_ref[1])
            total = jnp.where(where_ref[0] == q, picked, total)
        fringe.append(total)
    for side in range(2):
        own = [both_ref[side, v] for v in range(5)]
        theirs = [
            jnp.where(any_remote, turned[side, 25 * v : 25 * v + ROWS, :], own[v])
            for v in range(5)
        ]
        their = (theirs, *euler_wave(theirs, *by_lane(is_remote[0], is_remote[1])))
        mine = (own, [flux_ref[side, v] for v in range(5)], flux_ref[side, 5])
        common = mix(*mine, *their) if side else mix(*their, *mine)
        own = [edge_ref[side, v] for v in range(5)]
        theirs = []
        for v in range(5):
            pieces = [
                lane_gather(
                    jnp.broadcast_to(fringe[v][side * 4 + r : side * 4 + r + 1], (8, LANES)), spread
                )
                for r in range(4)
            ]
            theirs.append(jnp.where(any_fringe, jnp.concatenate(pieces, axis=0), own[v]))
        their = (theirs, *euler_wave(theirs, *by_lane(~(is_fringe[1] | is_fringe[2]), is_fringe[1])))
        mine = (own, [edge_ref[side, 5 + v] for v in range(5)], edge_ref[side, 10])
        outer = mix(*mine, *their) if side else mix(*their, *mine)
        for d in range(3):
            k = 2 * d + side
            index = jnp.broadcast_to(back_ref[k : k + 1, :], (ROWS, LANES))
            scale = size_ref[d : d + 1, :]
            for v in range(5):
                value = jnp.where(is_fringe[d], outer[v], local_ref[d, v])
                value = jnp.where(is_remote[d], common[v], value)
                wide[k * ROWS : (k + 1) * ROWS, v * LANES : (v + 1) * LANES] = (
                    lane_gather(value, index) * scale
                )
    values = wide[...]
    high = values.astype(jnp.bfloat16)
    low = (values - high.astype(jnp.float32)).astype(jnp.bfloat16)
    first = jnp.dot(lift_ref[...], high, preferred_element_type=jnp.float32)
    second = jnp.dot(lift_ref[:LANES], low, preferred_element_type=jnp.float32)
    total = part_ref[...] + (first[:125] + (first[LANES : LANES + 125] + second[:125]))
    for v in range(5):
        out_ref[v] = total[:, v * LANES : (v + 1) * LANES]


def call(kernel, name, out_shape, scratch, flops, size, *operands, limit=VMEM, **more):
    return pl.pallas_call(
        kernel,
        name=name,
        out_shape=out_shape,
        scratch_shapes=scratch,
        compiler_params=pltpu.CompilerParams(vmem_limit_bytes=limit),
        cost_estimate=pl.CostEstimate(flops=flops, bytes_accessed=size, transcendentals=0),
        **more,
    )(*operands)


def body(state, inv_size, plus_order, minus_order, donor_cell, donor_weights, recv_slot):
    columns = state.shape[-1]
    parts = lax.axis_size("dom")
    grids = lax.axis_size("grid")
    capacity = max(1, columns // (3 * parts))
    remote = parts * capacity
    fringes = recv_slot.shape[-1] // 150
    total = donor_cell.shape[-1]
    count = total // (grids * parts)
    held = -(-recv_slot.shape[-1] // LANES) * LANES
    outer = parts // 2
    height = -(-6 * capacity // 8) * 8
    span = parts * count
    blocks = (2 * (LANES - 1) + span) // LANES
    sets = grids - 1
    held_blocks = -(-total // LANES) + blocks
    faces, volume, lift = matrices()
    lift = np.pad(lift, ((0, LANES - 125), (0, 0)))
    high = lift.astype(ml_dtypes.bfloat16)
    lift = np.concatenate([high, (lift - high.astype(np.float32)).astype(ml_dtypes.bfloat16)])
    points = fringe_lanes(fringes)
    f32 = functools.partial(jax.ShapeDtypeStruct, dtype=jnp.float32)
    i32 = functools.partial(jax.ShapeDtypeStruct, dtype=jnp.int32)
    memory = functools.partial(pltpu.VMEM, dtype=jnp.float32)

    def exchange(values, step, move):
        pairs = [
            (g * parts + q, partner(g, step) * parts + partner(q, move))
            for g in range(grids)
            for q in range(parts)
        ]
        return lax.ppermute(values, ("grid", "dom"), pairs)

    weights = donor_weights.reshape(15, 1, total)
    mates = [exchange(values, 1, 0) for values in (state, donor_cell, weights)]
    expand, lanes = call(
        functools.partial(table_kernel, parts, capacity, fringes),
        "tables",
        (jax.ShapeDtypeStruct((2 * ROWS, 48), jnp.bfloat16), i32((8, LANES))),
        [],
        400_000_000,
        3_000_000,
    )
    slots, both, pay = call(
        functools.partial(face_kernel, parts, capacity, height),
        "faces",
        (
            f32((6, 5, ROWS, LANES)),
            f32((2, 5, ROWS, LANES)),
            f32((parts * height, LANES)),
        ),
        [memory((2, LANES, LANES))],
        200_000_000,
        1_500_000,
        state,
        plus_order,
        minus_order,
        faces,
        lanes,
    )
    keep, side, *sent = call(
        functools.partial(donor_kernel, grids, parts, count, height),
        "donors",
        (
            f32((outer, 8, LANES)),
            f32((outer * (height + 8), LANES)),
            *(f32((outer, 8, LANES)) for _ in range(grids - 2)),
        ),
        [
            pltpu.VMEM((2, held_blocks, 8, LANES), jnp.int32),
            memory((2, held_blocks, 16, LANES)),
            memory((sets, ROWS, blocks * LANES)),
            memory((sets, blocks + 1, 8, LANES)),
        ],
        5_000_000,
        500_000,
        state,
        mates[0],
        donor_cell,
        mates[1],
        weights,
        mates[2],
        expand,
        pay,
    )
    side = exchange(side, 0, 1)
    across = [exchange(sent[k + 1], k + 2, 1) for k in range(0, grids - 2, 2)]
    straight = [exchange(sent[k], k + 2, 0) for k in range(0, grids - 2, 2)]
    packed = call(
        functools.partial(repack_kernel, outer, height),
        "repack",
        tuple(f32((2 * height + 16, LANES)) for _ in range(outer)),
        [],
        50_000,
        200_000,
        pay,
        keep,
        side,
        *across,
        *straight,
    )
    come = [exchange(packed[z], 0, 2 * z) if z else packed[z] for z in distances(outer)]
    part, flux, edge, local, back, where = call(
        functools.partial(volume_kernel, grids, parts, count, remote, fringes),
        "volume",
        (
            f32((125, 5 * LANES)),
            f32((2, 6, ROWS, LANES)),
            f32((2, 11, ROWS, LANES)),
            f32((3, 5, ROWS, LANES)),
            i32((8, LANES)),
            i32((2, 8, LANES)),
        ),
        [
            memory((3 * LANES, 5 * LANES)),
            memory((LANES, LANES)),
            pltpu.VMEM((8, held), jnp.int32),
        ],
        400_000_000,
        3_000_000,
        state,
        inv_size,
        plus_order,
        minus_order,
        recv_slot,
        slots,
        both,
        volume,
        lanes,
        points,
    )
    return call(
        functools.partial(finish_kernel, parts, capacity, height, fringes),
        "finish",
        f32((5, 125, columns)),
        [
            memory((2, LANES, LANES)),
            memory((2, LANES + 8, LANES)),
            memory((6 * ROWS, 5 * LANES)),
        ],
        200_000_000,
        3_000_000,
        *come,
        both,
        flux,
        edge,
        local,
        back,
        where,
        part,
        inv_size,
        lift,
    )


def solution(mesh):
    return jax.shard_map(
        body,
        mesh=mesh,
        in_specs=(
            P(None, None, ("grid", "dom")),
            P(None, ("grid", "dom")),
            P(None, ("grid", "dom")),
            P(None, ("grid", "dom")),
            P(("grid", "dom"), None),
            P(("grid", "dom"), None, None, None),
            P(("grid", "dom"), None),
        ),
        out_specs=P(None, None, ("grid", "dom")),
        check_vma=False,
    )
```

```python
import functools
import math

import jax
import jax.numpy as jnp
import ml_dtypes
import numpy as np
from jax import lax
from jax.experimental import pallas as pl
from jax.experimental.pallas import tpu as pltpu
from jax.sharding import PartitionSpec as P

closer = lax.Precision.HIGH
LANES = 128
SHIFT = (1.0, 0.0, 0.0, 0.0, 2.5)
ROWS = 32
VMEM = 48 * 1024 * 1024


def gauss_nodes():
    outer = math.sqrt(5.0 + 2.0 * math.sqrt(10.0 / 7.0)) / 3.0
    inner = math.sqrt(5.0 - 2.0 * math.sqrt(10.0 / 7.0)) / 3.0
    return [-outer, -inner, 0.0, inner, outer]


def basis_value(nodes, column, target):
    value = 1.0
    for other in range(5):
        if other != column:
            value = value * (target - nodes[other]) / (nodes[column] - nodes[other])
    return value


def basis_slope(nodes, column, target):
    total = 0.0
    for skipped in range(5):
        if skipped != column:
            value = 1.0 / (nodes[column] - nodes[skipped])
            for other in range(5):
                if other != column and other != skipped:
                    value = value * (target - nodes[other]) / (nodes[column] - nodes[other])
            total = total + value
    return total


def legendre_slopes(target):
    values = [1.0, target]
    slopes = [0.0, 1.0]
    for order in range(1, 5):
        values.append(
            ((2 * order + 1) * target * values[order] - order * values[order - 1]) / (order + 1)
        )
        slopes.append(slopes[order - 1] + (2 * order + 1) * values[order])
    return (slopes[4], slopes[5])


def tables():
    nodes = gauss_nodes()
    deriv = [[basis_slope(nodes, column, nodes[row]) for column in range(5)] for row in range(5)]
    lower = [basis_value(nodes, column, -1.0) for column in range(5)]
    upper = [basis_value(nodes, column, 1.0) for column in range(5)]
    lift_low = []
    lift_high = []
    for row in range(5):
        slope_four, slope_five = legendre_slopes(nodes[row])
        lift_low.append(-0.5 * (slope_five - slope_four))
        lift_high.append(0.5 * (slope_five + slope_four))
    return tuple(np.asarray(m, np.float64) for m in (deriv, lower, upper, lift_low, lift_high))


def split_point(point, direction):
    index = [point // 25, point // 5 % 5, point % 5]
    along = index.pop(direction)
    return along, 5 * index[0] + index[1]


def matrices():
    deriv, lower, upper, lift_low, lift_high = tables()
    faces = np.zeros((6 * ROWS, 125))
    volume = np.zeros((125, 3 * LANES))
    lift = np.zeros((125, 6 * ROWS))
    own = deriv - np.outer(lift_low, lower) - np.outer(lift_high, upper)
    for d in range(3):
        for p in range(125):
            i, t = split_point(p, d)
            faces[(2 * d) * ROWS + t, p] = lower[i]
            faces[(2 * d + 1) * ROWS + t, p] = upper[i]
            lift[p, (2 * d) * ROWS + t] = -lift_low[i]
            lift[p, (2 * d + 1) * ROWS + t] = -lift_high[i]
            for other in range(125):
                m, line = split_point(other, d)
                if line == t:
                    volume[p, d * LANES + other] = -own[i, m]
    for k in range(6):
        faces[k * ROWS + 25 : (k + 1) * ROWS] = faces[k * ROWS + 24]
    return tuple(m.astype(np.float32) for m in (faces, volume, lift))


def fringe_lanes(fringes):
    found = np.zeros((8, LANES), np.int32)
    for side in range(2):
        for t in range(ROWS):
            for d in range(3):
                for i in range(fringes):
                    point = ((2 * d + side) * 25 + min(t, 24)) * fringes + i
                    found[side * 4 + t // 8, (t % 8 * 3 + d) * fringes + i] = point
    return found


def partner(index, step):
    return index ^ step


def lane_gather(values, index):
    return jnp.take_along_axis(values, index, axis=1, mode="promise_in_bounds")


def in_lanes(lane, start, width):
    start = start % LANES
    if start + width <= LANES:
        return (lane >= start) & (lane < start + width)
    return (lane >= start) | (lane < start + width - LANES)


def euler(state, choose, along):
    density, momenta, energy = state[0], state[1:4], state[4]
    inverse = 1.0 / density
    normal = choose(momenta)
    speed = normal * inverse
    squares = momenta[0] * momenta[0] + momenta[1] * momenta[1] + momenta[2] * momenta[2]
    pressure = 0.4 * (energy - 0.5 * squares * inverse)
    flux = [normal] + [m * speed for m in momenta] + [(energy + pressure) * speed]
    for d in range(3):
        flux[1 + d] = along(d, flux[1 + d], pressure - 1.0)
    return flux, speed, pressure, inverse


def euler_wave(state, choose, along):
    flux, speed, pressure, inverse = euler(state, choose, along)
    return flux, jnp.abs(speed) + jnp.sqrt(1.4 * pressure * inverse)


def fixed(direction):
    def choose(parts):
        return parts[direction]

    def along(d, flux, pressure):
        return flux + pressure if d == direction else flux

    return choose, along


def by_lane(first, second):
    def choose(parts):
        return jnp.where(first, parts[0], jnp.where(second, parts[1], parts[2]))

    third = ~(first | second)

    def along(d, flux, pressure):
        return flux + jnp.where((first, second, third)[d], pressure, 0.0)

    return choose, along


def mix(left, left_flux, left_wave, right, right_flux, right_wave):
    wave = 0.5 * jnp.maximum(left_wave, right_wave)
    return [
        0.5 * (left_flux[v] + right_flux[v]) - wave * (right[v] - left[v]) for v in range(5)
    ]


def floor_divide(values, divisor):
    return ((values.astype(jnp.float32) + 0.5) * (1.0 / divisor)).astype(jnp.int32)


def table_kernel(parts, capacity, fringes, expand_ref, lanes_ref):
    row = lax.broadcasted_iota(jnp.int32, expand_ref.shape, 0)
    column = lax.broadcasted_iota(jnp.int32, expand_ref.shape, 1) & 15
    point = row & (ROWS - 1)
    point = jnp.where(point >= 25, point - 25, point)
    tens = floor_divide(point, 5)
    wanted = jnp.where(row < ROWS, 5 + tens, 10 + point - 5 * tens)
    expand_ref[...] = jnp.where(column == wanted, 1.0, 0.0).astype(jnp.bfloat16)
    me = lax.axis_index("dom")
    remote = parts * capacity
    row = lax.broadcasted_iota(jnp.int32, (8, LANES), 0)
    lane = lax.broadcasted_iota(jnp.int32, (8, LANES), 1)
    total = jnp.zeros((8, LANES), jnp.int32)
    for d in range(3):
        near = jnp.clip(lane - d * remote, 0, remote - 1)
        away = floor_divide(near, capacity)
        slot = (away ^ me) * capacity + near - away * capacity
        edge = (lane - 3 * remote - d * fringes) & (LANES - 1)
        start = (3 * remote + d * fringes) % LANES
        taken = jnp.clip(lane - d * remote, 0, remote) + jnp.clip(
            lane - start, 0, min(fringes, LANES - start)
        )
        if start + fringes > LANES:
            taken = taken + jnp.clip(lane, 0, start + fringes - LANES)
        other = remote + fringes + lane - taken
        slot = jnp.where(
            in_lanes(lane, d * remote, remote),
            slot,
            jnp.where(edge < fringes, remote + edge, other),
        )
        total = jnp.where(row == d, slot, total)
    lanes_ref[...] = total


def donor_kernel(grids, parts, count, height, *refs):
    states, cell_refs, weight_refs, expand_ref, pay_ref = *(refs[k : k + 2] for k in (0, 2, 4)), *refs[6:8]
    keep_ref, side_ref = refs[8:10]
    outs = refs[10 : 8 + grids]
    cells, weights, planes, values = refs[8 + grids :]
    outer = parts // 2
    side_ref[: outer * height, :] = pay_ref[outer * height :, :]
    span = parts * count
    total = grids * span
    blocks = values.shape[1] - 1
    width = blocks * LANES
    cells[...] = jnp.zeros_like(cells)
    weights[...] = jnp.zeros_like(weights)
    halves = []
    for source in range(2):
        for block in range(-(-total // LANES)):
            lanes = slice(block * LANES, min((block + 1) * LANES, total))
            held = lanes.stop - lanes.start
            cells[source, block, 0:1, :held] = cell_refs[source][:, lanes]
            for k in range(15):
                weights[source, block, k : k + 1, :held] = weight_refs[source][k, :, lanes]
        for v in range(5):
            shifted = states[source][v] - SHIFT[v]
            high = shifted.astype(jnp.bfloat16)
            low = (shifted - high.astype(jnp.float32)).astype(jnp.bfloat16)
            halves.append(jnp.concatenate([high, low], axis=1))
    element = lax.broadcasted_iota(jnp.int32, (LANES, width), 0)
    row = lax.broadcasted_iota(jnp.int32, (8, width), 0)
    lane = lax.broadcasted_iota(jnp.int32, (8, LANES), 1)
    me = lax.axis_index("grid")
    here = lax.axis_index("dom")
    number = 0
    for step in range(0, grids, 2):
        start = partner(me, step) * span
        first = start // LANES
        found = [jnp.zeros((8, LANES), jnp.float32)] * parts
        for source in range(0 if step else 1, 2):
            held = jnp.concatenate([cells[source, first + i] for i in range(blocks)], axis=1)
            chosen = jnp.where(element == held[0:1], 1.0, 0.0).astype(jnp.bfloat16)
            chosen = jnp.concatenate([chosen, chosen], axis=0)
            held = jnp.concatenate([weights[source, first + i] for i in range(blocks)], axis=1)
            high = held.astype(jnp.bfloat16)
            rest = held - high.astype(jnp.float32)
            middle = rest.astype(jnp.bfloat16)
            low = (rest - middle.astype(jnp.float32)).astype(jnp.bfloat16)
            pieces = jnp.concatenate([high, middle, low], axis=0)
            plane = jnp.dot(expand_ref[...], pieces, preferred_element_type=jnp.float32)
            planes[number] = plane[:ROWS] * plane[ROWS:]
            tiles = []
            for top in range(0, LANES, 8):
                a = top // 25
                factor = jnp.broadcast_to(held[a : a + 1], (8, width))
                if top < 25 * (a + 1) < top + 8 and a < 4:
                    later = jnp.broadcast_to(held[a + 1 : a + 2], (8, width))
                    factor = jnp.where(row < 25 * (a + 1) - top, factor, later)
                tiles.append(factor * planes[number, top % 25 : top % 25 + 8, :])
            weight = jnp.concatenate(tiles, axis=0)[:125]
            for v in range(5):
                picked = jnp.dot(
                    halves[5 * source + v], chosen, preferred_element_type=jnp.float32
                )
                value = jnp.sum(picked * weight, axis=0, keepdims=True) + SHIFT[v]
                for block in range(blocks):
                    values[number, block, v : v + 1, :] = value[
                        :, block * LANES : (block + 1) * LANES
                    ]
            place = (step + source - 1) * count
            wanted = in_lanes(lane, place, count)
            for q in range(parts):
                offset = start - first * LANES + partner(here, q) * count
                block = offset // LANES
                index = lane + (offset - block * LANES - place)
                inside = index & (LANES - 1)
                near = lane_gather(values[number, block], inside)
                far = lane_gather(values[number, block + 1], inside)
                found[q] = jnp.where(wanted, jnp.where(index < LANES, near, far), found[q])
            number += 1
        for z in range(outer):
            if step:
                outs[step - 2][z] = found[2 * z]
                outs[step - 1][z] = found[2 * z + 1]
            else:
                keep_ref[z] = found[2 * z]
                side_ref[outer * height + 8 * z : outer * height + 8 * z + 8, :] = found[2 * z + 1]


def face_kernel(
    parts,
    capacity,
    height,
    state_ref,
    plus_ref,
    minus_ref,
    faces_ref,
    lanes_ref,
    slots_ref,
    both_ref,
    pay_ref,
    turn,
):
    remote = parts * capacity
    wide = jnp.concatenate([state_ref[v] - SHIFT[v] for v in range(5)], axis=1)
    face = jnp.dot(
        faces_ref[...], wide, precision=closer, preferred_element_type=jnp.float32
    )
    for side in range(2):
        order = (minus_ref, plus_ref)[side]
        for d in range(3):
            k = 2 * d + side
            index = lane_gather(
                jnp.broadcast_to(order[d : d + 1, :], (ROWS, LANES)),
                jnp.broadcast_to(lanes_ref[d : d + 1, :], (ROWS, LANES)),
            )
            for v in range(5):
                block = face[k * ROWS : (k + 1) * ROWS, v * LANES : (v + 1) * LANES]
                slots_ref[k, v] = lane_gather(block, index) + SHIFT[v]
    lane = lax.broadcasted_iota(jnp.int32, (ROWS, LANES), 1)
    turn[:, 120:128, :] = jnp.zeros((2, 8, LANES), jnp.float32)
    for side in range(2):
        for v in range(5):
            both = jnp.where(
                lane < remote,
                slots_ref[side, v],
                jnp.where(lane < 2 * remote, slots_ref[2 + side, v], slots_ref[4 + side, v]),
            )
            both_ref[side, v] = both
            turn[side, 25 * v : 25 * v + 25, :] = both[:25]
        turned = turn[side].T
        for d in range(3):
            for q in range(parts):
                start = d * remote + q * capacity
                place = (q % 2 * (parts // 2) + q // 2) * height + (2 * d + side) * capacity
                pay_ref[place : place + capacity, :] = turned[start : start + capacity]


def repack_kernel(outer, height, pay_ref, keep_ref, *refs):
    pairs = (len(refs) - outer - 1) // 2
    across, side_ref, straight, outs = refs[:pairs], refs[pairs], refs[pairs + 1 : 2 * pairs + 1], refs[2 * pairs + 1 :]
    for z in range(outer):
        outs[z][:height, :] = pay_ref[z * height : (z + 1) * height, :]
        outs[z][height : 2 * height, :] = side_ref[z * height : (z + 1) * height, :]
        total = keep_ref[z]
        for extra in straight:
            total = total + extra[z]
        outs[z][2 * height : 2 * height + 8, :] = total
        total = side_ref[outer * height + 8 * z : outer * height + 8 * z + 8, :]
        for extra in across:
            total = total + extra[z]
        outs[z][2 * height + 8 : 2 * height + 16, :] = total


def volume_kernel(
    grids,
    parts,
    count,
    remote,
    fringes,
    state_ref,
    size_ref,
    plus_ref,
    minus_ref,
    recv_ref,
    slots_ref,
    both_ref,
    volume_ref,
    lanes_ref,
    points_ref,
    part_ref,
    flux_ref,
    edge_ref,
    local_ref,
    back_ref,
    where_ref,
    wide,
    index,
    received,
):
    state = [state_ref[v] for v in range(5)]
    for d in range(3):
        flux = euler(state, *fixed(d))[0]
        scale = size_ref[d : d + 1, :]
        wide[d * LANES + 120 : (d + 1) * LANES, :] = jnp.zeros((8, 5 * LANES), jnp.float32)
        for v in range(5):
            wide[d * LANES : d * LANES + 125, v * LANES : (v + 1) * LANES] = flux[v] * scale
    part_ref[...] = jnp.dot(
        volume_ref[...], wide[...], precision=closer, preferred_element_type=jnp.float32
    )
    for d in range(3):
        low = [slots_ref[2 * d, v] for v in range(5)]
        high = [slots_ref[2 * d + 1, v] for v in range(5)]
        low_flux, low_wave = euler_wave(low, *fixed(d))
        high_flux, high_wave = euler_wave(high, *fixed(d))
        local = mix(high, high_flux, high_wave, low, low_flux, low_wave)
        for v in range(5):
            local_ref[d, v] = local[v]
    lane = lax.broadcasted_iota(jnp.int32, (ROWS, LANES), 1)
    for side in range(2):
        own = [both_ref[side, v] for v in range(5)]
        flux, wave = euler_wave(own, *by_lane(lane < remote, in_lanes(lane, remote, remote)))
        for v in range(5):
            flux_ref[side, v] = flux[v]
        flux_ref[side, 5] = wave
        second = in_lanes(lane, 3 * remote + fringes, fringes)
        third = in_lanes(lane, 3 * remote + 2 * fringes, fringes)
        edge = [
            jnp.where(
                second,
                slots_ref[2 + side, v],
                jnp.where(third, slots_ref[4 + side, v], slots_ref[side, v]),
            )
            for v in range(5)
        ]
        flux, wave = euler_wave(edge, *by_lane(~(second | third), second))
        for v in range(5):
            edge_ref[side, v] = edge[v]
            edge_ref[side, 5 + v] = flux[v]
        edge_ref[side, 10] = wave
    rank = lax.broadcasted_iota(jnp.int32, (LANES, LANES), 0)
    column = lax.broadcasted_iota(jnp.int32, (LANES, LANES), 1)
    index[...] = jnp.zeros_like(index)
    for k in range(6):
        d = k // 2
        order = lane_gather(
            jnp.broadcast_to((minus_ref, plus_ref)[k % 2][d : d + 1, :], (8, LANES)),
            jnp.broadcast_to(lanes_ref[d : d + 1, :], (8, LANES)),
        )
        index[k : k + 1, :] = order[0:1].astype(jnp.float32)
    turned = index[...].T.astype(jnp.int32)
    back_ref[...] = jnp.zeros_like(back_ref)
    for k in range(6):
        found = jnp.where(turned[:, k : k + 1] == column, rank, 0)
        back_ref[k : k + 1, :] = jnp.sum(found, axis=0, keepdims=True)
    me = lax.axis_index("grid")
    received[...] = jnp.zeros_like(received)
    received[0:1, : recv_ref.shape[1]] = recv_ref[...]
    points = points_ref[...]
    slot = jnp.zeros((8, LANES), jnp.int32)
    for block in range(received.shape[1] // LANES):
        held = jnp.broadcast_to(received[0:1, block * LANES : (block + 1) * LANES], (8, LANES))
        inside = (points >= block * LANES) & (points < (block + 1) * LANES)
        picked = lane_gather(held, jnp.where(inside, points - block * LANES, 0))
        slot = jnp.where(inside, picked, slot)
    device = floor_divide(slot, count)
    rest = slot - device * count
    grid = floor_divide(device, parts)
    step = jnp.zeros_like(grid)
    for g in range(grids):
        away = partner(me, g)
        step = jnp.where(grid == g, away, step)
    where_ref[0] = (device - grid * parts) ^ lax.axis_index("dom")
    where_ref[1] = jnp.maximum(step - 1, 0) * count + rest


def distances(outer):
    return [0, *sorted(range(1, outer), key=lambda z: (z ^ (outer // 2)) % outer)]


def finish_kernel(parts, capacity, height, fringes, *refs):
    come = dict(zip(distances(parts // 2), refs[: parts // 2]))
    both_ref, flux_ref, edge_ref, local_ref, back_ref, where_ref, part_ref, size_ref, lift_ref = refs[
        parts // 2 : parts // 2 + 9
    ]
    out_ref, turn, turned, wide = refs[parts // 2 + 9 :]
    remote = parts * capacity
    row = lax.broadcasted_iota(jnp.int32, (ROWS, LANES), 0)
    lane = lax.broadcasted_iota(jnp.int32, (ROWS, LANES), 1)
    is_remote = [in_lanes(lane, d * remote, remote) for d in range(3)]
    is_fringe = [in_lanes(lane, 3 * remote + d * fringes, fringes) for d in range(3)]
    any_remote = (lane < 3 * remote) & (row < 25)
    any_fringe = is_fringe[0] | is_fringe[1] | is_fringe[2]
    spread = row[:8] * (3 * fringes) + ((lane[:8] - 3 * remote) & (LANES - 1))
    spread = jnp.where(any_fringe[:8], spread, 0)
    for side in range(2):
        for d in range(3):
            for q in range(parts):
                start = d * remote + q * capacity
                place = q % 2 * height + (2 * d + 1 - side) * capacity
                turn[side, start : start + capacity, :] = come[q // 2][place : place + capacity, :]
        turned[side, :LANES, :] = turn[side].T
    fringe = []
    for v in range(5):
        total = jnp.zeros((8, LANES), jnp.float32)
        for q in range(parts):
            place = 2 * height + q % 2 * 8 + v
            sent = come[q // 2][place : place + 1, :]
            picked = lane_gather(jnp.broadcast_to(sent, (8, LANES)), where_ref[1])
            total = jnp.where(where_ref[0] == q, picked, total)
        fringe.append(total)
    for side in range(2):
        own = [both_ref[side, v] for v in range(5)]
        theirs = [
            jnp.where(any_remote, turned[side, 25 * v : 25 * v + ROWS, :], own[v])
            for v in range(5)
        ]
        their = (theirs, *euler_wave(theirs, *by_lane(is_remote[0], is_remote[1])))
        mine = (own, [flux_ref[side, v] for v in range(5)], flux_ref[side, 5])
        common = mix(*mine, *their) if side else mix(*their, *mine)
        own = [edge_ref[side, v] for v in range(5)]
        theirs = []
        for v in range(5):
            pieces = [
                lane_gather(
                    jnp.broadcast_to(fringe[v][side * 4 + r : side * 4 + r + 1], (8, LANES)), spread
                )
                for r in range(4)
            ]
            theirs.append(jnp.where(any_fringe, jnp.concatenate(pieces, axis=0), own[v]))
        their = (theirs, *euler_wave(theirs, *by_lane(~(is_fringe[1] | is_fringe[2]), is_fringe[1])))
        mine = (own, [edge_ref[side, 5 + v] for v in range(5)], edge_ref[side, 10])
        outer = mix(*mine, *their) if side else mix(*their, *mine)
        for d in range(3):
            k = 2 * d + side
            index = jnp.broadcast_to(back_ref[k : k + 1, :], (ROWS, LANES))
            scale = size_ref[d : d + 1, :]
            for v in range(5):
                value = jnp.where(is_fringe[d], outer[v], local_ref[d, v])
                value = jnp.where(is_remote[d], common[v], value)
                wide[k * ROWS : (k + 1) * ROWS, v * LANES : (v + 1) * LANES] = (
                    lane_gather(value, index) * scale
                )
    values = wide[...]
    high = values.astype(jnp.bfloat16)
    low = (values - high.astype(jnp.float32)).astype(jnp.bfloat16)
    first = jnp.dot(lift_ref[...], high, preferred_element_type=jnp.float32)
    second = jnp.dot(lift_ref[:LANES], low, preferred_element_type=jnp.float32)
    total = part_ref[...] + (first[:125] + (first[LANES : LANES + 125] + second[:125]))
    for v in range(5):
        out_ref[v] = total[:, v * LANES : (v + 1) * LANES]


def call(kernel, name, out_shape, scratch, flops, size, *operands, limit=VMEM, **more):
    return pl.pallas_call(
        kernel,
        name=name,
        out_shape=out_shape,
        scratch_shapes=scratch,
        compiler_params=pltpu.CompilerParams(vmem_limit_bytes=limit),
        cost_estimate=pl.CostEstimate(flops=flops, bytes_accessed=size, transcendentals=0),
        **more,
    )(*operands)


def body(state, inv_size, plus_order, minus_order, donor_cell, donor_weights, recv_slot):
    columns = state.shape[-1]
    parts = lax.axis_size("dom")
    grids = lax.axis_size("grid")
    capacity = max(1, columns // (3 * parts))
    remote = parts * capacity
    fringes = recv_slot.shape[-1] // 150
    total = donor_cell.shape[-1]
    count = total // (grids * parts)
    held = -(-recv_slot.shape[-1] // LANES) * LANES
    outer = parts // 2
    height = -(-6 * capacity // 8) * 8
    span = parts * count
    blocks = (2 * (LANES - 1) + span) // LANES
    sets = grids - 1
    held_blocks = -(-total // LANES) + blocks
    faces, volume, lift = matrices()
    lift = np.pad(lift, ((0, LANES - 125), (0, 0)))
    high = lift.astype(ml_dtypes.bfloat16)
    lift = np.concatenate([high, (lift - high.astype(np.float32)).astype(ml_dtypes.bfloat16)])
    points = fringe_lanes(fringes)
    f32 = functools.partial(jax.ShapeDtypeStruct, dtype=jnp.float32)
    i32 = functools.partial(jax.ShapeDtypeStruct, dtype=jnp.int32)
    memory = functools.partial(pltpu.VMEM, dtype=jnp.float32)

    def exchange(values, step, move):
        pairs = [
            (g * parts + q, partner(g, step) * parts + partner(q, move))
            for g in range(grids)
            for q in range(parts)
        ]
        return lax.ppermute(values, ("grid", "dom"), pairs)

    weights = donor_weights.reshape(15, 1, total)
    mates = [exchange(values, 1, 0) for values in (state, donor_cell, weights)]
    expand, lanes = call(
        functools.partial(table_kernel, parts, capacity, fringes),
        "tables",
        (jax.ShapeDtypeStruct((2 * ROWS, 48), jnp.bfloat16), i32((8, LANES))),
        [],
        400_000_000,
        3_000_000,
    )
    slots, both, pay = call(
        functools.partial(face_kernel, parts, capacity, height),
        "faces",
        (
            f32((6, 5, ROWS, LANES)),
            f32((2, 5, ROWS, LANES)),
            f32((parts * height, LANES)),
        ),
        [memory((2, LANES, LANES))],
        200_000_000,
        1_500_000,
        state,
        plus_order,
        minus_order,
        faces,
        lanes,
    )
    keep, side, *sent = call(
        functools.partial(donor_kernel, grids, parts, count, height),
        "donors",
        (
            f32((outer, 8, LANES)),
            f32((outer * (height + 8), LANES)),
            *(f32((outer, 8, LANES)) for _ in range(grids - 2)),
        ),
        [
            pltpu.VMEM((2, held_blocks, 8, LANES), jnp.int32),
            memory((2, held_blocks, 16, LANES)),
            memory((sets, ROWS, blocks * LANES)),
            memory((sets, blocks + 1, 8, LANES)),
        ],
        5_000_000,
        500_000,
        state,
        mates[0],
        donor_cell,
        mates[1],
        weights,
        mates[2],
        expand,
        pay,
    )
    side = exchange(side, 0, 1)
    across = [exchange(sent[k + 1], k + 2, 1) for k in range(0, grids - 2, 2)]
    straight = [exchange(sent[k], k + 2, 0) for k in range(0, grids - 2, 2)]
    packed = call(
        functools.partial(repack_kernel, outer, height),
        "repack",
        tuple(f32((2 * height + 16, LANES)) for _ in range(outer)),
        [],
        50_000,
        200_000,
        pay,
        keep,
        *across,
        side,
        *straight,
    )
    come = [exchange(packed[z], 0, 2 * z) if z else packed[z] for z in distances(outer)]
    part, flux, edge, local, back, where = call(
        functools.partial(volume_kernel, grids, parts, count, remote, fringes),
        "volume",
        (
            f32((125, 5 * LANES)),
            f32((2, 6, ROWS, LANES)),
            f32((2, 11, ROWS, LANES)),
            f32((3, 5, ROWS, LANES)),
            i32((8, LANES)),
            i32((2, 8, LANES)),
        ),
        [
            memory((3 * LANES, 5 * LANES)),
            memory((LANES, LANES)),
            pltpu.VMEM((8, held), jnp.int32),
        ],
        400_000_000,
        3_000_000,
        state,
        inv_size,
        plus_order,
        minus_order,
        recv_slot,
        slots,
        both,
        volume,
        lanes,
        points,
    )
    return call(
        functools.partial(finish_kernel, parts, capacity, height, fringes),
        "finish",
        f32((5, 125, columns)),
        [
            memory((2, LANES, LANES)),
            memory((2, LANES + 8, LANES)),
            memory((6 * ROWS, 5 * LANES)),
        ],
        200_000_000,
        3_000_000,
        *come,
        both,
        flux,
        edge,
        local,
        back,
        where,
        part,
        inv_size,
        lift,
    )


def solution(mesh):
    return jax.shard_map(
        body,
        mesh=mesh,
        in_specs=(
            P(None, None, ("grid", "dom")),
            P(None, ("grid", "dom")),
            P(None, ("grid", "dom")),
            P(None, ("grid", "dom")),
            P(("grid", "dom"), None),
            P(("grid", "dom"), None, None, None),
            P(("grid", "dom"), None),
        ),
        out_specs=P(None, None, ("grid", "dom")),
        check_vma=False,
    )
```

```python
import functools
import math

import jax
import jax.numpy as jnp
import ml_dtypes
import numpy as np
from jax import lax
from jax.experimental import pallas as pl
from jax.experimental.pallas import tpu as pltpu
from jax.sharding import PartitionSpec as P

closer = lax.Precision.HIGH
LANES = 128
SHIFT = (1.0, 0.0, 0.0, 0.0, 2.5)
ROWS = 32
VMEM = 48 * 1024 * 1024


def gauss_nodes():
    outer = math.sqrt(5.0 + 2.0 * math.sqrt(10.0 / 7.0)) / 3.0
    inner = math.sqrt(5.0 - 2.0 * math.sqrt(10.0 / 7.0)) / 3.0
    return [-outer, -inner, 0.0, inner, outer]


def basis_value(nodes, column, target):
    value = 1.0
    for other in range(5):
        if other != column:
            value = value * (target - nodes[other]) / (nodes[column] - nodes[other])
    return value


def basis_slope(nodes, column, target):
    total = 0.0
    for skipped in range(5):
        if skipped != column:
            value = 1.0 / (nodes[column] - nodes[skipped])
            for other in range(5):
                if other != column and other != skipped:
                    value = value * (target - nodes[other]) / (nodes[column] - nodes[other])
            total = total + value
    return total


def legendre_slopes(target):
    values = [1.0, target]
    slopes = [0.0, 1.0]
    for order in range(1, 5):
        values.append(
            ((2 * order + 1) * target * values[order] - order * values[order - 1]) / (order + 1)
        )
        slopes.append(slopes[order - 1] + (2 * order + 1) * values[order])
    return (slopes[4], slopes[5])


def tables():
    nodes = gauss_nodes()
    deriv = [[basis_slope(nodes, column, nodes[row]) for column in range(5)] for row in range(5)]
    lower = [basis_value(nodes, column, -1.0) for column in range(5)]
    upper = [basis_value(nodes, column, 1.0) for column in range(5)]
    lift_low = []
    lift_high = []
    for row in range(5):
        slope_four, slope_five = legendre_slopes(nodes[row])
        lift_low.append(-0.5 * (slope_five - slope_four))
        lift_high.append(0.5 * (slope_five + slope_four))
    return tuple(np.asarray(m, np.float64) for m in (deriv, lower, upper, lift_low, lift_high))


def split_point(point, direction):
    index = [point // 25, point // 5 % 5, point % 5]
    along = index.pop(direction)
    return along, 5 * index[0] + index[1]


def matrices():
    deriv, lower, upper, lift_low, lift_high = tables()
    faces = np.zeros((6 * ROWS, 125))
    volume = np.zeros((125, 3 * LANES))
    lift = np.zeros((125, 6 * ROWS))
    own = deriv - np.outer(lift_low, lower) - np.outer(lift_high, upper)
    for d in range(3):
        for p in range(125):
            i, t = split_point(p, d)
            faces[(2 * d) * ROWS + t, p] = lower[i]
            faces[(2 * d + 1) * ROWS + t, p] = upper[i]
            lift[p, (2 * d) * ROWS + t] = -lift_low[i]
            lift[p, (2 * d + 1) * ROWS + t] = -lift_high[i]
            for other in range(125):
                m, line = split_point(other, d)
                if line == t:
                    volume[p, d * LANES + other] = -own[i, m]
    for k in range(6):
        faces[k * ROWS + 25 : (k + 1) * ROWS] = faces[k * ROWS + 24]
    return tuple(m.astype(np.float32) for m in (faces, volume, lift))


def fringe_lanes(fringes):
    found = np.zeros((8, LANES), np.int32)
    for side in range(2):
        for t in range(ROWS):
            for d in range(3):
                for i in range(fringes):
                    point = ((2 * d + side) * 25 + min(t, 24)) * fringes + i
                    found[side * 4 + t // 8, (t % 8 * 3 + d) * fringes + i] = point
    return found


def partner(index, step):
    return index ^ step


def lane_gather(values, index):
    return jnp.take_along_axis(values, index, axis=1, mode="promise_in_bounds")


def in_lanes(lane, start, width):
    start = start % LANES
    if start + width <= LANES:
        return (lane >= start) & (lane < start + width)
    return (lane >= start) | (lane < start + width - LANES)


def euler(state, choose, along):
    density, momenta, energy = state[0], state[1:4], state[4]
    inverse = 1.0 / density
    normal = choose(momenta)
    speed = normal * inverse
    squares = momenta[0] * momenta[0] + momenta[1] * momenta[1] + momenta[2] * momenta[2]
    pressure = 0.4 * (energy - 0.5 * squares * inverse)
    flux = [normal] + [m * speed for m in momenta] + [(energy + pressure) * speed]
    for d in range(3):
        flux[1 + d] = along(d, flux[1 + d], pressure - 1.0)
    return flux, speed, pressure, inverse


def euler_wave(state, choose, along):
    flux, speed, pressure, inverse = euler(state, choose, along)
    return flux, jnp.abs(speed) + jnp.sqrt(1.4 * pressure * inverse)


def fixed(direction):
    def choose(parts):
        return parts[direction]

    def along(d, flux, pressure):
        return flux + pressure if d == direction else flux

    return choose, along


def by_lane(first, second):
    def choose(parts):
        return jnp.where(first, parts[0], jnp.where(second, parts[1], parts[2]))

    third = ~(first | second)

    def along(d, flux, pressure):
        return flux + jnp.where((first, second, third)[d], pressure, 0.0)

    return choose, along


def mix(left, left_flux, left_wave, right, right_flux, right_wave):
    wave = 0.5 * jnp.maximum(left_wave, right_wave)
    return [
        0.5 * (left_flux[v] + right_flux[v]) - wave * (right[v] - left[v]) for v in range(5)
    ]


def floor_divide(values, divisor):
    return ((values.astype(jnp.float32) + 0.5) * (1.0 / divisor)).astype(jnp.int32)


def table_kernel(parts, capacity, fringes, expand_ref, lanes_ref):
    row = lax.broadcasted_iota(jnp.int32, expand_ref.shape, 0)
    column = lax.broadcasted_iota(jnp.int32, expand_ref.shape, 1) & 15
    point = row & (ROWS - 1)
    point = jnp.where(point >= 25, point - 25, point)
    tens = floor_divide(point, 5)
    wanted = jnp.where(row < ROWS, 5 + tens, 10 + point - 5 * tens)
    expand_ref[...] = jnp.where(column == wanted, 1.0, 0.0).astype(jnp.bfloat16)
    me = lax.axis_index("dom")
    remote = parts * capacity
    row = lax.broadcasted_iota(jnp.int32, (8, LANES), 0)
    lane = lax.broadcasted_iota(jnp.int32, (8, LANES), 1)
    total = jnp.zeros((8, LANES), jnp.int32)
    for d in range(3):
        near = jnp.clip(lane - d * remote, 0, remote - 1)
        away = floor_divide(near, capacity)
        slot = (away ^ me) * capacity + near - away * capacity
        edge = (lane - 3 * remote - d * fringes) & (LANES - 1)
        start = (3 * remote + d * fringes) % LANES
        taken = jnp.clip(lane - d * remote, 0, remote) + jnp.clip(
            lane - start, 0, min(fringes, LANES - start)
        )
        if start + fringes > LANES:
            taken = taken + jnp.clip(lane, 0, start + fringes - LANES)
        other = remote + fringes + lane - taken
        slot = jnp.where(
            in_lanes(lane, d * remote, remote),
            slot,
            jnp.where(edge < fringes, remote + edge, other),
        )
        total = jnp.where(row == d, slot, total)
    lanes_ref[...] = total


def donor_kernel(grids, parts, count, height, *refs):
    states, cell_refs, weight_refs = (refs[k : k + 2] for k in (0, 2, 4))
    expand_ref, pay_ref, keep_ref, side_ref = refs[6:10]
    outs = refs[10 : 8 + grids]
    cells, weights, padded, planes, values = refs[8 + grids :]
    outer = parts // 2
    side_ref[: outer * height, :] = pay_ref[outer * height :, :]
    span = parts * count
    total = grids * span
    blocks = values.shape[1] - 1
    cells[...] = jnp.zeros_like(cells)
    weights[...] = jnp.zeros_like(weights)
    me = lax.axis_index("grid")
    here = lax.axis_index("dom")
    number = 0
    places = []
    for source in range(2):
        for block in range(-(-total // LANES)):
            lanes = slice(block * LANES, min((block + 1) * LANES, total))
            held = lanes.stop - lanes.start
            cells[source, block, 0:1, :held] = cell_refs[source][:, lanes]
            for k in range(15):
                weights[source, block, k : k + 1, :held] = weight_refs[source][k, :, lanes]
        halves = []
        for v in range(5):
            padded[source, v, 120:128, :] = jnp.zeros((8, LANES), jnp.float32)
            padded[source, v, :125, :] = states[source][v] - SHIFT[v]
            shifted = padded[source, v]
            high = shifted.astype(jnp.bfloat16)
            low = (shifted - high.astype(jnp.float32)).astype(jnp.bfloat16)
            halves.append(jnp.concatenate([high, low], axis=1))
        halves = jnp.concatenate(halves, axis=0)
        steps = range(0 if source else 2, grids, 2)
        starts = [partner(me, step) * span for step in steps]
        firsts = [start // LANES for start in starts]
        width = len(steps) * blocks * LANES
        pick = [(source, first + i) for first in firsts for i in range(blocks)]
        held = jnp.concatenate([cells[at] for at in pick], axis=1)
        element = lax.broadcasted_iota(jnp.int32, (LANES, width), 0)
        chosen = jnp.where(element == held[0:1], 1.0, 0.0).astype(jnp.bfloat16)
        chosen = jnp.concatenate([chosen, chosen], axis=0)
        held = jnp.concatenate([weights[at] for at in pick], axis=1)
        high = held.astype(jnp.bfloat16)
        rest = held - high.astype(jnp.float32)
        middle = rest.astype(jnp.bfloat16)
        low = (rest - middle.astype(jnp.float32)).astype(jnp.bfloat16)
        pieces = jnp.concatenate([high, middle, low], axis=0)
        plane = jnp.dot(expand_ref[...], pieces, preferred_element_type=jnp.float32)
        planes[source, :, :width] = plane[:ROWS] * plane[ROWS:]
        row = lax.broadcasted_iota(jnp.int32, (8, width), 0)
        tiles = []
        for top in range(0, LANES, 8):
            a = top // 25
            factor = jnp.broadcast_to(held[a : a + 1], (8, width))
            if a < 4 and 25 * (a + 1) < top + 8:
                later = jnp.broadcast_to(held[a + 1 : a + 2], (8, width))
                factor = jnp.where(row < 25 * (a + 1) - top, factor, later)
            tiles.append(factor * planes[source, top % 25 : top % 25 + 8, :width])
        weight = jnp.concatenate(tiles, axis=0)
        picked = jnp.dot(halves, chosen, preferred_element_type=jnp.float32)
        for v in range(5):
            value = jnp.sum(picked[v * LANES : (v + 1) * LANES] * weight, axis=0, keepdims=True)
            for k in range(len(steps) * blocks):
                values[number + k // blocks, k % blocks, v : v + 1, :] = (
                    value[:, k * LANES : (k + 1) * LANES] + SHIFT[v]
                )
        for step, start, first in zip(steps, starts, firsts):
            places.append((number, step, (step + source - 1) * count, start - first * LANES))
            number += 1
    lane = lax.broadcasted_iota(jnp.int32, (8, LANES), 1)
    found = {}
    for number, step, place, start in places:
        wanted = in_lanes(lane, place, count)
        for q in range(parts):
            offset = start + partner(here, q) * count
            block = offset // LANES
            index = lane + (offset - block * LANES - place)
            inside = index & (LANES - 1)
            near = lane_gather(values[number, block], inside)
            far = lane_gather(values[number, block + 1], inside)
            value = jnp.where(wanted, jnp.where(index < LANES, near, far), 0.0)
            found[step, q] = found[step, q] + value if (step, q) in found else value
    for z in range(outer):
        for step in range(2, grids, 2):
            outs[step - 2][z] = found[step, 2 * z]
            outs[step - 1][z] = found[step, 2 * z + 1]
        keep_ref[z] = found[0, 2 * z]
        side_ref[outer * height + 8 * z : outer * height + 8 * z + 8, :] = found[0, 2 * z + 1]


def face_kernel(
    parts,
    capacity,
    height,
    state_ref,
    plus_ref,
    minus_ref,
    faces_ref,
    lanes_ref,
    slots_ref,
    both_ref,
    pay_ref,
    turn,
):
    remote = parts * capacity
    wide = jnp.concatenate([state_ref[v] - SHIFT[v] for v in range(5)], axis=1)
    face = jnp.dot(
        faces_ref[...], wide, precision=closer, preferred_element_type=jnp.float32
    )
    for side in range(2):
        order = (minus_ref, plus_ref)[side]
        for d in range(3):
            k = 2 * d + side
            index = lane_gather(
                jnp.broadcast_to(order[d : d + 1, :], (ROWS, LANES)),
                jnp.broadcast_to(lanes_ref[d : d + 1, :], (ROWS, LANES)),
            )
            for v in range(5):
                block = face[k * ROWS : (k + 1) * ROWS, v * LANES : (v + 1) * LANES]
                slots_ref[k, v] = lane_gather(block, index) + SHIFT[v]
    lane = lax.broadcasted_iota(jnp.int32, (ROWS, LANES), 1)
    turn[:, 120:128, :] = jnp.zeros((2, 8, LANES), jnp.float32)
    for side in range(2):
        for v in range(5):
            both = jnp.where(
                lane < remote,
                slots_ref[side, v],
                jnp.where(lane < 2 * remote, slots_ref[2 + side, v], slots_ref[4 + side, v]),
            )
            both_ref[side, v] = both
            turn[side, 25 * v : 25 * v + 25, :] = both[:25]
        turned = turn[side].T
        for d in range(3):
            for q in range(parts):
                start = d * remote + q * capacity
                place = (q % 2 * (parts // 2) + q // 2) * height + (2 * d + side) * capacity
                pay_ref[place : place + capacity, :] = turned[start : start + capacity]


def repack_kernel(outer, height, pay_ref, keep_ref, *refs):
    pairs = (len(refs) - outer - 1) // 2
    across, side_ref, straight, outs = refs[:pairs], refs[pairs], refs[pairs + 1 : 2 * pairs + 1], refs[2 * pairs + 1 :]
    for z in range(outer):
        outs[z][:height, :] = pay_ref[z * height : (z + 1) * height, :]
        outs[z][height : 2 * height, :] = side_ref[z * height : (z + 1) * height, :]
        total = keep_ref[z]
        for extra in straight:
            total = total + extra[z]
        outs[z][2 * height : 2 * height + 8, :] = total
        total = side_ref[outer * height + 8 * z : outer * height + 8 * z + 8, :]
        for extra in across:
            total = total + extra[z]
        outs[z][2 * height + 8 : 2 * height + 16, :] = total


def volume_kernel(
    grids,
    parts,
    count,
    remote,
    fringes,
    state_ref,
    size_ref,
    plus_ref,
    minus_ref,
    recv_ref,
    slots_ref,
    both_ref,
    volume_ref,
    lanes_ref,
    points_ref,
    part_ref,
    flux_ref,
    edge_ref,
    local_ref,
    back_ref,
    where_ref,
    wide,
    index,
    received,
):
    state = [state_ref[v] for v in range(5)]
    for d in range(3):
        flux = euler(state, *fixed(d))[0]
        scale = size_ref[d : d + 1, :]
        wide[d * LANES + 120 : (d + 1) * LANES, :] = jnp.zeros((8, 5 * LANES), jnp.float32)
        for v in range(5):
            wide[d * LANES : d * LANES + 125, v * LANES : (v + 1) * LANES] = flux[v] * scale
    part_ref[...] = jnp.dot(
        volume_ref[...], wide[...], precision=closer, preferred_element_type=jnp.float32
    )
    for d in range(3):
        low = [slots_ref[2 * d, v] for v in range(5)]
        high = [slots_ref[2 * d + 1, v] for v in range(5)]
        low_flux, low_wave = euler_wave(low, *fixed(d))
        high_flux, high_wave = euler_wave(high, *fixed(d))
        local = mix(high, high_flux, high_wave, low, low_flux, low_wave)
        for v in range(5):
            local_ref[d, v] = local[v]
    lane = lax.broadcasted_iota(jnp.int32, (ROWS, LANES), 1)
    for side in range(2):
        own = [both_ref[side, v] for v in range(5)]
        flux, wave = euler_wave(own, *by_lane(lane < remote, in_lanes(lane, remote, remote)))
        for v in range(5):
            flux_ref[side, v] = flux[v]
        flux_ref[side, 5] = wave
        second = in_lanes(lane, 3 * remote + fringes, fringes)
        third = in_lanes(lane, 3 * remote + 2 * fringes, fringes)
        edge = [
            jnp.where(
                second,
                slots_ref[2 + side, v],
                jnp.where(third, slots_ref[4 + side, v], slots_ref[side, v]),
            )
            for v in range(5)
        ]
        flux, wave = euler_wave(edge, *by_lane(~(second | third), second))
        for v in range(5):
            edge_ref[side, v] = edge[v]
            edge_ref[side, 5 + v] = flux[v]
        edge_ref[side, 10] = wave
    rank = lax.broadcasted_iota(jnp.int32, (LANES, LANES), 0)
    column = lax.broadcasted_iota(jnp.int32, (LANES, LANES), 1)
    index[...] = jnp.zeros_like(index)
    for k in range(6):
        d = k // 2
        order = lane_gather(
            jnp.broadcast_to((minus_ref, plus_ref)[k % 2][d : d + 1, :], (8, LANES)),
            jnp.broadcast_to(lanes_ref[d : d + 1, :], (8, LANES)),
        )
        index[k : k + 1, :] = order[0:1].astype(jnp.float32)
    turned = index[...].T.astype(jnp.int32)
    back_ref[...] = jnp.zeros_like(back_ref)
    for k in range(6):
        found = jnp.where(turned[:, k : k + 1] == column, rank, 0)
        back_ref[k : k + 1, :] = jnp.sum(found, axis=0, keepdims=True)
    me = lax.axis_index("grid")
    received[...] = jnp.zeros_like(received)
    received[0:1, : recv_ref.shape[1]] = recv_ref[...]
    points = points_ref[...]
    slot = jnp.zeros((8, LANES), jnp.int32)
    for block in range(received.shape[1] // LANES):
        held = jnp.broadcast_to(received[0:1, block * LANES : (block + 1) * LANES], (8, LANES))
        inside = (points >= block * LANES) & (points < (block + 1) * LANES)
        picked = lane_gather(held, jnp.where(inside, points - block * LANES, 0))
        slot = jnp.where(inside, picked, slot)
    device = floor_divide(slot, count)
    rest = slot - device * count
    grid = floor_divide(device, parts)
    step = jnp.zeros_like(grid)
    for g in range(grids):
        away = partner(me, g)
        step = jnp.where(grid == g, away, step)
    where_ref[0] = (device - grid * parts) ^ lax.axis_index("dom")
    where_ref[1] = jnp.maximum(step - 1, 0) * count + rest


def distances(outer):
    return [0, *sorted(range(1, outer), key=lambda z: (z ^ (outer // 2)) % outer)]


def finish_kernel(parts, capacity, height, fringes, *refs):
    come = dict(zip(distances(parts // 2), refs[: parts // 2]))
    both_ref, flux_ref, edge_ref, local_ref, back_ref, where_ref, part_ref, size_ref, lift_ref = refs[
        parts // 2 : parts // 2 + 9
    ]
    out_ref, turn, turned, wide = refs[parts // 2 + 9 :]
    remote = parts * capacity
    row = lax.broadcasted_iota(jnp.int32, (ROWS, LANES), 0)
    lane = lax.broadcasted_iota(jnp.int32, (ROWS, LANES), 1)
    is_remote = [in_lanes(lane, d * remote, remote) for d in range(3)]
    is_fringe = [in_lanes(lane, 3 * remote + d * fringes, fringes) for d in range(3)]
    any_remote = (lane < 3 * remote) & (row < 25)
    any_fringe = is_fringe[0] | is_fringe[1] | is_fringe[2]
    spread = row[:8] * (3 * fringes) + ((lane[:8] - 3 * remote) & (LANES - 1))
    spread = jnp.where(any_fringe[:8], spread, 0)
    for side in range(2):
        for d in range(3):
            for q in range(parts):
                start = d * remote + q * capacity
                place = q % 2 * height + (2 * d + 1 - side) * capacity
                turn[side, start : start + capacity, :] = come[q // 2][place : place + capacity, :]
        turned[side, :LANES, :] = turn[side].T
    fringe = []
    for v in range(5):
        total = jnp.zeros((8, LANES), jnp.float32)
        for q in range(parts):
            place = 2 * height + q % 2 * 8 + v
            sent = come[q // 2][place : place + 1, :]
            picked = lane_gather(jnp.broadcast_to(sent, (8, LANES)), where_ref[1])
            total = jnp.where(where_ref[0] == q, picked, total)
        fringe.append(total)
    for side in range(2):
        own = [both_ref[side, v] for v in range(5)]
        theirs = [
            jnp.where(any_remote, turned[side, 25 * v : 25 * v + ROWS, :], own[v])
            for v in range(5)
        ]
        their = (theirs, *euler_wave(theirs, *by_lane(is_remote[0], is_remote[1])))
        mine = (own, [flux_ref[side, v] for v in range(5)], flux_ref[side, 5])
        common = mix(*mine, *their) if side else mix(*their, *mine)
        own = [edge_ref[side, v] for v in range(5)]
        theirs = []
        for v in range(5):
            pieces = [
                lane_gather(
                    jnp.broadcast_to(fringe[v][side * 4 + r : side * 4 + r + 1], (8, LANES)), spread
                )
                for r in range(4)
            ]
            theirs.append(jnp.where(any_fringe, jnp.concatenate(pieces, axis=0), own[v]))
        their = (theirs, *euler_wave(theirs, *by_lane(~(is_fringe[1] | is_fringe[2]), is_fringe[1])))
        mine = (own, [edge_ref[side, 5 + v] for v in range(5)], edge_ref[side, 10])
        outer = mix(*mine, *their) if side else mix(*their, *mine)
        for d in range(3):
            k = 2 * d + side
            index = jnp.broadcast_to(back_ref[k : k + 1, :], (ROWS, LANES))
            scale = size_ref[d : d + 1, :]
            for v in range(5):
                value = jnp.where(is_fringe[d], outer[v], local_ref[d, v])
                value = jnp.where(is_remote[d], common[v], value)
                wide[k * ROWS : (k + 1) * ROWS, v * LANES : (v + 1) * LANES] = (
                    lane_gather(value, index) * scale
                )
    values = wide[...]
    high = values.astype(jnp.bfloat16)
    low = (values - high.astype(jnp.float32)).astype(jnp.bfloat16)
    first = jnp.dot(lift_ref[...], high, preferred_element_type=jnp.float32)
    second = jnp.dot(lift_ref[:LANES], low, preferred_element_type=jnp.float32)
    total = part_ref[...] + (first[:125] + (first[LANES : LANES + 125] + second[:125]))
    for v in range(5):
        out_ref[v] = total[:, v * LANES : (v + 1) * LANES]


def call(kernel, name, out_shape, scratch, flops, size, *operands, limit=VMEM, **more):
    return pl.pallas_call(
        kernel,
        name=name,
        out_shape=out_shape,
        scratch_shapes=scratch,
        compiler_params=pltpu.CompilerParams(vmem_limit_bytes=limit),
        cost_estimate=pl.CostEstimate(flops=flops, bytes_accessed=size, transcendentals=0),
        **more,
    )(*operands)


def body(state, inv_size, plus_order, minus_order, donor_cell, donor_weights, recv_slot):
    columns = state.shape[-1]
    parts = lax.axis_size("dom")
    grids = lax.axis_size("grid")
    capacity = max(1, columns // (3 * parts))
    remote = parts * capacity
    fringes = recv_slot.shape[-1] // 150
    total = donor_cell.shape[-1]
    count = total // (grids * parts)
    held = -(-recv_slot.shape[-1] // LANES) * LANES
    outer = parts // 2
    height = -(-6 * capacity // 8) * 8
    span = parts * count
    blocks = (2 * (LANES - 1) + span) // LANES
    held_blocks = -(-total // LANES) + blocks
    faces, volume, lift = matrices()
    lift = np.pad(lift, ((0, LANES - 125), (0, 0)))
    high = lift.astype(ml_dtypes.bfloat16)
    lift = np.concatenate([high, (lift - high.astype(np.float32)).astype(ml_dtypes.bfloat16)])
    points = fringe_lanes(fringes)
    f32 = functools.partial(jax.ShapeDtypeStruct, dtype=jnp.float32)
    i32 = functools.partial(jax.ShapeDtypeStruct, dtype=jnp.int32)
    memory = functools.partial(pltpu.VMEM, dtype=jnp.float32)

    def exchange(values, step, move):
        pairs = [
            (g * parts + q, partner(g, step) * parts + partner(q, move))
            for g in range(grids)
            for q in range(parts)
        ]
        return lax.ppermute(values, ("grid", "dom"), pairs)

    weights = donor_weights.reshape(15, 1, total)
    mates = [exchange(values, 1, 0) for values in (state, donor_cell, weights)]
    expand, lanes = call(
        functools.partial(table_kernel, parts, capacity, fringes),
        "tables",
        (jax.ShapeDtypeStruct((2 * ROWS, 48), jnp.bfloat16), i32((8, LANES))),
        [],
        400_000_000,
        3_000_000,
    )
    slots, both, pay = call(
        functools.partial(face_kernel, parts, capacity, height),
        "faces",
        (
            f32((6, 5, ROWS, LANES)),
            f32((2, 5, ROWS, LANES)),
            f32((parts * height, LANES)),
        ),
        [memory((2, LANES, LANES))],
        200_000_000,
        1_500_000,
        state,
        plus_order,
        minus_order,
        faces,
        lanes,
    )
    keep, side, *sent = call(
        functools.partial(donor_kernel, grids, parts, count, height),
        "donors",
        (
            f32((outer, 8, LANES)),
            f32((outer * (height + 8), LANES)),
            *(f32((outer, 8, LANES)) for _ in range(grids - 2)),
        ),
        [
            pltpu.VMEM((2, held_blocks, 8, LANES), jnp.int32),
            memory((2, held_blocks, 16, LANES)),
            memory((2, 5, LANES, LANES)),
            memory((2, ROWS, grids // 2 * blocks * LANES)),
            memory((grids - 1, blocks + 1, 8, LANES)),
        ],
        5_000_000,
        500_000,
        state,
        mates[0],
        donor_cell,
        mates[1],
        weights,
        mates[2],
        expand,
        pay,
    )
    side = exchange(side, 0, 1)
    across = [exchange(sent[k + 1], k + 2, 1) for k in range(0, grids - 2, 2)]
    straight = [exchange(sent[k], k + 2, 0) for k in range(0, grids - 2, 2)]
    packed = call(
        functools.partial(repack_kernel, outer, height),
        "repack",
        tuple(f32((2 * height + 16, LANES)) for _ in range(outer)),
        [],
        50_000,
        200_000,
        pay,
        keep,
        *across,
        side,
        *straight,
    )
    come = [exchange(packed[z], 0, 2 * z) if z else packed[z] for z in distances(outer)]
    part, flux, edge, local, back, where = call(
        functools.partial(volume_kernel, grids, parts, count, remote, fringes),
        "volume",
        (
            f32((125, 5 * LANES)),
            f32((2, 6, ROWS, LANES)),
            f32((2, 11, ROWS, LANES)),
            f32((3, 5, ROWS, LANES)),
            i32((8, LANES)),
            i32((2, 8, LANES)),
        ),
        [
            memory((3 * LANES, 5 * LANES)),
            memory((LANES, LANES)),
            pltpu.VMEM((8, held), jnp.int32),
        ],
        400_000_000,
        3_000_000,
        state,
        inv_size,
        plus_order,
        minus_order,
        recv_slot,
        slots,
        both,
        volume,
        lanes,
        points,
    )
    return call(
        functools.partial(finish_kernel, parts, capacity, height, fringes),
        "finish",
        f32((5, 125, columns)),
        [
            memory((2, LANES, LANES)),
            memory((2, LANES + 8, LANES)),
            memory((6 * ROWS, 5 * LANES)),
        ],
        200_000_000,
        3_000_000,
        *come,
        both,
        flux,
        edge,
        local,
        back,
        where,
        part,
        inv_size,
        lift,
    )


def solution(mesh):
    return jax.shard_map(
        body,
        mesh=mesh,
        in_specs=(
            P(None, None, ("grid", "dom")),
            P(None, ("grid", "dom")),
            P(None, ("grid", "dom")),
            P(None, ("grid", "dom")),
            P(("grid", "dom"), None),
            P(("grid", "dom"), None, None, None),
            P(("grid", "dom"), None),
        ),
        out_specs=P(None, None, ("grid", "dom")),
        check_vma=False,
    )
```

```python
import functools
import math

import jax
import jax.numpy as jnp
import ml_dtypes
import numpy as np
from jax import lax
from jax.experimental import pallas as pl
from jax.experimental.pallas import tpu as pltpu
from jax.sharding import PartitionSpec as P

closer = lax.Precision.HIGH
LANES = 128
SHIFT = (1.0, 0.0, 0.0, 0.0, 2.5)
ROWS = 32
VMEM = 48 * 1024 * 1024


def gauss_nodes():
    outer = math.sqrt(5.0 + 2.0 * math.sqrt(10.0 / 7.0)) / 3.0
    inner = math.sqrt(5.0 - 2.0 * math.sqrt(10.0 / 7.0)) / 3.0
    return [-outer, -inner, 0.0, inner, outer]


def basis_value(nodes, column, target):
    value = 1.0
    for other in range(5):
        if other != column:
            value = value * (target - nodes[other]) / (nodes[column] - nodes[other])
    return value


def basis_slope(nodes, column, target):
    total = 0.0
    for skipped in range(5):
        if skipped != column:
            value = 1.0 / (nodes[column] - nodes[skipped])
            for other in range(5):
                if other != column and other != skipped:
                    value = value * (target - nodes[other]) / (nodes[column] - nodes[other])
            total = total + value
    return total


def legendre_slopes(target):
    values = [1.0, target]
    slopes = [0.0, 1.0]
    for order in range(1, 5):
        values.append(
            ((2 * order + 1) * target * values[order] - order * values[order - 1]) / (order + 1)
        )
        slopes.append(slopes[order - 1] + (2 * order + 1) * values[order])
    return (slopes[4], slopes[5])


def tables():
    nodes = gauss_nodes()
    deriv = [[basis_slope(nodes, column, nodes[row]) for column in range(5)] for row in range(5)]
    lower = [basis_value(nodes, column, -1.0) for column in range(5)]
    upper = [basis_value(nodes, column, 1.0) for column in range(5)]
    lift_low = []
    lift_high = []
    for row in range(5):
        slope_four, slope_five = legendre_slopes(nodes[row])
        lift_low.append(-0.5 * (slope_five - slope_four))
        lift_high.append(0.5 * (slope_five + slope_four))
    return tuple(np.asarray(m, np.float64) for m in (deriv, lower, upper, lift_low, lift_high))


def split_point(point, direction):
    index = [point // 25, point // 5 % 5, point % 5]
    along = index.pop(direction)
    return along, 5 * index[0] + index[1]


def matrices():
    deriv, lower, upper, lift_low, lift_high = tables()
    faces = np.zeros((6 * ROWS, 125))
    volume = np.zeros((125, 3 * LANES))
    lift = np.zeros((125, 6 * ROWS))
    own = deriv - np.outer(lift_low, lower) - np.outer(lift_high, upper)
    for d in range(3):
        for p in range(125):
            i, t = split_point(p, d)
            faces[(2 * d) * ROWS + t, p] = lower[i]
            faces[(2 * d + 1) * ROWS + t, p] = upper[i]
            lift[p, (2 * d) * ROWS + t] = -lift_low[i]
            lift[p, (2 * d + 1) * ROWS + t] = -lift_high[i]
            for other in range(125):
                m, line = split_point(other, d)
                if line == t:
                    volume[p, d * LANES + other] = -own[i, m]
    for k in range(6):
        faces[k * ROWS + 25 : (k + 1) * ROWS] = faces[k * ROWS + 24]
    return tuple(m.astype(np.float32) for m in (faces, volume, lift))


def fringe_lanes(fringes):
    found = np.zeros((8, LANES), np.int32)
    for side in range(2):
        for t in range(ROWS):
            for d in range(3):
                for i in range(fringes):
                    point = ((2 * d + side) * 25 + min(t, 24)) * fringes + i
                    found[side * 4 + t // 8, (t % 8 * 3 + d) * fringes + i] = point
    return found


def partner(index, step):
    return index ^ step


def lane_gather(values, index):
    return jnp.take_along_axis(values, index, axis=1, mode="promise_in_bounds")


def in_lanes(lane, start, width):
    start = start % LANES
    if start + width <= LANES:
        return (lane >= start) & (lane < start + width)
    return (lane >= start) | (lane < start + width - LANES)


def euler(state, choose, along):
    density, momenta, energy = state[0], state[1:4], state[4]
    inverse = 1.0 / density
    normal = choose(momenta)
    speed = normal * inverse
    squares = momenta[0] * momenta[0] + momenta[1] * momenta[1] + momenta[2] * momenta[2]
    pressure = 0.4 * (energy - 0.5 * squares * inverse)
    flux = [normal] + [m * speed for m in momenta] + [(energy + pressure) * speed]
    for d in range(3):
        flux[1 + d] = along(d, flux[1 + d], pressure - 1.0)
    return flux, speed, pressure, inverse


def euler_wave(state, choose, along):
    flux, speed, pressure, inverse = euler(state, choose, along)
    return flux, jnp.abs(speed) + jnp.sqrt(1.4 * pressure * inverse)


def fixed(direction):
    def choose(parts):
        return parts[direction]

    def along(d, flux, pressure):
        return flux + pressure if d == direction else flux

    return choose, along


def by_lane(first, second):
    def choose(parts):
        return jnp.where(first, parts[0], jnp.where(second, parts[1], parts[2]))

    third = ~(first | second)

    def along(d, flux, pressure):
        return flux + jnp.where((first, second, third)[d], pressure, 0.0)

    return choose, along


def mix(left, left_flux, left_wave, right, right_flux, right_wave):
    wave = 0.5 * jnp.maximum(left_wave, right_wave)
    return [
        0.5 * (left_flux[v] + right_flux[v]) - wave * (right[v] - left[v]) for v in range(5)
    ]


def floor_divide(values, divisor):
    return ((values.astype(jnp.float32) + 0.5) * (1.0 / divisor)).astype(jnp.int32)


def table_kernel(parts, capacity, fringes, expand_ref, lanes_ref):
    row = lax.broadcasted_iota(jnp.int32, expand_ref.shape, 0)
    column = lax.broadcasted_iota(jnp.int32, expand_ref.shape, 1) & 15
    point = row & (ROWS - 1)
    point = jnp.where(point >= 25, point - 25, point)
    tens = floor_divide(point, 5)
    wanted = jnp.where(row < ROWS, 5 + tens, 10 + point - 5 * tens)
    expand_ref[...] = jnp.where(column == wanted, 1.0, 0.0).astype(jnp.bfloat16)
    me = lax.axis_index("dom")
    remote = parts * capacity
    row = lax.broadcasted_iota(jnp.int32, (8, LANES), 0)
    lane = lax.broadcasted_iota(jnp.int32, (8, LANES), 1)
    total = jnp.zeros((8, LANES), jnp.int32)
    for d in range(3):
        near = jnp.clip(lane - d * remote, 0, remote - 1)
        away = floor_divide(near, capacity)
        slot = (away ^ me) * capacity + near - away * capacity
        edge = (lane - 3 * remote - d * fringes) & (LANES - 1)
        start = (3 * remote + d * fringes) % LANES
        taken = jnp.clip(lane - d * remote, 0, remote) + jnp.clip(
            lane - start, 0, min(fringes, LANES - start)
        )
        if start + fringes > LANES:
            taken = taken + jnp.clip(lane, 0, start + fringes - LANES)
        other = remote + fringes + lane - taken
        slot = jnp.where(
            in_lanes(lane, d * remote, remote),
            slot,
            jnp.where(edge < fringes, remote + edge, other),
        )
        total = jnp.where(row == d, slot, total)
    lanes_ref[...] = total


def donor_kernel(grids, parts, count, height, *refs):
    weight_refs, cell_refs, states = (refs[k : k + 2] for k in (0, 2, 4))
    expand_ref, pay_ref, keep_ref, side_ref = refs[6:10]
    outs = refs[10 : 8 + grids]
    cells, weights, padded, planes, values = refs[8 + grids :]
    outer = parts // 2
    side_ref[: outer * height, :] = pay_ref[outer * height :, :]
    span = parts * count
    total = grids * span
    blocks = values.shape[1] - 1
    cells[...] = jnp.zeros_like(cells)
    weights[...] = jnp.zeros_like(weights)
    me = lax.axis_index("grid")
    here = lax.axis_index("dom")
    number = 0
    places = []
    for source in range(2):
        for block in range(-(-total // LANES)):
            lanes = slice(block * LANES, min((block + 1) * LANES, total))
            held = lanes.stop - lanes.start
            cells[source, block, 0:1, :held] = cell_refs[source][:, lanes]
            for k in range(15):
                weights[source, block, k : k + 1, :held] = weight_refs[source][k, :, lanes]
        halves = []
        for v in range(5):
            padded[source, v, 120:128, :] = jnp.zeros((8, LANES), jnp.float32)
            padded[source, v, :125, :] = states[source][v] - SHIFT[v]
            shifted = padded[source, v]
            high = shifted.astype(jnp.bfloat16)
            low = (shifted - high.astype(jnp.float32)).astype(jnp.bfloat16)
            halves.append(jnp.concatenate([high, low], axis=1))
        halves = jnp.concatenate(halves, axis=0)
        steps = range(0 if source else 2, grids, 2)
        starts = [partner(me, step) * span for step in steps]
        firsts = [start // LANES for start in starts]
        width = len(steps) * blocks * LANES
        pick = [(source, first + i) for first in firsts for i in range(blocks)]
        held = jnp.concatenate([cells[at] for at in pick], axis=1)
        element = lax.broadcasted_iota(jnp.int32, (LANES, width), 0)
        chosen = jnp.where(element == held[0:1], 1.0, 0.0).astype(jnp.bfloat16)
        chosen = jnp.concatenate([chosen, chosen], axis=0)
        held = jnp.concatenate([weights[at] for at in pick], axis=1)
        high = held.astype(jnp.bfloat16)
        rest = held - high.astype(jnp.float32)
        middle = rest.astype(jnp.bfloat16)
        low = (rest - middle.astype(jnp.float32)).astype(jnp.bfloat16)
        pieces = jnp.concatenate([high, middle, low], axis=0)
        plane = jnp.dot(expand_ref[...], pieces, preferred_element_type=jnp.float32)
        planes[source, :, :width] = plane[:ROWS] * plane[ROWS:]
        row = lax.broadcasted_iota(jnp.int32, (8, width), 0)
        tiles = []
        for top in range(0, LANES, 8):
            a = top // 25
            factor = jnp.broadcast_to(held[a : a + 1], (8, width))
            if a < 4 and 25 * (a + 1) < top + 8:
                later = jnp.broadcast_to(held[a + 1 : a + 2], (8, width))
                factor = jnp.where(row < 25 * (a + 1) - top, factor, later)
            tiles.append(factor * planes[source, top % 25 : top % 25 + 8, :width])
        weight = jnp.concatenate(tiles, axis=0)
        picked = jnp.dot(halves, chosen, preferred_element_type=jnp.float32)
        for v in range(5):
            value = jnp.sum(picked[v * LANES : (v + 1) * LANES] * weight, axis=0, keepdims=True)
            for k in range(len(steps) * blocks):
                values[number + k // blocks, k % blocks, v : v + 1, :] = (
                    value[:, k * LANES : (k + 1) * LANES] + SHIFT[v]
                )
        for step, start, first in zip(steps, starts, firsts):
            places.append((number, step, (step + source - 1) * count, start - first * LANES))
            number += 1
    lane = lax.broadcasted_iota(jnp.int32, (8, LANES), 1)
    found = {}
    for number, step, place, start in places:
        wanted = in_lanes(lane, place, count)
        for q in range(parts):
            offset = start + partner(here, q) * count
            block = offset // LANES
            index = lane + (offset - block * LANES - place)
            inside = index & (LANES - 1)
            near = lane_gather(values[number, block], inside)
            far = lane_gather(values[number, block + 1], inside)
            value = jnp.where(wanted, jnp.where(index < LANES, near, far), 0.0)
            found[step, q] = found[step, q] + value if (step, q) in found else value
    for z in range(outer):
        for step in range(2, grids, 2):
            outs[step - 2][z] = found[step, 2 * z]
            outs[step - 1][z] = found[step, 2 * z + 1]
        keep_ref[z] = found[0, 2 * z]
        side_ref[outer * height + 8 * z : outer * height + 8 * z + 8, :] = found[0, 2 * z + 1]


def face_kernel(
    parts,
    capacity,
    height,
    state_ref,
    plus_ref,
    minus_ref,
    faces_ref,
    lanes_ref,
    slots_ref,
    both_ref,
    pay_ref,
    turn,
):
    remote = parts * capacity
    wide = jnp.concatenate([state_ref[v] - SHIFT[v] for v in range(5)], axis=1)
    face = jnp.dot(
        faces_ref[...], wide, precision=closer, preferred_element_type=jnp.float32
    )
    for side in range(2):
        order = (minus_ref, plus_ref)[side]
        for d in range(3):
            k = 2 * d + side
            index = lane_gather(
                jnp.broadcast_to(order[d : d + 1, :], (ROWS, LANES)),
                jnp.broadcast_to(lanes_ref[d : d + 1, :], (ROWS, LANES)),
            )
            for v in range(5):
                block = face[k * ROWS : (k + 1) * ROWS, v * LANES : (v + 1) * LANES]
                slots_ref[k, v] = lane_gather(block, index) + SHIFT[v]
    lane = lax.broadcasted_iota(jnp.int32, (ROWS, LANES), 1)
    turn[:, 120:128, :] = jnp.zeros((2, 8, LANES), jnp.float32)
    for side in range(2):
        for v in range(5):
            both = jnp.where(
                lane < remote,
                slots_ref[side, v],
                jnp.where(lane < 2 * remote, slots_ref[2 + side, v], slots_ref[4 + side, v]),
            )
            both_ref[side, v] = both
            turn[side, 25 * v : 25 * v + 25, :] = both[:25]
        turned = turn[side].T
        for d in range(3):
            for q in range(parts):
                start = d * remote + q * capacity
                place = (q % 2 * (parts // 2) + q // 2) * height + (2 * d + side) * capacity
                pay_ref[place : place + capacity, :] = turned[start : start + capacity]


def repack_kernel(outer, height, pay_ref, keep_ref, *refs):
    pairs = (len(refs) - outer - 1) // 2
    across, side_ref, straight, outs = refs[:pairs], refs[pairs], refs[pairs + 1 : 2 * pairs + 1], refs[2 * pairs + 1 :]
    for z in range(outer):
        outs[z][:height, :] = pay_ref[z * height : (z + 1) * height, :]
        outs[z][height : 2 * height, :] = side_ref[z * height : (z + 1) * height, :]
        total = keep_ref[z]
        for extra in straight:
            total = total + extra[z]
        outs[z][2 * height : 2 * height + 8, :] = total
        total = side_ref[outer * height + 8 * z : outer * height + 8 * z + 8, :]
        for extra in across:
            total = total + extra[z]
        outs[z][2 * height + 8 : 2 * height + 16, :] = total


def volume_kernel(
    grids,
    parts,
    count,
    remote,
    fringes,
    state_ref,
    size_ref,
    plus_ref,
    minus_ref,
    recv_ref,
    slots_ref,
    both_ref,
    volume_ref,
    lanes_ref,
    points_ref,
    part_ref,
    flux_ref,
    edge_ref,
    local_ref,
    back_ref,
    where_ref,
    wide,
    index,
    received,
):
    state = [state_ref[v] for v in range(5)]
    for d in range(3):
        flux = euler(state, *fixed(d))[0]
        scale = size_ref[d : d + 1, :]
        wide[d * LANES + 120 : (d + 1) * LANES, :] = jnp.zeros((8, 5 * LANES), jnp.float32)
        for v in range(5):
            wide[d * LANES : d * LANES + 125, v * LANES : (v + 1) * LANES] = flux[v] * scale
    part_ref[...] = jnp.dot(
        volume_ref[...], wide[...], precision=closer, preferred_element_type=jnp.float32
    )
    for d in range(3):
        low = [slots_ref[2 * d, v] for v in range(5)]
        high = [slots_ref[2 * d + 1, v] for v in range(5)]
        low_flux, low_wave = euler_wave(low, *fixed(d))
        high_flux, high_wave = euler_wave(high, *fixed(d))
        local = mix(high, high_flux, high_wave, low, low_flux, low_wave)
        for v in range(5):
            local_ref[d, v] = local[v]
    lane = lax.broadcasted_iota(jnp.int32, (ROWS, LANES), 1)
    for side in range(2):
        own = [both_ref[side, v] for v in range(5)]
        flux, wave = euler_wave(own, *by_lane(lane < remote, in_lanes(lane, remote, remote)))
        for v in range(5):
            flux_ref[side, v] = flux[v]
        flux_ref[side, 5] = wave
        second = in_lanes(lane, 3 * remote + fringes, fringes)
        third = in_lanes(lane, 3 * remote + 2 * fringes, fringes)
        edge = [
            jnp.where(
                second,
                slots_ref[2 + side, v],
                jnp.where(third, slots_ref[4 + side, v], slots_ref[side, v]),
            )
            for v in range(5)
        ]
        flux, wave = euler_wave(edge, *by_lane(~(second | third), second))
        for v in range(5):
            edge_ref[side, v] = edge[v]
            edge_ref[side, 5 + v] = flux[v]
        edge_ref[side, 10] = wave
    rank = lax.broadcasted_iota(jnp.int32, (LANES, LANES), 0)
    column = lax.broadcasted_iota(jnp.int32, (LANES, LANES), 1)
    index[...] = jnp.zeros_like(index)
    for k in range(6):
        d = k // 2
        order = lane_gather(
            jnp.broadcast_to((minus_ref, plus_ref)[k % 2][d : d + 1, :], (8, LANES)),
            jnp.broadcast_to(lanes_ref[d : d + 1, :], (8, LANES)),
        )
        index[k : k + 1, :] = order[0:1].astype(jnp.float32)
    turned = index[...].T.astype(jnp.int32)
    back_ref[...] = jnp.zeros_like(back_ref)
    for k in range(6):
        found = jnp.where(turned[:, k : k + 1] == column, rank, 0)
        back_ref[k : k + 1, :] = jnp.sum(found, axis=0, keepdims=True)
    me = lax.axis_index("grid")
    received[...] = jnp.zeros_like(received)
    received[0:1, : recv_ref.shape[1]] = recv_ref[...]
    points = points_ref[...]
    slot = jnp.zeros((8, LANES), jnp.int32)
    for block in range(received.shape[1] // LANES):
        held = jnp.broadcast_to(received[0:1, block * LANES : (block + 1) * LANES], (8, LANES))
        inside = (points >= block * LANES) & (points < (block + 1) * LANES)
        picked = lane_gather(held, jnp.where(inside, points - block * LANES, 0))
        slot = jnp.where(inside, picked, slot)
    device = floor_divide(slot, count)
    rest = slot - device * count
    grid = floor_divide(device, parts)
    step = jnp.zeros_like(grid)
    for g in range(grids):
        away = partner(me, g)
        step = jnp.where(grid == g, away, step)
    where_ref[0] = (device - grid * parts) ^ lax.axis_index("dom")
    where_ref[1] = jnp.maximum(step - 1, 0) * count + rest


def distances(outer):
    return [0, *sorted(range(1, outer), key=lambda z: (z ^ (outer // 2)) % outer)]


def finish_kernel(parts, capacity, height, fringes, *refs):
    come = dict(zip(distances(parts // 2), refs[: parts // 2]))
    both_ref, flux_ref, edge_ref, local_ref, back_ref, where_ref, part_ref, size_ref, lift_ref = refs[
        parts // 2 : parts // 2 + 9
    ]
    out_ref, turn, turned, wide = refs[parts // 2 + 9 :]
    remote = parts * capacity
    row = lax.broadcasted_iota(jnp.int32, (ROWS, LANES), 0)
    lane = lax.broadcasted_iota(jnp.int32, (ROWS, LANES), 1)
    is_remote = [in_lanes(lane, d * remote, remote) for d in range(3)]
    is_fringe = [in_lanes(lane, 3 * remote + d * fringes, fringes) for d in range(3)]
    any_remote = (lane < 3 * remote) & (row < 25)
    any_fringe = is_fringe[0] | is_fringe[1] | is_fringe[2]
    spread = row[:8] * (3 * fringes) + ((lane[:8] - 3 * remote) & (LANES - 1))
    spread = jnp.where(any_fringe[:8], spread, 0)
    for side in range(2):
        for d in range(3):
            for q in range(parts):
                start = d * remote + q * capacity
                place = q % 2 * height + (2 * d + 1 - side) * capacity
                turn[side, start : start + capacity, :] = come[q // 2][place : place + capacity, :]
        turned[side, :LANES, :] = turn[side].T
    fringe = []
    for v in range(5):
        total = jnp.zeros((8, LANES), jnp.float32)
        for q in range(parts):
            place = 2 * height + q % 2 * 8 + v
            sent = come[q // 2][place : place + 1, :]
            picked = lane_gather(jnp.broadcast_to(sent, (8, LANES)), where_ref[1])
            total = jnp.where(where_ref[0] == q, picked, total)
        fringe.append(total)
    for side in range(2):
        own = [both_ref[side, v] for v in range(5)]
        theirs = [
            jnp.where(any_remote, turned[side, 25 * v : 25 * v + ROWS, :], own[v])
            for v in range(5)
        ]
        their = (theirs, *euler_wave(theirs, *by_lane(is_remote[0], is_remote[1])))
        mine = (own, [flux_ref[side, v] for v in range(5)], flux_ref[side, 5])
        common = mix(*mine, *their) if side else mix(*their, *mine)
        own = [edge_ref[side, v] for v in range(5)]
        theirs = []
        for v in range(5):
            pieces = [
                lane_gather(
                    jnp.broadcast_to(fringe[v][side * 4 + r : side * 4 + r + 1], (8, LANES)), spread
                )
                for r in range(4)
            ]
            theirs.append(jnp.where(any_fringe, jnp.concatenate(pieces, axis=0), own[v]))
        their = (theirs, *euler_wave(theirs, *by_lane(~(is_fringe[1] | is_fringe[2]), is_fringe[1])))
        mine = (own, [edge_ref[side, 5 + v] for v in range(5)], edge_ref[side, 10])
        outer = mix(*mine, *their) if side else mix(*their, *mine)
        for d in range(3):
            k = 2 * d + side
            index = jnp.broadcast_to(back_ref[k : k + 1, :], (ROWS, LANES))
            scale = size_ref[d : d + 1, :]
            for v in range(5):
                value = jnp.where(is_fringe[d], outer[v], local_ref[d, v])
                value = jnp.where(is_remote[d], common[v], value)
                wide[k * ROWS : (k + 1) * ROWS, v * LANES : (v + 1) * LANES] = (
                    lane_gather(value, index) * scale
                )
    values = wide[...]
    high = values.astype(jnp.bfloat16)
    low = (values - high.astype(jnp.float32)).astype(jnp.bfloat16)
    first = jnp.dot(lift_ref[...], high, preferred_element_type=jnp.float32)
    second = jnp.dot(lift_ref[:LANES], low, preferred_element_type=jnp.float32)
    total = part_ref[...] + (first[:125] + (first[LANES : LANES + 125] + second[:125]))
    for v in range(5):
        out_ref[v] = total[:, v * LANES : (v + 1) * LANES]


def call(kernel, name, out_shape, scratch, flops, size, *operands, limit=VMEM, **more):
    return pl.pallas_call(
        kernel,
        name=name,
        out_shape=out_shape,
        scratch_shapes=scratch,
        compiler_params=pltpu.CompilerParams(vmem_limit_bytes=limit),
        cost_estimate=pl.CostEstimate(flops=flops, bytes_accessed=size, transcendentals=0),
        **more,
    )(*operands)


def body(state, inv_size, plus_order, minus_order, donor_cell, donor_weights, recv_slot):
    columns = state.shape[-1]
    parts = lax.axis_size("dom")
    grids = lax.axis_size("grid")
    capacity = max(1, columns // (3 * parts))
    remote = parts * capacity
    fringes = recv_slot.shape[-1] // 150
    total = donor_cell.shape[-1]
    count = total // (grids * parts)
    held = -(-recv_slot.shape[-1] // LANES) * LANES
    outer = parts // 2
    height = -(-6 * capacity // 8) * 8
    span = parts * count
    blocks = (2 * (LANES - 1) + span) // LANES
    held_blocks = -(-total // LANES) + blocks
    faces, volume, lift = matrices()
    lift = np.pad(lift, ((0, LANES - 125), (0, 0)))
    high = lift.astype(ml_dtypes.bfloat16)
    lift = np.concatenate([high, (lift - high.astype(np.float32)).astype(ml_dtypes.bfloat16)])
    points = fringe_lanes(fringes)
    f32 = functools.partial(jax.ShapeDtypeStruct, dtype=jnp.float32)
    i32 = functools.partial(jax.ShapeDtypeStruct, dtype=jnp.int32)
    memory = functools.partial(pltpu.VMEM, dtype=jnp.float32)

    def exchange(values, step, move):
        pairs = [
            (g * parts + q, partner(g, step) * parts + partner(q, move))
            for g in range(grids)
            for q in range(parts)
        ]
        return lax.ppermute(values, ("grid", "dom"), pairs)

    weights = donor_weights.reshape(15, 1, total)
    mates = [exchange(values, 1, 0) for values in (state, donor_cell, weights)]
    expand, lanes = call(
        functools.partial(table_kernel, parts, capacity, fringes),
        "tables",
        (jax.ShapeDtypeStruct((2 * ROWS, 48), jnp.bfloat16), i32((8, LANES))),
        [],
        400_000_000,
        3_000_000,
    )
    slots, both, pay = call(
        functools.partial(face_kernel, parts, capacity, height),
        "faces",
        (
            f32((6, 5, ROWS, LANES)),
            f32((2, 5, ROWS, LANES)),
            f32((parts * height, LANES)),
        ),
        [memory((2, LANES, LANES))],
        200_000_000,
        1_500_000,
        state,
        plus_order,
        minus_order,
        faces,
        lanes,
    )
    keep, side, *sent = call(
        functools.partial(donor_kernel, grids, parts, count, height),
        "donors",
        (
            f32((outer, 8, LANES)),
            f32((outer * (height + 8), LANES)),
            *(f32((outer, 8, LANES)) for _ in range(grids - 2)),
        ),
        [
            pltpu.VMEM((2, held_blocks, 8, LANES), jnp.int32),
            memory((2, held_blocks, 16, LANES)),
            memory((2, 5, LANES, LANES)),
            memory((2, ROWS, grids // 2 * blocks * LANES)),
            memory((grids - 1, blocks + 1, 8, LANES)),
        ],
        5_000_000,
        500_000,
        weights,
        mates[2],
        donor_cell,
        mates[1],
        state,
        mates[0],
        expand,
        pay,
    )
    side = exchange(side, 0, 1)
    across = [exchange(sent[k + 1], k + 2, 1) for k in range(0, grids - 2, 2)]
    straight = [exchange(sent[k], k + 2, 0) for k in range(0, grids - 2, 2)]
    packed = call(
        functools.partial(repack_kernel, outer, height),
        "repack",
        tuple(f32((2 * height + 16, LANES)) for _ in range(outer)),
        [],
        50_000,
        200_000,
        pay,
        keep,
        *across,
        side,
        *straight,
    )
    come = [exchange(packed[z], 0, 2 * z) if z else packed[z] for z in distances(outer)]
    part, flux, edge, local, back, where = call(
        functools.partial(volume_kernel, grids, parts, count, remote, fringes),
        "volume",
        (
            f32((125, 5 * LANES)),
            f32((2, 6, ROWS, LANES)),
            f32((2, 11, ROWS, LANES)),
            f32((3, 5, ROWS, LANES)),
            i32((8, LANES)),
            i32((2, 8, LANES)),
        ),
        [
            memory((3 * LANES, 5 * LANES)),
            memory((LANES, LANES)),
            pltpu.VMEM((8, held), jnp.int32),
        ],
        400_000_000,
        3_000_000,
        state,
        inv_size,
        plus_order,
        minus_order,
        recv_slot,
        slots,
        both,
        volume,
        lanes,
        points,
    )
    return call(
        functools.partial(finish_kernel, parts, capacity, height, fringes),
        "finish",
        f32((5, 125, columns)),
        [
            memory((2, LANES, LANES)),
            memory((2, LANES + 8, LANES)),
            memory((6 * ROWS, 5 * LANES)),
        ],
        200_000_000,
        3_000_000,
        *come,
        both,
        flux,
        edge,
        local,
        back,
        where,
        part,
        inv_size,
        lift,
    )


def solution(mesh):
    return jax.shard_map(
        body,
        mesh=mesh,
        in_specs=(
            P(None, None, ("grid", "dom")),
            P(None, ("grid", "dom")),
            P(None, ("grid", "dom")),
            P(None, ("grid", "dom")),
            P(("grid", "dom"), None),
            P(("grid", "dom"), None, None, None),
            P(("grid", "dom"), None),
        ),
        out_specs=P(None, None, ("grid", "dom")),
        check_vma=False,
    )
```

```python
import functools
import math

import jax
import jax.numpy as jnp
import ml_dtypes
import numpy as np
from jax import lax
from jax.experimental import pallas as pl
from jax.experimental.pallas import tpu as pltpu
from jax.sharding import PartitionSpec as P

closer = lax.Precision.HIGH
LANES = 128
SHIFT = (1.0, 0.0, 0.0, 0.0, 2.5)
ROWS = 32
VMEM = 24 * 1024 * 1024


def gauss_nodes():
    outer = math.sqrt(5.0 + 2.0 * math.sqrt(10.0 / 7.0)) / 3.0
    inner = math.sqrt(5.0 - 2.0 * math.sqrt(10.0 / 7.0)) / 3.0
    return [-outer, -inner, 0.0, inner, outer]


def basis_value(nodes, column, target):
    value = 1.0
    for other in range(5):
        if other != column:
            value = value * (target - nodes[other]) / (nodes[column] - nodes[other])
    return value


def basis_slope(nodes, column, target):
    total = 0.0
    for skipped in range(5):
        if skipped != column:
            value = 1.0 / (nodes[column] - nodes[skipped])
            for other in range(5):
                if other != column and other != skipped:
                    value = value * (target - nodes[other]) / (nodes[column] - nodes[other])
            total = total + value
    return total


def legendre_slopes(target):
    values = [1.0, target]
    slopes = [0.0, 1.0]
    for order in range(1, 5):
        values.append(
            ((2 * order + 1) * target * values[order] - order * values[order - 1]) / (order + 1)
        )
        slopes.append(slopes[order - 1] + (2 * order + 1) * values[order])
    return (slopes[4], slopes[5])


def tables():
    nodes = gauss_nodes()
    deriv = [[basis_slope(nodes, column, nodes[row]) for column in range(5)] for row in range(5)]
    lower = [basis_value(nodes, column, -1.0) for column in range(5)]
    upper = [basis_value(nodes, column, 1.0) for column in range(5)]
    lift_low = []
    lift_high = []
    for row in range(5):
        slope_four, slope_five = legendre_slopes(nodes[row])
        lift_low.append(-0.5 * (slope_five - slope_four))
        lift_high.append(0.5 * (slope_five + slope_four))
    return tuple(np.asarray(m, np.float64) for m in (deriv, lower, upper, lift_low, lift_high))


def split_point(point, direction):
    index = [point // 25, point // 5 % 5, point % 5]
    along = index.pop(direction)
    return along, 5 * index[0] + index[1]


def matrices():
    deriv, lower, upper, lift_low, lift_high = tables()
    faces = np.zeros((6 * ROWS, 125))
    volume = np.zeros((125, 3 * LANES))
    lift = np.zeros((125, 6 * ROWS))
    own = deriv - np.outer(lift_low, lower) - np.outer(lift_high, upper)
    for d in range(3):
        for p in range(125):
            i, t = split_point(p, d)
            faces[(2 * d) * ROWS + t, p] = lower[i]
            faces[(2 * d + 1) * ROWS + t, p] = upper[i]
            lift[p, (2 * d) * ROWS + t] = -lift_low[i]
            lift[p, (2 * d + 1) * ROWS + t] = -lift_high[i]
            for other in range(125):
                m, line = split_point(other, d)
                if line == t:
                    volume[p, d * LANES + other] = -own[i, m]
    for k in range(6):
        faces[k * ROWS + 25 : (k + 1) * ROWS] = faces[k * ROWS + 24]
    return tuple(m.astype(np.float32) for m in (faces, volume, lift))


def fringe_lanes(fringes):
    found = np.zeros((8, LANES), np.int32)
    for side in range(2):
        for t in range(ROWS):
            for d in range(3):
                for i in range(fringes):
                    point = ((2 * d + side) * 25 + min(t, 24)) * fringes + i
                    found[side * 4 + t // 8, (t % 8 * 3 + d) * fringes + i] = point
    return found


def partner(index, step):
    return index ^ step


def lane_gather(values, index):
    return jnp.take_along_axis(values, index, axis=1, mode="promise_in_bounds")


def in_lanes(lane, start, width):
    start = start % LANES
    if start + width <= LANES:
        return (lane >= start) & (lane < start + width)
    return (lane >= start) | (lane < start + width - LANES)


def euler(state, choose, along):
    density, momenta, energy = state[0], state[1:4], state[4]
    inverse = 1.0 / density
    normal = choose(momenta)
    speed = normal * inverse
    squares = momenta[0] * momenta[0] + momenta[1] * momenta[1] + momenta[2] * momenta[2]
    pressure = 0.4 * (energy - 0.5 * squares * inverse)
    flux = [normal] + [m * speed for m in momenta] + [(energy + pressure) * speed]
    for d in range(3):
        flux[1 + d] = along(d, flux[1 + d], pressure - 1.0)
    return flux, speed, pressure, inverse


def euler_wave(state, choose, along):
    flux, speed, pressure, inverse = euler(state, choose, along)
    return flux, jnp.abs(speed) + jnp.sqrt(1.4 * pressure * inverse)


def fixed(direction):
    def choose(parts):
        return parts[direction]

    def along(d, flux, pressure):
        return flux + pressure if d == direction else flux

    return choose, along


def by_lane(first, second):
    def choose(parts):
        return jnp.where(first, parts[0], jnp.where(second, parts[1], parts[2]))

    third = ~(first | second)

    def along(d, flux, pressure):
        return flux + jnp.where((first, second, third)[d], pressure, 0.0)

    return choose, along


def mix(left, left_flux, left_wave, right, right_flux, right_wave):
    wave = 0.5 * jnp.maximum(left_wave, right_wave)
    return [
        0.5 * (left_flux[v] + right_flux[v]) - wave * (right[v] - left[v]) for v in range(5)
    ]


def floor_divide(values, divisor):
    return ((values.astype(jnp.float32) + 0.5) * (1.0 / divisor)).astype(jnp.int32)


def table_kernel(parts, capacity, fringes, expand_ref, lanes_ref):
    row = lax.broadcasted_iota(jnp.int32, expand_ref.shape, 0)
    column = lax.broadcasted_iota(jnp.int32, expand_ref.shape, 1) & 15
    point = row & (ROWS - 1)
    point = jnp.where(point >= 25, point - 25, point)
    tens = floor_divide(point, 5)
    wanted = jnp.where(row < ROWS, 5 + tens, 10 + point - 5 * tens)
    expand_ref[...] = jnp.where(column == wanted, 1.0, 0.0).astype(jnp.bfloat16)
    me = lax.axis_index("dom")
    remote = parts * capacity
    row = lax.broadcasted_iota(jnp.int32, (8, LANES), 0)
    lane = lax.broadcasted_iota(jnp.int32, (8, LANES), 1)
    total = jnp.zeros((8, LANES), jnp.int32)
    for d in range(3):
        near = jnp.clip(lane - d * remote, 0, remote - 1)
        away = floor_divide(near, capacity)
        slot = (away ^ me) * capacity + near - away * capacity
        edge = (lane - 3 * remote - d * fringes) & (LANES - 1)
        start = (3 * remote + d * fringes) % LANES
        taken = jnp.clip(lane - d * remote, 0, remote) + jnp.clip(
            lane - start, 0, min(fringes, LANES - start)
        )
        if start + fringes > LANES:
            taken = taken + jnp.clip(lane, 0, start + fringes - LANES)
        other = remote + fringes + lane - taken
        slot = jnp.where(
            in_lanes(lane, d * remote, remote),
            slot,
            jnp.where(edge < fringes, remote + edge, other),
        )
        total = jnp.where(row == d, slot, total)
    lanes_ref[...] = total


def donor_kernel(grids, parts, count, height, *refs):
    weight_refs, cell_refs, states = (refs[k : k + 2] for k in (0, 2, 4))
    expand_ref, pay_ref, keep_ref, side_ref = refs[6:10]
    outs = refs[10 : 8 + grids]
    cells, weights, padded, planes, values = refs[8 + grids :]
    outer = parts // 2
    side_ref[: outer * height, :] = pay_ref[outer * height :, :]
    span = parts * count
    total = grids * span
    blocks = values.shape[1] - 1
    cells[...] = jnp.zeros_like(cells)
    weights[...] = jnp.zeros_like(weights)
    me = lax.axis_index("grid")
    here = lax.axis_index("dom")
    number = 0
    places = []
    for source in range(2):
        for block in range(-(-total // LANES)):
            lanes = slice(block * LANES, min((block + 1) * LANES, total))
            held = lanes.stop - lanes.start
            cells[source, block, 0:1, :held] = cell_refs[source][:, lanes]
            for k in range(15):
                weights[source, block, k : k + 1, :held] = weight_refs[source][k, :, lanes]
        halves = []
        for v in range(5):
            padded[source, v, 120:128, :] = jnp.zeros((8, LANES), jnp.float32)
            padded[source, v, :125, :] = states[source][v] - SHIFT[v]
            shifted = padded[source, v]
            high = shifted.astype(jnp.bfloat16)
            low = (shifted - high.astype(jnp.float32)).astype(jnp.bfloat16)
            halves.append(jnp.concatenate([high, low], axis=1))
        halves = jnp.concatenate(halves, axis=0)
        steps = range(0 if source else 2, grids, 2)
        starts = [partner(me, step) * span for step in steps]
        firsts = [start // LANES for start in starts]
        width = len(steps) * blocks * LANES
        pick = [(source, first + i) for first in firsts for i in range(blocks)]
        held = jnp.concatenate([cells[at] for at in pick], axis=1)
        element = lax.broadcasted_iota(jnp.int32, (LANES, width), 0)
        chosen = jnp.where(element == held[0:1], 1.0, 0.0).astype(jnp.bfloat16)
        chosen = jnp.concatenate([chosen, chosen], axis=0)
        held = jnp.concatenate([weights[at] for at in pick], axis=1)
        high = held.astype(jnp.bfloat16)
        rest = held - high.astype(jnp.float32)
        middle = rest.astype(jnp.bfloat16)
        low = (rest - middle.astype(jnp.float32)).astype(jnp.bfloat16)
        pieces = jnp.concatenate([high, middle, low], axis=0)
        plane = jnp.dot(expand_ref[...], pieces, preferred_element_type=jnp.float32)
        planes[source, :, :width] = plane[:ROWS] * plane[ROWS:]
        row = lax.broadcasted_iota(jnp.int32, (8, width), 0)
        tiles = []
        for top in range(0, LANES, 8):
            a = top // 25
            factor = jnp.broadcast_to(held[a : a + 1], (8, width))
            if a < 4 and 25 * (a + 1) < top + 8:
                later = jnp.broadcast_to(held[a + 1 : a + 2], (8, width))
                factor = jnp.where(row < 25 * (a + 1) - top, factor, later)
            tiles.append(factor * planes[source, top % 25 : top % 25 + 8, :width])
        weight = jnp.concatenate(tiles, axis=0)
        picked = jnp.dot(halves, chosen, preferred_element_type=jnp.float32)
        for v in range(5):
            value = jnp.sum(picked[v * LANES : (v + 1) * LANES] * weight, axis=0, keepdims=True)
            for k in range(len(steps) * blocks):
                values[number + k // blocks, k % blocks, v : v + 1, :] = (
                    value[:, k * LANES : (k + 1) * LANES] + SHIFT[v]
                )
        for step, start, first in zip(steps, starts, firsts):
            places.append((number, step, (step + source - 1) * count, start - first * LANES))
            number += 1
    lane = lax.broadcasted_iota(jnp.int32, (8, LANES), 1)
    found = {}
    for number, step, place, start in places:
        wanted = in_lanes(lane, place, count)
        for q in range(parts):
            offset = start + partner(here, q) * count
            block = offset // LANES
            index = lane + (offset - block * LANES - place)
            inside = index & (LANES - 1)
            near = lane_gather(values[number, block], inside)
            far = lane_gather(values[number, block + 1], inside)
            value = jnp.where(wanted, jnp.where(index < LANES, near, far), 0.0)
            found[step, q] = found[step, q] + value if (step, q) in found else value
    for z in range(outer):
        for step in range(2, grids, 2):
            outs[step - 2][z] = found[step, 2 * z]
            outs[step - 1][z] = found[step, 2 * z + 1]
        keep_ref[z] = found[0, 2 * z]
        side_ref[outer * height + 8 * z : outer * height + 8 * z + 8, :] = found[0, 2 * z + 1]


def face_kernel(
    parts,
    capacity,
    height,
    state_ref,
    plus_ref,
    minus_ref,
    faces_ref,
    lanes_ref,
    slots_ref,
    both_ref,
    pay_ref,
    turn,
):
    remote = parts * capacity
    wide = jnp.concatenate([state_ref[v] - SHIFT[v] for v in range(5)], axis=1)
    face = jnp.dot(
        faces_ref[...], wide, precision=closer, preferred_element_type=jnp.float32
    )
    for side in range(2):
        order = (minus_ref, plus_ref)[side]
        for d in range(3):
            k = 2 * d + side
            index = lane_gather(
                jnp.broadcast_to(order[d : d + 1, :], (ROWS, LANES)),
                jnp.broadcast_to(lanes_ref[d : d + 1, :], (ROWS, LANES)),
            )
            for v in range(5):
                block = face[k * ROWS : (k + 1) * ROWS, v * LANES : (v + 1) * LANES]
                slots_ref[k, v] = lane_gather(block, index) + SHIFT[v]
    lane = lax.broadcasted_iota(jnp.int32, (ROWS, LANES), 1)
    turn[:, 120:128, :] = jnp.zeros((2, 8, LANES), jnp.float32)
    for side in range(2):
        for v in range(5):
            both = jnp.where(
                lane < remote,
                slots_ref[side, v],
                jnp.where(lane < 2 * remote, slots_ref[2 + side, v], slots_ref[4 + side, v]),
            )
            both_ref[side, v] = both
            turn[side, 25 * v : 25 * v + 25, :] = both[:25]
        turned = turn[side].T
        for d in range(3):
            for q in range(parts):
                start = d * remote + q * capacity
                place = (q % 2 * (parts // 2) + q // 2) * height + (2 * d + side) * capacity
                pay_ref[place : place + capacity, :] = turned[start : start + capacity]


def repack_kernel(outer, height, pay_ref, keep_ref, *refs):
    pairs = (len(refs) - outer - 1) // 2
    across, side_ref, straight, outs = refs[:pairs], refs[pairs], refs[pairs + 1 : 2 * pairs + 1], refs[2 * pairs + 1 :]
    for z in range(outer):
        outs[z][:height, :] = pay_ref[z * height : (z + 1) * height, :]
        outs[z][height : 2 * height, :] = side_ref[z * height : (z + 1) * height, :]
        total = keep_ref[z]
        for extra in straight:
            total = total + extra[z]
        outs[z][2 * height : 2 * height + 8, :] = total
        total = side_ref[outer * height + 8 * z : outer * height + 8 * z + 8, :]
        for extra in across:
            total = total + extra[z]
        outs[z][2 * height + 8 : 2 * height + 16, :] = total


def volume_kernel(
    grids,
    parts,
    count,
    remote,
    fringes,
    state_ref,
    size_ref,
    plus_ref,
    minus_ref,
    recv_ref,
    slots_ref,
    both_ref,
    volume_ref,
    lanes_ref,
    points_ref,
    part_ref,
    flux_ref,
    edge_ref,
    local_ref,
    back_ref,
    where_ref,
    wide,
    index,
    received,
):
    state = [state_ref[v] for v in range(5)]
    for d in range(3):
        flux = euler(state, *fixed(d))[0]
        scale = size_ref[d : d + 1, :]
        wide[d * LANES + 120 : (d + 1) * LANES, :] = jnp.zeros((8, 5 * LANES), jnp.float32)
        for v in range(5):
            wide[d * LANES : d * LANES + 125, v * LANES : (v + 1) * LANES] = flux[v] * scale
    part_ref[...] = jnp.dot(
        volume_ref[...], wide[...], precision=closer, preferred_element_type=jnp.float32
    )
    for d in range(3):
        low = [slots_ref[2 * d, v] for v in range(5)]
        high = [slots_ref[2 * d + 1, v] for v in range(5)]
        low_flux, low_wave = euler_wave(low, *fixed(d))
        high_flux, high_wave = euler_wave(high, *fixed(d))
        local = mix(high, high_flux, high_wave, low, low_flux, low_wave)
        for v in range(5):
            local_ref[d, v] = local[v]
    lane = lax.broadcasted_iota(jnp.int32, (ROWS, LANES), 1)
    for side in range(2):
        own = [both_ref[side, v] for v in range(5)]
        flux, wave = euler_wave(own, *by_lane(lane < remote, in_lanes(lane, remote, remote)))
        for v in range(5):
            flux_ref[side, v] = flux[v]
        flux_ref[side, 5] = wave
        second = in_lanes(lane, 3 * remote + fringes, fringes)
        third = in_lanes(lane, 3 * remote + 2 * fringes, fringes)
        edge = [
            jnp.where(
                second,
                slots_ref[2 + side, v],
                jnp.where(third, slots_ref[4 + side, v], slots_ref[side, v]),
            )
            for v in range(5)
        ]
        flux, wave = euler_wave(edge, *by_lane(~(second | third), second))
        for v in range(5):
            edge_ref[side, v] = edge[v]
            edge_ref[side, 5 + v] = flux[v]
        edge_ref[side, 10] = wave
    rank = lax.broadcasted_iota(jnp.int32, (LANES, LANES), 0)
    column = lax.broadcasted_iota(jnp.int32, (LANES, LANES), 1)
    index[...] = jnp.zeros_like(index)
    for k in range(6):
        d = k // 2
        order = lane_gather(
            jnp.broadcast_to((minus_ref, plus_ref)[k % 2][d : d + 1, :], (8, LANES)),
            jnp.broadcast_to(lanes_ref[d : d + 1, :], (8, LANES)),
        )
        index[k : k + 1, :] = order[0:1].astype(jnp.float32)
    turned = index[...].T.astype(jnp.int32)
    back_ref[...] = jnp.zeros_like(back_ref)
    for k in range(6):
        found = jnp.where(turned[:, k : k + 1] == column, rank, 0)
        back_ref[k : k + 1, :] = jnp.sum(found, axis=0, keepdims=True)
    me = lax.axis_index("grid")
    received[...] = jnp.zeros_like(received)
    received[0:1, : recv_ref.shape[1]] = recv_ref[...]
    points = points_ref[...]
    slot = jnp.zeros((8, LANES), jnp.int32)
    for block in range(received.shape[1] // LANES):
        held = jnp.broadcast_to(received[0:1, block * LANES : (block + 1) * LANES], (8, LANES))
        inside = (points >= block * LANES) & (points < (block + 1) * LANES)
        picked = lane_gather(held, jnp.where(inside, points - block * LANES, 0))
        slot = jnp.where(inside, picked, slot)
    device = floor_divide(slot, count)
    rest = slot - device * count
    grid = floor_divide(device, parts)
    step = jnp.zeros_like(grid)
    for g in range(grids):
        away = partner(me, g)
        step = jnp.where(grid == g, away, step)
    where_ref[0] = (device - grid * parts) ^ lax.axis_index("dom")
    where_ref[1] = jnp.maximum(step - 1, 0) * count + rest


def distances(outer):
    return [0, *sorted(range(1, outer), key=lambda z: (z ^ (outer // 2)) % outer)]


def finish_kernel(parts, capacity, height, fringes, *refs):
    come = dict(zip(distances(parts // 2), refs[: parts // 2]))
    both_ref, flux_ref, edge_ref, local_ref, back_ref, where_ref, part_ref, size_ref, lift_ref = refs[
        parts // 2 : parts // 2 + 9
    ]
    out_ref, turn, turned, wide = refs[parts // 2 + 9 :]
    remote = parts * capacity
    row = lax.broadcasted_iota(jnp.int32, (ROWS, LANES), 0)
    lane = lax.broadcasted_iota(jnp.int32, (ROWS, LANES), 1)
    is_remote = [in_lanes(lane, d * remote, remote) for d in range(3)]
    is_fringe = [in_lanes(lane, 3 * remote + d * fringes, fringes) for d in range(3)]
    any_remote = (lane < 3 * remote) & (row < 25)
    any_fringe = is_fringe[0] | is_fringe[1] | is_fringe[2]
    spread = row[:8] * (3 * fringes) + ((lane[:8] - 3 * remote) & (LANES - 1))
    spread = jnp.where(any_fringe[:8], spread, 0)
    for side in range(2):
        for d in range(3):
            for q in range(parts):
                start = d * remote + q * capacity
                place = q % 2 * height + (2 * d + 1 - side) * capacity
                turn[side, start : start + capacity, :] = come[q // 2][place : place + capacity, :]
        turned[side, :LANES, :] = turn[side].T
    fringe = []
    for v in range(5):
        total = jnp.zeros((8, LANES), jnp.float32)
        for q in range(parts):
            place = 2 * height + q % 2 * 8 + v
            sent = come[q // 2][place : place + 1, :]
            picked = lane_gather(jnp.broadcast_to(sent, (8, LANES)), where_ref[1])
            total = jnp.where(where_ref[0] == q, picked, total)
        fringe.append(total)
    for side in range(2):
        own = [both_ref[side, v] for v in range(5)]
        theirs = [
            jnp.where(any_remote, turned[side, 25 * v : 25 * v + ROWS, :], own[v])
            for v in range(5)
        ]
        their = (theirs, *euler_wave(theirs, *by_lane(is_remote[0], is_remote[1])))
        mine = (own, [flux_ref[side, v] for v in range(5)], flux_ref[side, 5])
        common = mix(*mine, *their) if side else mix(*their, *mine)
        own = [edge_ref[side, v] for v in range(5)]
        theirs = []
        for v in range(5):
            pieces = [
                lane_gather(
                    jnp.broadcast_to(fringe[v][side * 4 + r : side * 4 + r + 1], (8, LANES)), spread
                )
                for r in range(4)
            ]
            theirs.append(jnp.where(any_fringe, jnp.concatenate(pieces, axis=0), own[v]))
        their = (theirs, *euler_wave(theirs, *by_lane(~(is_fringe[1] | is_fringe[2]), is_fringe[1])))
        mine = (own, [edge_ref[side, 5 + v] for v in range(5)], edge_ref[side, 10])
        outer = mix(*mine, *their) if side else mix(*their, *mine)
        for d in range(3):
            k = 2 * d + side
            index = jnp.broadcast_to(back_ref[k : k + 1, :], (ROWS, LANES))
            scale = size_ref[d : d + 1, :]
            for v in range(5):
                value = jnp.where(is_fringe[d], outer[v], local_ref[d, v])
                value = jnp.where(is_remote[d], common[v], value)
                wide[k * ROWS : (k + 1) * ROWS, v * LANES : (v + 1) * LANES] = (
                    lane_gather(value, index) * scale
                )
    values = wide[...]
    high = values.astype(jnp.bfloat16)
    low = (values - high.astype(jnp.float32)).astype(jnp.bfloat16)
    first = jnp.dot(lift_ref[...], high, preferred_element_type=jnp.float32)
    second = jnp.dot(lift_ref[:LANES], low, preferred_element_type=jnp.float32)
    total = part_ref[...] + (first[:125] + (first[LANES : LANES + 125] + second[:125]))
    for v in range(5):
        out_ref[v] = total[:, v * LANES : (v + 1) * LANES]


def call(kernel, name, out_shape, scratch, flops, size, *operands, limit=VMEM, **more):
    return pl.pallas_call(
        kernel,
        name=name,
        out_shape=out_shape,
        scratch_shapes=scratch,
        compiler_params=pltpu.CompilerParams(vmem_limit_bytes=limit),
        cost_estimate=pl.CostEstimate(flops=flops, bytes_accessed=size, transcendentals=0),
        **more,
    )(*operands)


def body(state, inv_size, plus_order, minus_order, donor_cell, donor_weights, recv_slot):
    columns = state.shape[-1]
    parts = lax.axis_size("dom")
    grids = lax.axis_size("grid")
    capacity = max(1, columns // (3 * parts))
    remote = parts * capacity
    fringes = recv_slot.shape[-1] // 150
    total = donor_cell.shape[-1]
    count = total // (grids * parts)
    held = -(-recv_slot.shape[-1] // LANES) * LANES
    outer = parts // 2
    height = -(-6 * capacity // 8) * 8
    span = parts * count
    blocks = (2 * (LANES - 1) + span) // LANES
    held_blocks = -(-total // LANES) + blocks
    faces, volume, lift = matrices()
    lift = np.pad(lift, ((0, LANES - 125), (0, 0)))
    high = lift.astype(ml_dtypes.bfloat16)
    lift = np.concatenate([high, (lift - high.astype(np.float32)).astype(ml_dtypes.bfloat16)])
    points = fringe_lanes(fringes)
    f32 = functools.partial(jax.ShapeDtypeStruct, dtype=jnp.float32)
    i32 = functools.partial(jax.ShapeDtypeStruct, dtype=jnp.int32)
    memory = functools.partial(pltpu.VMEM, dtype=jnp.float32)

    def exchange(values, step, move):
        pairs = [
            (g * parts + q, partner(g, step) * parts + partner(q, move))
            for g in range(grids)
            for q in range(parts)
        ]
        return lax.ppermute(values, ("grid", "dom"), pairs)

    weights = donor_weights.reshape(15, 1, total)
    mates = [exchange(values, 1, 0) for values in (state, donor_cell, weights)]
    expand, lanes = call(
        functools.partial(table_kernel, parts, capacity, fringes),
        "tables",
        (jax.ShapeDtypeStruct((2 * ROWS, 48), jnp.bfloat16), i32((8, LANES))),
        [],
        400_000_000,
        3_000_000,
    )
    slots, both, pay = call(
        functools.partial(face_kernel, parts, capacity, height),
        "faces",
        (
            f32((6, 5, ROWS, LANES)),
            f32((2, 5, ROWS, LANES)),
            f32((parts * height, LANES)),
        ),
        [memory((2, LANES, LANES))],
        200_000_000,
        1_500_000,
        state,
        plus_order,
        minus_order,
        faces,
        lanes,
    )
    keep, side, *sent = call(
        functools.partial(donor_kernel, grids, parts, count, height),
        "donors",
        (
            f32((outer, 8, LANES)),
            f32((outer * (height + 8), LANES)),
            *(f32((outer, 8, LANES)) for _ in range(grids - 2)),
        ),
        [
            pltpu.VMEM((2, held_blocks, 8, LANES), jnp.int32),
            memory((2, held_blocks, 16, LANES)),
            memory((2, 5, LANES, LANES)),
            memory((2, ROWS, grids // 2 * blocks * LANES)),
            memory((grids - 1, blocks + 1, 8, LANES)),
        ],
        5_000_000,
        500_000,
        weights,
        mates[2],
        donor_cell,
        mates[1],
        state,
        mates[0],
        expand,
        pay,
    )
    side = exchange(side, 0, 1)
    across = [exchange(sent[k + 1], k + 2, 1) for k in range(0, grids - 2, 2)]
    straight = [exchange(sent[k], k + 2, 0) for k in range(0, grids - 2, 2)]
    packed = call(
        functools.partial(repack_kernel, outer, height),
        "repack",
        tuple(f32((2 * height + 16, LANES)) for _ in range(outer)),
        [],
        50_000,
        200_000,
        pay,
        keep,
        *across,
        side,
        *straight,
    )
    come = [exchange(packed[z], 0, 2 * z) if z else packed[z] for z in distances(outer)]
    part, flux, edge, local, back, where = call(
        functools.partial(volume_kernel, grids, parts, count, remote, fringes),
        "volume",
        (
            f32((125, 5 * LANES)),
            f32((2, 6, ROWS, LANES)),
            f32((2, 11, ROWS, LANES)),
            f32((3, 5, ROWS, LANES)),
            i32((8, LANES)),
            i32((2, 8, LANES)),
        ),
        [
            memory((3 * LANES, 5 * LANES)),
            memory((LANES, LANES)),
            pltpu.VMEM((8, held), jnp.int32),
        ],
        400_000_000,
        3_000_000,
        state,
        inv_size,
        plus_order,
        minus_order,
        recv_slot,
        slots,
        both,
        volume,
        lanes,
        points,
    )
    return call(
        functools.partial(finish_kernel, parts, capacity, height, fringes),
        "finish",
        f32((5, 125, columns)),
        [
            memory((2, LANES, LANES)),
            memory((2, LANES + 8, LANES)),
            memory((6 * ROWS, 5 * LANES)),
        ],
        200_000_000,
        3_000_000,
        *come,
        both,
        flux,
        edge,
        local,
        back,
        where,
        part,
        inv_size,
        lift,
    )


def solution(mesh):
    return jax.shard_map(
        body,
        mesh=mesh,
        in_specs=(
            P(None, None, ("grid", "dom")),
            P(None, ("grid", "dom")),
            P(None, ("grid", "dom")),
            P(None, ("grid", "dom")),
            P(("grid", "dom"), None),
            P(("grid", "dom"), None, None, None),
            P(("grid", "dom"), None),
        ),
        out_specs=P(None, None, ("grid", "dom")),
        check_vma=False,
    )
```
